32 devices in a mesh: img: 4 (over y, x), atom: 8 (over z, core).
Axes of the slice: x: 2, y: 2, z: 4, core: 2. Of those that a mesh axis runs over, the one named last changes fastest.
Arguments:
- positions: float32 [4, 3, 8192], P('img', None, 'atom'), may hold values from -9.8 to 9.8, as said below
- species: int32 [8192], P('atom'), may hold values from 0 to 3
- counts: int32 [8192], P('atom'), may hold values from 1 to 16, as said below
- neighbours: int32 [16, 8192], P(None, 'atom'), may hold values from 0 to 1535, as said below
- send_list: int32 [4096], P('atom'), may hold values from 0 to 1023
- climb: int32 [4], P('img'), may hold values 0 or 1
- embed: bfloat16 [4, 128], replicated, may hold values from -6 to 6
- ref_energy: float32 [4], replicated, may hold values from -2 to 2
- rad_in: bfloat16 [3, 8, 64], replicated, may hold values from -24 to 24
- rad_out: bfloat16 [3, 64, 128], replicated, may hold values from -0.047851562 to 0.047851562
- mixing: bfloat16 [2, 128, 128], replicated, may hold values from -0.5 to 0.5
- w_energy: bfloat16 [128], replicated, may hold values from -0.5 to 0.5
Outputs:
- neb_force: float32 [4, 3, 8192], P('img', None, 'atom')
- energies: float32 [4], P('img')
The draws below stay inside these ranges and needn't reach their ends.
Inputs may be any that keep to these rules, and one draw needn't show every extreme that they name: `positions`: positions of image p are those of image 0 plus a sum of p random displacements. `counts`: the first atom of every tile has all 16 slots live. `neighbours`: every slot of the atom with local index i (its index mod 1024) names a row from i to i + 512 of its tile's table, never row i + 256. `send_list`: values are local atom indices of the owning tile.
All inputs are finite; a program needn't handle non-finite values. No bound on the sum of `climb` on one device may be relied on, other than what follows from the above.
Results may differ from the reference program's by a relative error of at most 0.007.
Values may be sent and summed in bfloat16 or wider, within the bound.
No kernel may reach another device: no remote copies, remote signals or barrier semaphores. Data moves between devices by JAX's collectives and lax.ppermute only.
A program may use at most 64 MiB of HBM per device.

```python
import math
import jax
import jax.numpy as jnp
from jax import lax

C = 128
RAD = 64
NB = 8
SPECIES = 4
LAYERS = 2
NBR = 16
HALO = 256
ATOM_DEV = 1024
ATOMS = 8192
IMAGES = 4
N_ATOM = 8


def draw_positions(key, part):
    first, second, third, fourth, fifth, sixth = jax.random.split(key, 6)
    base = jnp.clip(jax.random.normal(first, (3, ATOMS), jnp.float32), -5.0, 5.0)
    tile_total = ATOMS // ATOM_DEV
    tile_of = jnp.arange(ATOMS, dtype=jnp.int32) // ATOM_DEV
    hot_tiles = jax.random.randint(fourth, (2,), 0, tile_total)
    cold_weight = jnp.exp(jax.random.uniform(fifth, (tile_total,), jnp.float32, jnp.log(0.003), jnp.log(0.1)))
    atom_weight = jnp.take(cold_weight, tile_of)
    is_hot = jnp.logical_or(tile_of == hot_tiles[0], tile_of == hot_tiles[1])
    atom_weight = jnp.where(is_hot, 1.0, atom_weight)
    path_dir = jnp.clip(jax.random.normal(second, (3, ATOMS), jnp.float32), -2.5, 2.5)
    wobble = jnp.clip(jax.random.normal(sixth, (IMAGES, 3, ATOMS), jnp.float32), -2.5, 2.5)
    moves = (path_dir[None] + 0.5 * wobble) * atom_weight[None, None, :]
    scales = jnp.exp(jax.random.uniform(third, (IMAGES, 1, 1), jnp.float32, jnp.log(0.05), jnp.log(0.3)))
    order = jax.lax.broadcasted_iota(jnp.int32, (IMAGES, 1, 1), 0)
    moves = jnp.where(order == 0, 0.0, moves * scales)
    return base[None] + jnp.cumsum(moves, axis=0)


def draw_counts(key, part):
    raw = jax.random.randint(key, (ATOMS,), 1, NBR + 1)
    first = jnp.arange(ATOMS, dtype=jnp.int32) % ATOM_DEV == 0
    return jnp.where(first, NBR, raw).astype(jnp.int32)


def draw_neighbours(key, part):
    raw = jax.random.randint(key, (NBR, ATOMS), -HALO, HALO)
    offset = jnp.where(raw >= 0, raw + 1, raw)
    local = (jnp.arange(ATOMS, dtype=jnp.int32) % ATOM_DEV)[None, :]
    slot = jax.lax.broadcasted_iota(jnp.int32, (NBR, ATOMS), 0)
    offset = jnp.where(jnp.logical_and(slot == 0, local == 0), -HALO, offset)
    offset = jnp.where(jnp.logical_and(slot == 0, local == ATOM_DEV - 1), HALO, offset)
    return (HALO + local + offset).astype(jnp.int32)


def place_ends(values, key, least, high):
    place = [jax.random.randint(jax.random.fold_in(key, axis), (), 0, length) for axis, length in enumerate(values.shape)]
    widest = values.shape.index(max(values.shape))
    next_to = place[:widest] + [(place[widest] + 1) % values.shape[widest]] + place[widest + 1:]
    return values.at[tuple(place)].set(least).at[tuple(next_to)].set(high)


def centred(rng, shape, spread, most, held_as=jnp.bfloat16):
    drawn = spread * jax.random.normal(rng, shape, jnp.float32)
    return jnp.clip(drawn, min=-most, max=most).astype(held_as)


def setup_inputs(seed: int = 0) -> dict:
    key_of = jax.random.split(jax.random.key(seed), 13)
    positions = draw_positions(jax.random.fold_in(key_of[12], 71), 0)
    species = place_ends(jax.random.randint(key_of[1], (ATOMS,), 0, SPECIES), jax.random.fold_in(key_of[1], 1), 0, SPECIES - 1).astype(jnp.int32)
    counts = draw_counts(jax.random.fold_in(key_of[12], 71), 0)
    neighbours = draw_neighbours(jax.random.fold_in(key_of[12], 71), 0)
    send_list = place_ends(jax.random.randint(key_of[4], (2 * HALO * N_ATOM,), 0, ATOM_DEV), jax.random.fold_in(key_of[4], 1), 0, ATOM_DEV - 1).astype(jnp.int32)
    climb = place_ends((jax.random.randint(key_of[5], (IMAGES,), 0, 2) < 1).astype(jnp.int32), jax.random.fold_in(key_of[5], 1), 0, 1)
    embed = centred(key_of[6], (SPECIES, C), 1.0, 6.0)
    ref_energy = jnp.clip(jax.random.uniform(key_of[7], (SPECIES,), jnp.float32, -2.0, 2.0), -2.0, 2.0)
    rad_in = centred(key_of[8], (LAYERS + 1, NB, RAD), 4.0, 24.0)
    rad_out = centred(key_of[9], (LAYERS + 1, RAD, C), 0.008, 0.047851562)
    mixing = centred(key_of[10], (LAYERS, C, C), C ** -0.5, 0.5)
    w_energy = centred(key_of[11], (C,), C ** -0.5, 0.5)
    return {"positions": positions, "species": species, "counts": counts, "neighbours": neighbours, "send_list": send_list, "climb": climb, "embed": embed, "ref_energy": ref_energy, "rad_in": rad_in, "rad_out": rad_out, "mixing": mixing, "w_energy": w_energy}


spring_constant = 5.0

def radial_field(basis, w_in, w_out):
    hidden = lax.dot_general(w_in, basis, (((0,), (0,)), ((), ())), preferred_element_type=jnp.float32)
    hidden = jax.nn.silu(hidden).astype(jnp.bfloat16)
    return lax.dot_general(hidden, w_out, (((0,), (0,)), ((), ())), preferred_element_type=jnp.float32)

def species_table(kinds, embed):
    onehot = (kinds[:, None] == jnp.arange(SPECIES, dtype=jnp.int32)[None, :]).astype(jnp.bfloat16)
    return jnp.dot(onehot, embed, preferred_element_type=jnp.float32).astype(jnp.bfloat16)

def to_tiles(arr):
    lead = arr.shape[:-1]
    arr = arr.reshape(lead + (N_ATOM, ATOM_DEV))
    return jnp.moveaxis(arr, -2, 0)

def reference(positions, species, counts, neighbours, send_list, climb, embed, ref_energy, rad_in, rad_out, mixing, w_energy):
    lists = send_list.reshape(N_ATOM, 2 * HALO)
    starts = (jnp.arange(N_ATOM, dtype=jnp.int32) * ATOM_DEV)[:, None]
    glob = lists + starts
    lower = jnp.roll(glob[:, HALO:], 1, axis=0)
    upper = jnp.roll(glob[:, :HALO], -1, axis=0)
    local = starts + jnp.arange(ATOM_DEV, dtype=jnp.int32)[None, :]
    tables = jnp.concatenate([lower, local, upper], axis=1)
    tiled = to_tiles(neighbours).reshape(N_ATOM, NBR * ATOM_DEV)
    partner = jnp.take_along_axis(tables, tiled, axis=1).reshape(N_ATOM, NBR, ATOM_DEV)
    partner = jnp.moveaxis(partner, 0, 1).reshape(NBR, ATOMS)
    slots = lax.broadcasted_iota(jnp.int32, (NBR, ATOMS), 0)
    live = (slots < counts[None, :]).astype(jnp.float32)
    centres = 2.0 * jnp.arange(NB, dtype=jnp.float32)
    onehot_ref = jnp.where(species[:, None] == jnp.arange(SPECIES, dtype=jnp.int32)[None, :], ref_energy[None, :], jnp.float32(0.0))
    atom_ref = lax.optimization_barrier(jnp.sum(onehot_ref, axis=1))
    forces = []
    energies = []
    for image in range(IMAGES):
        coords = positions[image]
        delta = coords[:, partner] - coords[:, None, :]
        dist_sq = lax.optimization_barrier(jnp.sum(delta * delta, axis=0))
        basis = jnp.exp(-jnp.square(dist_sq[None] - centres[:, None, None]) / 8.0).astype(jnp.bfloat16)
        basis_tiles = to_tiles(basis).reshape(N_ATOM, NB, NBR * ATOM_DEV)
        partner_tiles = to_tiles(partner)
        live_tiles = to_tiles(live)
        delta_tiles = to_tiles(delta)
        feats = species_table(species, embed)
        for layer in range(LAYERS):

            def step(items, table=feats, layer=layer):
                nbr_b, basis_b, live_b, feats_b = items
                field = radial_field(basis_b, rad_in[layer], rad_out[layer]).reshape(NBR, ATOM_DEV, C)
                far = table[nbr_b].astype(jnp.float32)
                summed = lax.optimization_barrier(jnp.sum(field * far * live_b[:, :, None], axis=0))
                scaled = (summed / math.sqrt(NBR)).astype(jnp.bfloat16)
                update = jax.nn.silu(jnp.dot(scaled, mixing[layer], preferred_element_type=jnp.float32))
                return (feats_b.astype(jnp.float32) + update).astype(jnp.bfloat16)
            feats = lax.map(step, (partner_tiles, basis_tiles, live_tiles, feats.reshape(N_ATOM, ATOM_DEV, C))).reshape(ATOMS, C)

        def force_step(items, table=feats):
            nbr_b, basis_b, live_b, feats_b, delta_b = items
            field = radial_field(basis_b, rad_in[LAYERS], rad_out[LAYERS]).reshape(NBR, ATOM_DEV, C)
            far = table[nbr_b].astype(jnp.float32)
            near = feats_b.astype(jnp.float32)[None]
            pair = lax.optimization_barrier(jnp.sum(field * near * far, axis=2)) * (live_b / math.sqrt(C))
            return lax.optimization_barrier(jnp.sum(pair[None] * delta_b, axis=1))
        force_tiles = lax.map(force_step, (partner_tiles, basis_tiles, live_tiles, feats.reshape(N_ATOM, ATOM_DEV, C), delta_tiles))
        forces.append(jnp.moveaxis(force_tiles, 0, 1).reshape(3, ATOMS))
        per_atom = jnp.dot(feats, w_energy, preferred_element_type=jnp.float32) + atom_ref
        energies.append(jnp.sum(per_atom) / ATOMS)
    outputs = []
    for image in range(IMAGES):
        force = forces[image]
        if image == 0 or image == IMAGES - 1:
            outputs.append(force)
        else:
            back = positions[image] - positions[image - 1]
            fore = positions[image + 1] - positions[image]
            back_len = jnp.sqrt(jnp.sum(back * back) + 1e-06)
            fore_len = jnp.sqrt(jnp.sum(fore * fore) + 1e-06)
            tangent = back / back_len + fore / fore_len
            tau_sq = jnp.sum(tangent * tangent)
            along = jnp.sum(force * tangent)
            proj = along / tau_sq
            interior = force - proj * tangent + spring_constant * (fore_len - back_len) / jnp.sqrt(tau_sq) * tangent
            climbing = force - 2.0 * proj * tangent
            outputs.append(jnp.where(climb[image] == 1, climbing, interior))
    return (jnp.stack(outputs, axis=0), jnp.stack(energies, axis=0))
```

```python
import functools
import math

import jax
import jax.numpy as jnp
from jax import lax
from jax.experimental import pallas as pl
from jax.experimental.pallas import tpu as pltpu
from jax.sharding import PartitionSpec as P

F32 = jnp.float32
BF16 = jnp.bfloat16
I32 = jnp.int32
LANES = 128
SPRING = 5.0
SPECIES_ROW = 3
COUNT_ROW = 4
SEND_ROW = 5
PACK_ROWS = 8
SUM_ROWS = 8
VMEM = pl.BlockSpec(memory_space=pltpu.VMEM)
SMEM = pl.BlockSpec(memory_space=pltpu.SMEM)


def dot(a, b):
    return jnp.dot(a, b, preferred_element_type=F32)


def silu_of_half(half):
    return half + half * jnp.tanh(half)


def aligned(start, step):
    return pl.multiple_of(start, step)


def lane_fetch(windows, group, place):
    found = jnp.zeros(place.shape, F32)
    for k, window in enumerate(windows):
        rows = jnp.broadcast_to(window, place.shape)
        picked = jnp.take_along_axis(rows, place, axis=1, mode="promise_in_bounds")
        found = jnp.where(group == k, picked, found)
    return found


def live_slots(pk, lo, fan, width):
    slots = lax.broadcasted_iota(I32, (fan, width), 0).astype(F32)
    return slots < pk[COUNT_ROW : COUNT_ROW + 1, pl.ds(lo, width)]


def geometry(table, table_lo, pk, nbr, lo, rim):
    fan = nbr.shape[0]
    parts = []
    for half in range(rim // LANES):
        first = lo + half * LANES
        start = table_lo + half * LANES
        rel = nbr[:, pl.ds(aligned(first, LANES), LANES)] - first
        place = rel & (LANES - 1)
        group = rel // LANES
        live = live_slots(pk, aligned(first, LANES), fan, LANES)
        spans = [
            table[:, pl.ds(aligned(start + k * LANES, LANES), LANES)]
            for k in range(2 * rim // LANES + 1)
        ]
        deltas = []
        for c in range(3):
            far = lane_fetch([span[c : c + 1] for span in spans], group, place)
            deltas.append(far - pk[c : c + 1, pl.ds(aligned(first, LANES), LANES)])
        kinds = lane_fetch([span[SPECIES_ROW : SPECIES_ROW + 1] for span in spans], group, place)
        parts.append(deltas + [jnp.where(live, kinds, -1.0)])
    joined = [jnp.concatenate(list(piece), axis=1) for piece in zip(*parts)]
    return joined[:3], joined[3]


def basis_of(deltas, basis_count):
    dist_sq = deltas[0] * deltas[0] + deltas[1] * deltas[1] + deltas[2] * deltas[2]
    fan, width = dist_sq.shape
    centres = 2.0 * lax.broadcasted_iota(I32, (basis_count, width), 0).astype(F32)
    rows = []
    for s in range(fan):
        away = jnp.broadcast_to(dist_sq[s : s + 1], (basis_count, width)) - centres
        rows.append(jnp.exp(away * away * -0.125))
    return jnp.concatenate(rows, axis=0).astype(BF16)


def spread_first_layer(rad_in, layer, spread):
    count, units = rad_in.shape[1:]
    fan = spread.shape[0] // units
    half = rad_in[layer].astype(F32) * 0.5
    turned = jnp.concatenate([half] * fan, axis=0).T
    owner = lax.broadcasted_iota(I32, turned.shape, 1) // count
    for s in range(fan):
        spread[s * units : (s + 1) * units, :] = jnp.where(owner == s, turned, 0.0).astype(BF16)


def hidden_of(spread, basis):
    return silu_of_half(dot(spread[...], basis)).astype(BF16)


def turned_weight(ref, layer, scale=1.0):
    return (ref[layer].astype(F32) * scale).T.astype(BF16)


def fetch_rows(table, table_lo, places, s, rim):
    rows = lax.broadcasted_iota(I32, (rim, rim), 0).astype(F32).astype(BF16)
    one, zero = jnp.ones((), BF16), jnp.zeros((), BF16)
    picks = jnp.concatenate(
        [jnp.where(rows == place[s : s + 1], one, zero) for place in places], axis=0
    )
    return dot(table[:, pl.ds(table_lo, len(places) * rim)], picks)


def places_of(pk, nbr, lo, rim):
    fan = nbr.shape[0]
    rel = nbr[:, pl.ds(lo, rim)] - lo
    rel = jnp.where(live_slots(pk, lo, fan, rim), rel, -1)
    return [jnp.clip(rel - k * rim, -1, rim).astype(F32).astype(BF16) for k in range(3)]


def update_of(feats, summed, mix_half, fan):
    scaled = (summed * (1.0 / math.sqrt(fan))).astype(BF16)
    return (feats.astype(F32) + silu_of_half(dot(mix_half, scaled))).astype(BF16)


def first_block(table, table_lo, pk, nbr, lo, rim, weights, spread, hid):
    embed_t, first, mix_half = weights
    fan = nbr.shape[0]
    chans = mix_half.shape[0]
    kinds_count = embed_t.shape[1]
    units = spread.shape[0] // fan
    species = first.shape[1] // units
    deltas, kinds = geometry(table, table_lo, pk, nbr, lo, rim)
    basis = basis_of(deltas, spread.shape[1] // fan)
    hid[...] = hidden_of(spread, basis)
    kinds = kinds.astype(BF16)
    zero = jnp.zeros((), BF16)
    summed = jnp.zeros((chans, rim), F32)
    for s in range(fan):
        mine = hid[s * units : (s + 1) * units, :]
        kind = jnp.broadcast_to(kinds[s : s + 1], (units, rim))
        sorted_out = [
            jnp.where(kind == jnp.full((), k, BF16), mine, zero) for k in range(species)
        ]
        summed = summed + dot(first, jnp.concatenate(sorted_out, axis=0))
    rows = lax.broadcasted_iota(I32, (kinds_count, rim), 0).astype(F32)
    own = rows == pk[SPECIES_ROW : SPECIES_ROW + 1, pl.ds(lo, rim)]
    feats = dot(embed_t, jnp.where(own, 1.0, 0.0).astype(BF16))
    return deltas, basis, update_of(feats, summed, mix_half, fan)


def first_weights(embed, rad_in, rad_out, mixing, spread):
    spread_first_layer(rad_in, 0, spread)
    out = rad_out[0].astype(F32)
    table = embed[...].astype(F32)
    species = table.shape[0]
    kinds_count = -(-species // 16) * 16
    padded = jnp.concatenate(
        [table, jnp.zeros((kinds_count - species, table.shape[1]), F32)], axis=0
    )
    embed_t = padded.T.astype(BF16)
    first = jnp.concatenate([out * table[k : k + 1] for k in range(species)], axis=0)
    return embed_t, first.T.astype(BF16), turned_weight(mixing, 0, 0.5)


def store_block(i, deltas, basis, delta_out, basis_out):
    fan = deltas[0].shape[0]
    for c in range(3):
        delta_out[i, c * fan : (c + 1) * fan, :] = deltas[c]
    basis_out[i] = basis


def first_inner(rim, pk, nbr, embed, rad_in, rad_out, mixing, delta_out, basis_out, feats_out, spread, hid):
    weights = first_weights(embed, rad_in, rad_out, mixing, spread)

    def body(i, carry):
        lo = aligned((i + 1) * rim, rim)
        deltas, basis, feats = first_block(
            pk, lo - rim, pk, nbr, lo, rim, weights, spread, hid
        )
        store_block(i, deltas, basis, delta_out, basis_out)
        feats_out[:, pl.ds(aligned(i * rim, rim), rim)] = feats
        return carry

    lax.fori_loop(0, feats_out.shape[1] // rim, body, 0)


def pack_halo(feats, pk, core, rim, to_mate, to_cross):
    atoms = feats.shape[1]
    rows = lax.broadcasted_iota(I32, (rim, rim), 0).astype(F32).astype(BF16)
    one, zero = jnp.ones((), BF16), jnp.zeros((), BF16)
    for ref, start in ((to_mate, (1 - core) * rim), (to_cross, core * rim)):
        wanted = pk[SEND_ROW : SEND_ROW + 1, pl.ds(aligned(start, rim), rim)]
        picks = jnp.concatenate(
            [
                jnp.where(
                    rows == jnp.clip(wanted - k * rim, -1.0, float(rim)).astype(BF16), one, zero
                )
                for k in range(atoms // rim)
            ],
            axis=0,
        )
        ref[...] = dot(feats[...], picks).astype(BF16)


def halo_places(core, atoms, rim):
    top = atoms + rim
    return aligned((1 - core) * top, rim), aligned(core * top, rim)


def first_outer(rim, core_ref, pk, mate, cross, nbr, embed, rad_in, rad_out, mixing, inner, delta_out, basis_out, feats_out, to_mate, to_cross, table, spread, hid):
    core = core_ref[0]
    atoms = pk.shape[1]
    weights = first_weights(embed, rad_in, rad_out, mixing, spread)
    table[:, rim : rim + atoms] = pk[...]
    at_mate, at_cross = halo_places(core, atoms, rim)
    for ref, start, at in ((mate, core * rim, at_mate), (cross, (1 - core) * rim, at_cross)):
        for half in range(rim // LANES):
            wanted = ref[SEND_ROW : SEND_ROW + 1, pl.ds(aligned(start + half * LANES, LANES), LANES)]
            wanted = jnp.broadcast_to(wanted.astype(I32), (PACK_ROWS, LANES))
            spans = [ref[:, k * LANES : (k + 1) * LANES] for k in range(atoms // LANES)]
            table[:, pl.ds(aligned(at + half * LANES, LANES), LANES)] = lane_fetch(
                spans, wanted // LANES, wanted & (LANES - 1)
            )
    feats_out[:, rim : atoms - rim] = inner[...]

    def body(i, carry):
        lo = aligned(i * (atoms - rim), rim)
        deltas, basis, feats = first_block(table, lo, pk, nbr, lo, rim, weights, spread, hid)
        store_block(i, deltas, basis, delta_out, basis_out)
        feats_out[:, pl.ds(lo, rim)] = feats
        return carry

    lax.fori_loop(0, 2, body, 0)
    pack_halo(feats_out, pk, core, rim, to_mate, to_cross)


def layer_block(table, table_lo, pk, nbr, lo, rim, hid, out_t, mix_half, own):
    fan = nbr.shape[0]
    units = out_t.shape[1]
    places = places_of(pk, nbr, lo, rim)
    summed = jnp.zeros(own.shape, F32)
    for s in range(fan):
        far = fetch_rows(table, table_lo, places, s, rim)
        summed = summed + far * dot(out_t, hid(slice(s * units, (s + 1) * units)))
    return update_of(own, summed, mix_half, fan)


def layer_inner(rim, layer, pk, nbr, rad_in, rad_out, mixing, feats, basis, basis_edge, feats_out, hid_edge, spread, hid):
    spread_first_layer(rad_in, layer, spread)
    out_t = turned_weight(rad_out, layer)
    mix_half = turned_weight(mixing, layer, 0.5)

    def body(i, carry):
        lo = aligned((i + 1) * rim, rim)
        hid[...] = hidden_of(spread, basis[i])
        own = feats[:, pl.ds(lo, rim)]
        feats_out[:, pl.ds(aligned(i * rim, rim), rim)] = layer_block(
            feats, aligned(lo - rim, rim), pk, nbr, lo, rim, lambda r: hid[r, :], out_t, mix_half, own
        )
        return carry

    lax.fori_loop(0, basis.shape[0], body, 0)
    for i in range(2):
        hid_edge[i] = hidden_of(spread, basis_edge[i])


def fill_table(table, feats, mate, cross, core, rim):
    atoms = feats.shape[1]
    at_mate, at_cross = halo_places(core, atoms, rim)
    table[:, rim : rim + atoms] = feats[...]
    table[:, pl.ds(at_mate, rim)] = mate[...]
    table[:, pl.ds(at_cross, rim)] = cross[...]


def layer_outer(rim, layer, core_ref, pk, nbr, rad_out, mixing, feats, mate, cross, hid_edge, inner, feats_out, to_mate, to_cross, table):
    core = core_ref[0]
    atoms = pk.shape[1]
    out_t = turned_weight(rad_out, layer)
    mix_half = turned_weight(mixing, layer, 0.5)
    fill_table(table, feats, mate, cross, core, rim)
    feats_out[:, rim : atoms - rim] = inner[...]

    def body(i, carry):
        lo = aligned(i * (atoms - rim), rim)
        own = feats[:, pl.ds(lo, rim)]
        feats_out[:, pl.ds(lo, rim)] = layer_block(
            table, lo, pk, nbr, lo, rim, lambda r: hid_edge[i, r, :], out_t, mix_half, own
        )
        return carry

    lax.fori_loop(0, 2, body, 0)
    pack_halo(feats_out, pk, core, rim, to_mate, to_cross)


def head_block(table, table_lo, pk, nbr, lo, rim, hid, out_t, own, delta):
    fan = nbr.shape[0]
    chans, units = out_t.shape
    places = places_of(pk, nbr, lo, rim)
    near = own.astype(F32)
    pairs = []
    for s in range(fan):
        far = fetch_rows(table, table_lo, places, s, rim)
        terms = far * (dot(out_t, hid(slice(s * units, (s + 1) * units))) * near)
        pairs.append(jnp.sum(terms, axis=0, keepdims=True))
    pair = jnp.concatenate(pairs, axis=0) * (1.0 / math.sqrt(chans))
    rows = [
        jnp.sum(pair * delta[c * fan : (c + 1) * fan, :], axis=0, keepdims=True) for c in range(3)
    ]
    return jnp.concatenate(rows + [jnp.zeros((PACK_ROWS - 3, rim), F32)], axis=0)


def head_inner(rim, layer, pk, nbr, rad_in, rad_out, feats, basis, delta, basis_edge, force_out, hid_edge, spread, hid):
    spread_first_layer(rad_in, layer, spread)
    out_t = turned_weight(rad_out, layer)

    def body(i, carry):
        lo = aligned((i + 1) * rim, rim)
        hid[...] = hidden_of(spread, basis[i])
        force_out[:, pl.ds(aligned(i * rim, rim), rim)] = head_block(
            feats, aligned(lo - rim, rim), pk, nbr, lo, rim, lambda r: hid[r, :], out_t,
            feats[:, pl.ds(lo, rim)], delta.at[i],
        )
        return carry

    lax.fori_loop(0, basis.shape[0], body, 0)
    for i in range(2):
        hid_edge[i] = hidden_of(spread, basis_edge[i])


def lane_sum(values):
    total = values[:, :LANES]
    for k in range(1, values.shape[1] // LANES):
        total = total + values[:, k * LANES : (k + 1) * LANES]
    return jnp.sum(total, axis=0, keepdims=True)


def head_outer(rim, layer, core_ref, ref_energy, pk, behind, ahead, nbr, rad_out, w_energy, feats, mate, cross, hid_edge, delta, inner, force_out, sums_out, table):
    core = core_ref[0]
    atoms = pk.shape[1]
    out_t = turned_weight(rad_out, layer)
    fill_table(table, feats, mate, cross, core, rim)
    force_out[:, rim : atoms - rim] = inner[...]

    def body(i, carry):
        lo = aligned(i * (atoms - rim), rim)
        force_out[:, pl.ds(lo, rim)] = head_block(
            table, lo, pk, nbr, lo, rim, lambda r: hid_edge[i, r, :], out_t,
            feats[:, pl.ds(lo, rim)], delta.at[i],
        )
        return carry

    lax.fori_loop(0, 2, body, 0)
    readout = dot(w_energy[...], feats[...])
    kinds = pk[SPECIES_ROW : SPECIES_ROW + 1, :]
    energy = readout
    for k in range(ref_energy.shape[0]):
        energy = energy + jnp.where(kinds == float(k), ref_energy[k], 0.0)
    here = pk[0:3, :]
    back = here - behind[0:3, :]
    fore = ahead[0:3, :] - here
    force = force_out[0:3, :]
    rows = [energy, back * back, fore * fore, back * fore, force * back, force * fore]
    sums = [lane_sum(row) for row in rows]
    sums.append(jnp.zeros((SUM_ROWS - len(sums), LANES), F32))
    total = jnp.concatenate(sums, axis=0)
    for peer in range(sums_out.shape[0]):
        sums_out[peer] = total


def finish(count, flags, pk, behind, ahead, force, sums, result, energy_out):
    total = sums[0]
    for peer in range(1, sums.shape[0]):
        total = total + sums[peer]
    total = jnp.sum(total, axis=1, keepdims=True)
    energy, back_sq, fore_sq, cross, along_back, along_fore = (total[i : i + 1] for i in range(6))
    back_len = jnp.sqrt(back_sq + 1e-06)
    fore_len = jnp.sqrt(fore_sq + 1e-06)
    by_back, by_fore = 1.0 / back_len, 1.0 / fore_len
    tau_sq = (
        back_sq * by_back * by_back + fore_sq * by_fore * by_fore + 2.0 * cross * by_back * by_fore
    )
    proj = (along_back * by_back + along_fore * by_fore) / tau_sq
    spring = SPRING * (fore_len - back_len) / jnp.sqrt(tau_sq)
    climbing = flags[1] == 1
    is_end = flags[0] == 1
    factor = jnp.where(climbing, -2.0 * proj, spring - proj)
    here = pk[0:3, :]
    tangent = (here - behind[0:3, :]) * by_back + (ahead[0:3, :] - here) * by_fore
    moved = force[0:3, :] + factor * tangent
    result[0] = jnp.where(is_end, force[0:3, :], moved)
    energy_out[...] = energy * (1.0 / count)


def swap_pairs(count, offset):
    pairs = []
    for low in range(offset, count, 2):
        high = (low + 1) % count
        pairs += [(low, high), (high, low)]
    return pairs


def on_device(positions, species, counts, neighbours, send_list, climb, embed, ref_energy, rad_in, rad_out, mixing, w_energy):
    atoms = species.shape[0]
    rim = send_list.shape[0] // 2
    fan = neighbours.shape[0]
    chans = embed.shape[1]
    layers = mixing.shape[0]
    basis_count, units = rad_in.shape[1:]
    inner_blocks = atoms // rim - 2
    inner_atoms = inner_blocks * rim
    tiles = lax.axis_size("atom")
    images = lax.axis_size("img")
    core = lax.rem(lax.axis_index("atom"), 2)
    image = lax.axis_index("img")

    def call(body, operands, outs, scratch=()):
        scalars = {id(x) for x in (core_arr, ref_energy, flags)}
        return pl.pallas_call(
            body,
            out_shape=[jax.ShapeDtypeStruct(shape, dtype) for shape, dtype in outs],
            in_specs=[SMEM if id(x) in scalars else VMEM for x in operands],
            out_specs=[VMEM] * len(outs),
            scratch_shapes=[pltpu.VMEM(shape, dtype) for shape, dtype in scratch],
            compiler_params=pltpu.CompilerParams(vmem_limit_bytes=40 * 2**20),
        )(*operands)

    def swap(block, axis, offset):
        return lax.ppermute(block, axis, swap_pairs(lax.axis_size(axis), offset))

    core_arr = core.reshape(1).astype(I32)
    is_end = jnp.logical_or(image == 0, image == images - 1)
    flags = jnp.stack([is_end.astype(I32), climb[0]])
    pk = jnp.concatenate(
        [
            positions[0],
            species.astype(F32)[None],
            counts.astype(F32)[None],
            jnp.pad(send_list.astype(F32), (0, atoms - 2 * rim))[None],
            jnp.zeros((PACK_ROWS - 6, atoms), F32),
        ],
        axis=0,
    )
    w_row = w_energy[None]
    mate = swap(pk, "atom", 0)
    cross = swap(pk, "atom", 1)
    even = swap(pk, "img", 0)
    odd = swap(pk, "img", 1)

    feats_type = ((chans, atoms), BF16)
    halo_type = ((chans, rim), BF16)
    hid_scratch = [((fan * units, fan * basis_count), BF16), ((fan * units, rim), BF16)]
    table_scratch = [((chans, atoms + 2 * rim), BF16)]

    def block_outs(blocks):
        return [((blocks, 3 * fan, rim), F32), ((blocks, fan * basis_count, rim), BF16)]

    delta_in, basis_in, inner = call(
        functools.partial(first_inner, rim),
        (pk, neighbours, embed, rad_in, rad_out, mixing),
        block_outs(inner_blocks) + [((chans, inner_atoms), BF16)],
        hid_scratch,
    )
    delta_out, basis_out, feats, to_mate, to_cross = call(
        functools.partial(first_outer, rim),
        (core_arr, pk, mate, cross, neighbours, embed, rad_in, rad_out, mixing, inner),
        block_outs(2) + [feats_type, halo_type, halo_type],
        [((PACK_ROWS, atoms + 2 * rim), F32)] + hid_scratch,
    )
    hid_type = ((2, fan * units, rim), BF16)
    for layer in range(1, layers):
        mate = swap(to_mate, "atom", 0)
        cross = swap(to_cross, "atom", 1)
        inner, hid_edge = call(
            functools.partial(layer_inner, rim, layer),
            (pk, neighbours, rad_in, rad_out, mixing, feats, basis_in, basis_out),
            [((chans, inner_atoms), BF16), hid_type],
            hid_scratch,
        )
        feats, to_mate, to_cross = call(
            functools.partial(layer_outer, rim, layer),
            (core_arr, pk, neighbours, rad_out, mixing, feats, mate, cross, hid_edge, inner),
            [feats_type, halo_type, halo_type],
            table_scratch,
        )
    mate = swap(to_mate, "atom", 0)
    cross = swap(to_cross, "atom", 1)
    force_type = ((PACK_ROWS, atoms), F32)
    inner, hid_edge = call(
        functools.partial(head_inner, rim, layers),
        (pk, neighbours, rad_in, rad_out, feats, basis_in, delta_in, basis_out),
        [((PACK_ROWS, inner_atoms), F32), hid_type],
        hid_scratch,
    )
    odd_image = lax.rem(image, 2) == 1
    behind = jnp.where(odd_image, even, odd)
    ahead = jnp.where(odd_image, odd, even)
    force, sums = call(
        functools.partial(head_outer, rim, layers),
        (core_arr, ref_energy, pk, behind, ahead, neighbours, rad_out, w_row, feats, mate, cross, hid_edge, delta_out, inner),
        [force_type, ((tiles, SUM_ROWS, LANES), F32)],
        table_scratch,
    )
    sums = lax.all_to_all(sums, "atom", 0, 0)
    result, energy = call(
        functools.partial(finish, atoms * tiles),
        (flags, pk, behind, ahead, force, sums),
        [((1, 3, atoms), F32), ((1, 1), F32)],
    )
    return result, energy.reshape(1)


def solution(mesh):
    return jax.shard_map(
        on_device,
        mesh=mesh,
        in_specs=(
            P("img", None, "atom"),
            P("atom"),
            P("atom"),
            P(None, "atom"),
            P("atom"),
            P("img"),
            P(),
            P(),
            P(),
            P(),
            P(),
            P(),
        ),
        out_specs=(P("img", None, "atom"), P("img")),
        check_vma=False,
    )
```

```python
import functools
import math

import jax
import jax.numpy as jnp
from jax import lax
from jax.experimental import pallas as pl
from jax.experimental.pallas import tpu as pltpu
from jax.sharding import PartitionSpec as P

F32 = jnp.float32
BF16 = jnp.bfloat16
I32 = jnp.int32
LANES = 128
SPRING = 5.0
SPECIES_ROW = 3
COUNT_ROW = 4
SEND_ROW = 5
PACK_ROWS = 8
SUM_ROWS = 8
REDUCE_CHIPS = 4
VMEM = pl.BlockSpec(memory_space=pltpu.VMEM)
SMEM = pl.BlockSpec(memory_space=pltpu.SMEM)


def dot(a, b):
    return jnp.dot(a, b, preferred_element_type=F32)


def silu_of_half(half):
    return half + half * jnp.tanh(half)


def aligned(start, step):
    return pl.multiple_of(start, step)


def lane_fetch(windows, group, place):
    found = jnp.zeros(place.shape, F32)
    for k, window in enumerate(windows):
        rows = jnp.broadcast_to(window, place.shape)
        picked = jnp.take_along_axis(rows, place, axis=1, mode="promise_in_bounds")
        found = jnp.where(group == k, picked, found)
    return found


def live_slots(pk, lo, fan, width):
    slots = lax.broadcasted_iota(I32, (fan, width), 0).astype(F32)
    return slots < pk[COUNT_ROW : COUNT_ROW + 1, pl.ds(lo, width)]


def geometry(table, table_lo, pk, nbr, lo, rim):
    fan = nbr.shape[0]
    parts = []
    for half in range(rim // LANES):
        first = lo + half * LANES
        start = table_lo + half * LANES
        rel = nbr[:, pl.ds(aligned(first, LANES), LANES)] - first
        place = rel & (LANES - 1)
        group = rel // LANES
        live = live_slots(pk, aligned(first, LANES), fan, LANES)
        spans = [
            table[:, pl.ds(aligned(start + k * LANES, LANES), LANES)]
            for k in range(2 * rim // LANES + 1)
        ]
        deltas = []
        for c in range(3):
            far = lane_fetch([span[c : c + 1] for span in spans], group, place)
            deltas.append(far - pk[c : c + 1, pl.ds(aligned(first, LANES), LANES)])
        kinds = lane_fetch([span[SPECIES_ROW : SPECIES_ROW + 1] for span in spans], group, place)
        parts.append(deltas + [jnp.where(live, kinds, -1.0)])
    joined = [jnp.concatenate(list(piece), axis=1) for piece in zip(*parts)]
    return joined[:3], joined[3]


def basis_of(deltas, basis_count):
    dist_sq = deltas[0] * deltas[0] + deltas[1] * deltas[1] + deltas[2] * deltas[2]
    fan, width = dist_sq.shape
    centres = 2.0 * lax.broadcasted_iota(I32, (basis_count, width), 0).astype(F32)
    rows = []
    for s in range(fan):
        away = jnp.broadcast_to(dist_sq[s : s + 1], (basis_count, width)) - centres
        rows.append(jnp.exp(away * away * -0.125))
    return jnp.concatenate(rows, axis=0).astype(BF16)


def spread_first_layer(rad_in, layer, spread):
    count, units = rad_in.shape[1:]
    fan = spread.shape[0] // units
    half = rad_in[layer].astype(F32) * 0.5
    turned = jnp.concatenate([half] * fan, axis=0).T
    owner = lax.broadcasted_iota(I32, turned.shape, 1) // count
    for s in range(fan):
        spread[s * units : (s + 1) * units, :] = jnp.where(owner == s, turned, 0.0).astype(BF16)


def hidden_of(spread, basis):
    return silu_of_half(dot(spread[...], basis)).astype(BF16)


def turned_weight(ref, layer, scale=1.0):
    return (ref[layer].astype(F32) * scale).T.astype(BF16)


def fetch_rows(table, table_lo, places, s, rim):
    rows = lax.broadcasted_iota(I32, (rim, rim), 0).astype(F32).astype(BF16)
    one, zero = jnp.ones((), BF16), jnp.zeros((), BF16)
    picks = jnp.concatenate(
        [jnp.where(rows == place[s : s + 1], one, zero) for place in places], axis=0
    )
    return dot(table[:, pl.ds(table_lo, len(places) * rim)], picks)


def places_of(pk, nbr, lo, rim):
    fan = nbr.shape[0]
    rel = nbr[:, pl.ds(lo, rim)] - lo
    rel = jnp.where(live_slots(pk, lo, fan, rim), rel, -1)
    return [jnp.clip(rel - k * rim, -1, rim).astype(F32).astype(BF16) for k in range(3)]


def update_of(feats, summed, mix_half, fan):
    scaled = (summed * (1.0 / math.sqrt(fan))).astype(BF16)
    return (feats.astype(F32) + silu_of_half(dot(mix_half, scaled))).astype(BF16)


def first_block(table, table_lo, pk, nbr, lo, rim, weights, hid):
    embed_t, first, mix_half, spread = weights
    fan = nbr.shape[0]
    chans = mix_half.shape[0]
    kinds_count = embed_t.shape[1]
    units = spread.shape[0] // fan
    species = first.shape[1] // units
    deltas, kinds = geometry(table, table_lo, pk, nbr, lo, rim)
    basis = basis_of(deltas, spread.shape[1] // fan)
    hid[...] = hidden_of(spread, basis)
    kinds = kinds.astype(BF16)
    zero = jnp.zeros((), BF16)
    summed = jnp.zeros((chans, rim), F32)
    for s in range(fan):
        mine = hid[s * units : (s + 1) * units, :]
        kind = jnp.broadcast_to(kinds[s : s + 1], (units, rim))
        sorted_out = [
            jnp.where(kind == jnp.full((), k, BF16), mine, zero) for k in range(species)
        ]
        summed = summed + dot(first[...], jnp.concatenate(sorted_out, axis=0))
    rows = lax.broadcasted_iota(I32, (kinds_count, rim), 0).astype(F32)
    own = rows == pk[SPECIES_ROW : SPECIES_ROW + 1, pl.ds(lo, rim)]
    feats = dot(embed_t[...], jnp.where(own, 1.0, 0.0).astype(BF16))
    return deltas, basis, update_of(feats, summed, mix_half[...], fan)


def prepare(embed, rad_in, rad_out, mixing, embed_t, first, spread, out_t, mix_half):
    for layer in range(rad_in.shape[0]):
        spread_first_layer(rad_in, layer, spread.at[layer])
        out_t[layer] = turned_weight(rad_out, layer)
    for layer in range(mixing.shape[0]):
        mix_half[layer] = turned_weight(mixing, layer, 0.5)
    out = rad_out[0].astype(F32)
    table = embed[...].astype(F32)
    species = table.shape[0]
    kinds_count = embed_t.shape[1]
    padded = jnp.concatenate(
        [table, jnp.zeros((kinds_count - species, table.shape[1]), F32)], axis=0
    )
    embed_t[...] = padded.T.astype(BF16)
    scaled = jnp.concatenate([out * table[k : k + 1] for k in range(species)], axis=0)
    first[...] = scaled.T.astype(BF16)


def store_block(i, deltas, basis, delta_out, basis_out):
    fan = deltas[0].shape[0]
    for c in range(3):
        delta_out[i, c * fan : (c + 1) * fan, :] = deltas[c]
    basis_out[i] = basis


def first_inner(rim, pk, nbr, embed_hbm, rad_in_hbm, rad_out_hbm, mixing_hbm, w_hbm, ref_hbm, delta_out, basis_out, feats_out, embed_t, first, spread, out_t, mix_half, w_row, ref_row, embed, rad_in, rad_out, mixing, ref_energy, hid, sems):
    copies = [
        pltpu.make_async_copy(source, target, sems.at[i])
        for i, (source, target) in enumerate(
            (
                (embed_hbm, embed),
                (rad_in_hbm, rad_in),
                (rad_out_hbm, rad_out),
                (mixing_hbm, mixing),
                (w_hbm, w_row),
                (ref_hbm, ref_energy),
            )
        )
    ]
    for copy in copies:
        copy.start()
    for copy in copies:
        copy.wait()
    prepare(embed, rad_in, rad_out, mixing, embed_t, first, spread, out_t, mix_half)
    weights = (embed_t, first, mix_half.at[0], spread.at[0])

    def body(i, carry):
        lo = aligned((i + 1) * rim, rim)
        deltas, basis, feats = first_block(pk, lo - rim, pk, nbr, lo, rim, weights, hid)
        store_block(i, deltas, basis, delta_out, basis_out)
        feats_out[:, pl.ds(aligned(i * rim, rim), rim)] = feats
        return carry

    lax.fori_loop(0, feats_out.shape[1] // rim, body, 0)
    kinds = pk[SPECIES_ROW : SPECIES_ROW + 1, :]
    energy = jnp.zeros(kinds.shape, F32)
    for k in range(ref_energy.shape[0]):
        energy = jnp.where(kinds == float(k), ref_energy[k], energy)
    ref_row[...] = energy


def pack_halo(feats, pk, core, rim, to_mate, to_cross):
    atoms = feats.shape[1]
    rows = lax.broadcasted_iota(I32, (rim, rim), 0).astype(F32).astype(BF16)
    one, zero = jnp.ones((), BF16), jnp.zeros((), BF16)
    for ref, start in ((to_mate, (1 - core) * rim), (to_cross, core * rim)):
        wanted = pk[SEND_ROW : SEND_ROW + 1, pl.ds(aligned(start, rim), rim)]
        picks = jnp.concatenate(
            [
                jnp.where(
                    rows == jnp.clip(wanted - k * rim, -1.0, float(rim)).astype(BF16), one, zero
                )
                for k in range(atoms // rim)
            ],
            axis=0,
        )
        ref[...] = dot(feats[...], picks).astype(BF16)


def halo_places(core, atoms, rim):
    top = atoms + rim
    return aligned((1 - core) * top, rim), aligned(core * top, rim)


def first_outer(rim, core_ref, pk, mate, cross, nbr, embed_t, first, spread, mix_half, inner, delta_out, basis_out, feats_out, to_mate, to_cross, pair_out, table, hid):
    core = core_ref[0]
    atoms = pk.shape[1]
    weights = (embed_t, first, mix_half.at[0], spread.at[0])
    table[:, rim : rim + atoms] = pk[...]
    at_mate, at_cross = halo_places(core, atoms, rim)
    for ref, start, at in ((mate, core * rim, at_mate), (cross, (1 - core) * rim, at_cross)):
        for half in range(rim // LANES):
            wanted = ref[SEND_ROW : SEND_ROW + 1, pl.ds(aligned(start + half * LANES, LANES), LANES)]
            wanted = jnp.broadcast_to(wanted.astype(I32), (PACK_ROWS, LANES))
            spans = [ref[:, k * LANES : (k + 1) * LANES] for k in range(atoms // LANES)]
            table[:, pl.ds(aligned(at + half * LANES, LANES), LANES)] = lane_fetch(
                spans, wanted // LANES, wanted & (LANES - 1)
            )
    feats_out[:, rim : atoms - rim] = inner[...]
    pair_out[...] = jnp.concatenate([pk[0:4, :], mate[0:4, :]], axis=0)

    def body(i, carry):
        lo = aligned(i * (atoms - rim), rim)
        deltas, basis, feats = first_block(table, lo, pk, nbr, lo, rim, weights, hid)
        store_block(i, deltas, basis, delta_out, basis_out)
        feats_out[:, pl.ds(lo, rim)] = feats
        return carry

    lax.fori_loop(0, 2, body, 0)
    pack_halo(feats_out, pk, core, rim, to_mate, to_cross)


def layer_block(table, table_lo, pk, nbr, lo, rim, hid, out_t, mix_half, own):
    fan = nbr.shape[0]
    units = out_t.shape[1]
    places = places_of(pk, nbr, lo, rim)
    summed = jnp.zeros(own.shape, F32)
    for s in range(fan):
        far = fetch_rows(table, table_lo, places, s, rim)
        summed = summed + far * dot(out_t, hid(slice(s * units, (s + 1) * units)))
    return update_of(own, summed, mix_half, fan)


def layer_inner(rim, layer, pk, nbr, spreads, outs_t, mixes, feats, basis, basis_edge, feats_out, hid_edge, hid):
    spread, out_t, mix_half = spreads.at[layer], outs_t[layer], mixes[layer]

    def body(i, carry):
        lo = aligned((i + 1) * rim, rim)
        hid[...] = hidden_of(spread, basis[i])
        own = feats[:, pl.ds(lo, rim)]
        feats_out[:, pl.ds(aligned(i * rim, rim), rim)] = layer_block(
            feats, aligned(lo - rim, rim), pk, nbr, lo, rim, lambda r: hid[r, :], out_t, mix_half, own
        )
        return carry

    lax.fori_loop(0, basis.shape[0], body, 0)
    for i in range(2):
        hid_edge[i] = hidden_of(spread, basis_edge[i])


def fill_table(table, feats, mate, cross, core, rim):
    atoms = feats.shape[1]
    at_mate, at_cross = halo_places(core, atoms, rim)
    table[:, rim : rim + atoms] = feats[...]
    table[:, pl.ds(at_mate, rim)] = mate[...]
    table[:, pl.ds(at_cross, rim)] = cross[...]


def layer_outer(rim, layer, core_ref, pk, nbr, outs_t, mixes, feats, mate, cross, hid_edge, inner, feats_out, to_mate, to_cross, table):
    core = core_ref[0]
    atoms = pk.shape[1]
    out_t, mix_half = outs_t[layer], mixes[layer]
    fill_table(table, feats, mate, cross, core, rim)
    feats_out[:, rim : atoms - rim] = inner[...]

    def body(i, carry):
        lo = aligned(i * (atoms - rim), rim)
        own = feats[:, pl.ds(lo, rim)]
        feats_out[:, pl.ds(lo, rim)] = layer_block(
            table, lo, pk, nbr, lo, rim, lambda r: hid_edge[i, r, :], out_t, mix_half, own
        )
        return carry

    lax.fori_loop(0, 2, body, 0)
    pack_halo(feats_out, pk, core, rim, to_mate, to_cross)


def head_block(table, table_lo, pk, nbr, lo, rim, hid, out_t, own, delta):
    fan = nbr.shape[0]
    chans, units = out_t.shape
    places = places_of(pk, nbr, lo, rim)
    near = own.astype(F32)
    pairs = []
    for s in range(fan):
        far = fetch_rows(table, table_lo, places, s, rim)
        terms = far * (dot(out_t, hid(slice(s * units, (s + 1) * units))) * near)
        pairs.append(jnp.sum(terms, axis=0, keepdims=True))
    pair = jnp.concatenate(pairs, axis=0) * (1.0 / math.sqrt(chans))
    rows = [
        jnp.sum(pair * delta[c * fan : (c + 1) * fan, :], axis=0, keepdims=True) for c in range(3)
    ]
    return jnp.concatenate(rows + [jnp.zeros((PACK_ROWS - 3, rim), F32)], axis=0)


def head_inner(rim, layer, pk, nbr, spreads, outs_t, feats, basis, delta, basis_edge, force_out, hid_edge, hid):
    spread, out_t = spreads.at[layer], outs_t[layer]

    def body(i, carry):
        lo = aligned((i + 1) * rim, rim)
        hid[...] = hidden_of(spread, basis[i])
        force_out[:, pl.ds(aligned(i * rim, rim), rim)] = head_block(
            feats, aligned(lo - rim, rim), pk, nbr, lo, rim, lambda r: hid[r, :], out_t,
            feats[:, pl.ds(lo, rim)], delta.at[i],
        )
        return carry

    lax.fori_loop(0, basis.shape[0], body, 0)
    for i in range(2):
        hid_edge[i] = hidden_of(spread, basis_edge[i])


def lane_sum(values):
    total = values[:, :LANES]
    for k in range(1, values.shape[1] // LANES):
        total = total + values[:, k * LANES : (k + 1) * LANES]
    return jnp.sum(total, axis=0, keepdims=True)


def neighbour_images(core, received, relayed):
    first = core == 0
    behind = jnp.where(first, relayed[0:3, :], received[4:7, :])
    ahead = jnp.where(first, received[4:7, :], relayed[0:3, :])
    return behind, ahead


def head_outer(rim, layer, core_ref, pk, received, relayed, nbr, outs_t, w_row, ref_row, feats, mate, cross, hid_edge, delta, inner, force_out, sums_out, table):
    core = core_ref[0]
    atoms = pk.shape[1]
    out_t = outs_t[layer]
    fill_table(table, feats, mate, cross, core, rim)
    force_out[:, rim : atoms - rim] = inner[...]

    def body(i, carry):
        lo = aligned(i * (atoms - rim), rim)
        force_out[:, pl.ds(lo, rim)] = head_block(
            table, lo, pk, nbr, lo, rim, lambda r: hid_edge[i, r, :], out_t,
            feats[:, pl.ds(lo, rim)], delta.at[i],
        )
        return carry

    lax.fori_loop(0, 2, body, 0)
    energy = dot(w_row[...], feats[...]) + ref_row[...]
    behind, ahead = neighbour_images(core, received, relayed)
    here = pk[0:3, :]
    back = here - behind
    fore = ahead - here
    force = force_out[0:3, :]
    rows = [energy, back * back, fore * fore, back * fore, force * back, force * fore]
    sums = [lane_sum(row) for row in rows]
    sums.append(jnp.zeros((SUM_ROWS - len(sums), LANES), F32))
    sums_out[...] = jnp.concatenate(sums, axis=0)


def finish(count, core_ref, flags, pk, received, relayed, force, *rest):
    *parts, result, energy_out = rest
    total = parts[0][...]
    for part in parts[1:]:
        total = total + part[...]
    total = total[:SUM_ROWS] + total[SUM_ROWS:]
    total = jnp.sum(total, axis=1, keepdims=True)
    energy, back_sq, fore_sq, cross, along_back, along_fore = (total[i : i + 1] for i in range(6))
    back_len = jnp.sqrt(back_sq + 1e-06)
    fore_len = jnp.sqrt(fore_sq + 1e-06)
    by_back, by_fore = 1.0 / back_len, 1.0 / fore_len
    tau_sq = (
        back_sq * by_back * by_back + fore_sq * by_fore * by_fore + 2.0 * cross * by_back * by_fore
    )
    proj = (along_back * by_back + along_fore * by_fore) / tau_sq
    spring = SPRING * (fore_len - back_len) / jnp.sqrt(tau_sq)
    climbing = flags[1] == 1
    is_end = flags[0] == 1
    factor = jnp.where(climbing, -2.0 * proj, spring - proj)
    here = pk[0:3, :]
    behind, ahead = neighbour_images(core_ref[0], received, relayed)
    tangent = (here - behind) * by_back + (ahead - here) * by_fore
    moved = jnp.where(is_end, force[0:3, :], force[0:3, :] + factor * tangent)
    for c in range(3):
        result[c] = moved[c : c + 1]
    energy_out[...] = energy * (1.0 / count)


def swap_pairs(count, offset):
    pairs = []
    for low in range(offset, count, 2):
        high = (low + 1) % count
        pairs += [(low, high), (high, low)]
    return pairs


def on_device(positions, species, counts, neighbours, send_list, climb, embed, ref_energy, rad_in, rad_out, mixing, w_energy):
    atoms = species.shape[0]
    rim = send_list.shape[0] // 2
    fan = neighbours.shape[0]
    chans = embed.shape[1]
    layers = mixing.shape[0]
    basis_count, units = rad_in.shape[1:]
    inner_blocks = atoms // rim - 2
    inner_atoms = inner_blocks * rim
    tiles = lax.axis_size("atom")
    images = lax.axis_size("img")
    core = lax.rem(lax.axis_index("atom"), 2)
    image = lax.axis_index("img")

    def call(body, operands, outs, scratch=(), far=()):
        scalars = {id(x) for x in (core_arr, flags)}
        far = {id(x) for x in far}
        return pl.pallas_call(
            body,
            out_shape=[jax.ShapeDtypeStruct(shape, dtype) for shape, dtype in outs],
            in_specs=[
                SMEM if id(x) in scalars else pl.BlockSpec(memory_space=pl.ANY) if id(x) in far else VMEM
                for x in operands
            ],
            out_specs=[VMEM] * len(outs),
            scratch_shapes=[
                x if not isinstance(x, tuple) else pltpu.VMEM(*x) for x in scratch
            ],
            compiler_params=pltpu.CompilerParams(vmem_limit_bytes=40 * 2**20),
        )(*operands)

    def swap(block, offset):
        return lax.ppermute(block, "atom", swap_pairs(tiles, offset))

    core_arr = core.reshape(1).astype(I32)
    is_end = jnp.logical_or(image == 0, image == images - 1)
    flags = jnp.stack([is_end.astype(I32), climb[0]])
    pk = jnp.concatenate(
        [
            positions[0],
            species.astype(F32)[None],
            counts.astype(F32)[None],
            jnp.pad(send_list.astype(F32), (0, atoms - 2 * rim))[None],
            jnp.zeros((PACK_ROWS - 6, atoms), F32),
        ],
        axis=0,
    )
    w_row = w_energy[None]
    mate = swap(pk, 0)
    cross = swap(pk, 1)

    feats_type = ((chans, atoms), BF16)
    halo_type = ((chans, rim), BF16)
    kinds_count = -(-embed.shape[0] // 16) * 16
    weight_types = [
        ((chans, kinds_count), BF16),
        ((chans, embed.shape[0] * units), BF16),
        ((layers + 1, fan * units, fan * basis_count), BF16),
        ((layers + 1, chans, units), BF16),
        ((layers, chans, chans), BF16),
        ((1, chans), BF16),
        ((1, atoms), F32),
    ]
    hid_scratch = ((fan * units, rim), BF16)
    table_scratch = [((chans, atoms + 2 * rim), BF16)]

    def block_outs(blocks):
        return [((blocks, 3 * fan, rim), F32), ((blocks, fan * basis_count, rim), BF16)]

    weights = (embed, rad_in, rad_out, mixing, w_row, ref_energy)
    delta_in, basis_in, inner, embed_t, first, spread, out_t, mix_half, w_row, ref_row = call(
        functools.partial(first_inner, rim),
        (pk, neighbours) + weights,
        block_outs(inner_blocks) + [((chans, inner_atoms), BF16)] + weight_types,
        [(x.shape, x.dtype) for x in weights[:4]]
        + [pltpu.SMEM(ref_energy.shape, F32), hid_scratch, pltpu.SemaphoreType.DMA((6,))],
        weights,
    )
    delta_out, basis_out, feats, to_mate, to_cross, pair = call(
        functools.partial(first_outer, rim),
        (core_arr, pk, mate, cross, neighbours, embed_t, first, spread, mix_half, inner),
        block_outs(2) + [feats_type, halo_type, halo_type, ((PACK_ROWS, atoms), F32)],
        [((PACK_ROWS, atoms + 2 * rim), F32), hid_scratch],
    )
    image_pairs = []
    for low in range(images):
        high = (low + 1) % images
        for tile in range(0, tiles, 2):
            a, b = low * tiles + tile, high * tiles + tile + 1
            image_pairs += [(a, b), (b, a)]
    hid_type = ((2, fan * units, rim), BF16)
    for layer in range(1, layers):
        mate = swap(to_mate, 0)
        cross = swap(to_cross, 1)
        inner, hid_edge = call(
            functools.partial(layer_inner, rim, layer),
            (pk, neighbours, spread, out_t, mix_half, feats, basis_in, basis_out),
            [((chans, inner_atoms), BF16), hid_type],
            [hid_scratch],
        )
        feats, to_mate, to_cross = call(
            functools.partial(layer_outer, rim, layer),
            (core_arr, pk, neighbours, out_t, mix_half, feats, mate, cross, hid_edge, inner),
            [feats_type, halo_type, halo_type],
            table_scratch,
        )
    received = lax.ppermute(pair, ("img", "atom"), image_pairs)
    relayed = swap(received, 0)
    mate = swap(to_mate, 0)
    cross = swap(to_cross, 1)
    force_type = ((PACK_ROWS, atoms), F32)
    inner, hid_edge = call(
        functools.partial(head_inner, rim, layers),
        (pk, neighbours, spread, out_t, feats, basis_in, delta_in, basis_out),
        [((PACK_ROWS, inner_atoms), F32), hid_type],
        [hid_scratch],
    )
    force, sums = call(
        functools.partial(head_outer, rim, layers),
        (core_arr, pk, received, relayed, neighbours, out_t, w_row, ref_row, feats, mate, cross, hid_edge, delta_out, inner),
        [force_type, ((SUM_ROWS, LANES), F32)],
        table_scratch,
    )
    step = 2 * REDUCE_CHIPS
    while step < tiles:
        sums = sums + lax.ppermute(sums, "atom", [(i, i ^ step) for i in range(tiles)])
        step *= 2
    both = jnp.concatenate([sums, swap(sums, 0)], axis=0)
    near = lax.ppermute(both, "atom", [(i, i ^ 2 if i % 2 == 0 else i ^ 6) for i in range(tiles)])
    far = lax.ppermute(both, "atom", [(i, i ^ 4) for i in range(tiles)])
    other = swap(near, 0)
    result, energy = call(
        functools.partial(finish, atoms * tiles),
        (core_arr, flags, pk, received, relayed, force, both, near, far, other),
        [((3, 1, atoms), F32), ((1, 1), F32)],
    )
    return jnp.transpose(result, (1, 0, 2)), energy.reshape(1)


def solution(mesh):
    return jax.shard_map(
        on_device,
        mesh=mesh,
        in_specs=(
            P("img", None, "atom"),
            P("atom"),
            P("atom"),
            P(None, "atom"),
            P("atom"),
            P("img"),
            P(),
            P(),
            P(),
            P(),
            P(),
            P(),
        ),
        out_specs=(P("img", None, "atom"), P("img")),
        check_vma=False,
    )
```

```python
import functools
import math

import jax
import jax.numpy as jnp
from jax import lax
from jax.experimental import pallas as pl
from jax.experimental.pallas import tpu as pltpu
from jax.sharding import PartitionSpec as P

F32 = jnp.float32
BF16 = jnp.bfloat16
I32 = jnp.int32
LANES = 128
SPRING = 5.0
SPECIES_ROW = 3
COUNT_ROW = 4
SEND_ROW = 5
SEAT_ROW = 6
PACK_ROWS = 8
SUM_ROWS = 8
REDUCE_CHIPS = 4
VMEM = pl.BlockSpec(memory_space=pltpu.VMEM)
SMEM = pl.BlockSpec(memory_space=pltpu.SMEM)


def dot(a, b):
    return jnp.dot(a, b, preferred_element_type=F32)


def silu_of_half(half):
    return half + half * jnp.tanh(half)


def aligned(start, step):
    return pl.multiple_of(start, step)


def halves(width):
    return [slice(k * LANES, (k + 1) * LANES) for k in range(width // LANES)]


def short_rows(fan):
    return -(-5 * fan // 8)


def lane_fetch(windows, group, place):
    found = jnp.zeros(place.shape, F32)
    for k, window in enumerate(windows):
        rows = jnp.broadcast_to(window, place.shape)
        picked = jnp.take_along_axis(rows, place, axis=1, mode="promise_in_bounds")
        found = jnp.where(group == k, picked, found)
    return found


def lane_lookup(windows, index):
    return lane_fetch(windows, index // LANES, index & (LANES - 1))


def seat_atoms(pk, lo, width):
    counts = pk[COUNT_ROW : COUNT_ROW + 1, lo : lo + width]
    lane = lax.broadcasted_iota(I32, (1, width), 1).astype(F32)
    key = counts * float(width) - lane

    def down(row):
        turned = jnp.broadcast_to(row, (LANES, width)).T
        return jnp.concatenate([turned] * (width // LANES), axis=1)

    rank = jnp.sum(jnp.where(down(key) > key, 1.0, 0.0), axis=0, keepdims=True)
    seat = jnp.where(rank < width // 2, rank, 1.5 * width - 1.0 - rank)
    atom = lax.broadcasted_iota(I32, (width, width), 0).astype(F32)
    taker = jnp.sum(jnp.where(down(seat) == lane, atom, 0.0), axis=0, keepdims=True)
    return seat, taker


def seat_block(b, pk, nbr, lo, width, seated, edges, owns, depth):
    fan = nbr.shape[0]
    short = short_rows(fan)
    seat, taker = seat_atoms(pk, lo, width)
    pieces, tables = [], []
    for part in halves(width):
        who = taker[:, part].astype(I32)
        spans = [nbr[:, lo + p.start : lo + p.stop] for p in halves(width)]
        pieces.append(lane_lookup(spans, jnp.broadcast_to(who, (fan, LANES))) - float(lo))
        spans = [pk[:, lo + p.start : lo + p.stop] for p in halves(width)]
        tables.append(lane_lookup(spans, jnp.broadcast_to(who, (PACK_ROWS, LANES))))
    first, second = pieces
    first_count, second_count = (x[COUNT_ROW : COUNT_ROW + 1] for x in tables)
    most = jnp.max(first_count + second_count, axis=1, keepdims=True)
    fits = most <= float(2 * short)
    limit = jnp.where(fits, float(short), float(fan))
    row = lax.broadcasted_iota(I32, (fan, LANES), 0).astype(F32)
    mine = row < second_count
    over = [first[2 * short - 1 - r : 2 * short - r] if 0 <= 2 * short - 1 - r < fan else first[:1] for r in range(fan)]
    over = jnp.concatenate(over, axis=0)
    spilled = jnp.logical_and(fits, 2.0 * short - 1.0 - row < first_count)
    spilled = jnp.logical_and(spilled, row < float(short))
    spilled = jnp.logical_and(spilled, row >= float(2 * short - fan))
    spilled = jnp.logical_and(spilled, jnp.logical_not(mine))
    first = jnp.where(row < jnp.minimum(first_count, limit), first, -1.0)
    second = jnp.where(mine, second, jnp.where(spilled, over, -1.0))
    edges[b] = jnp.concatenate([first, second], axis=1)
    owns[b] = jnp.where(spilled, 0.0, 1.0)
    depth[b] = jnp.broadcast_to(limit, (PACK_ROWS, LANES))
    seated[:, lo : lo + width] = jnp.concatenate(tables, axis=1)
    return seat


def by_depth(depth, fan, run):
    shallow = jnp.max(depth) < float(short_rows(fan)) + 0.5

    @pl.when(shallow)
    def _():
        run(short_rows(fan))

    @pl.when(jnp.logical_not(shallow))
    def _():
        run(fan)


def locate_block(i, table, table_lo, seated, edges, own, lo, width, delta_out, basis_out, kinds_out, place_out):
    fan = edges.shape[0]
    spans = [
        table[:, pl.ds(aligned(table_lo + k * LANES, LANES), LANES)]
        for k in range(3 * width // LANES)
    ]
    mine = own > 0.5
    home = seated[:, pl.ds(lo, width)]
    parts = []
    for part in halves(width):
        rel = edges[:, part].astype(I32)
        live = rel >= 0
        group, place = rel >> 7, rel & (LANES - 1)
        fetch = lambda r: lane_fetch([span[r : r + 1] for span in spans], group, place)
        values = []
        for c in range(3):
            here = home[c : c + 1, part]
            if part.start > 0:
                here = jnp.where(mine, here, home[c : c + 1, :LANES])
            values.append(fetch(c) - here)
        values.append(jnp.where(live, fetch(SPECIES_ROW), -1.0))
        tile = (rel // width).astype(F32) * float(width)
        values.append(jnp.where(live, fetch(SEAT_ROW) + tile, -1.0))
        parts.append(values)
    joined = [jnp.concatenate(list(piece), axis=1) for piece in zip(*parts)]
    for c in range(3):
        delta_out[i, c * fan : (c + 1) * fan, :] = joined[c]
    kinds_out[i] = joined[3]
    place_out[i] = joined[4]
    dist_sq = joined[0] * joined[0] + joined[1] * joined[1] + joined[2] * joined[2]
    count = basis_out.shape[1] // fan
    centres = 2.0 * lax.broadcasted_iota(I32, (count, width), 0).astype(F32)
    rows = []
    for s in range(fan):
        away = jnp.broadcast_to(dist_sq[s : s + 1], (count, width)) - centres
        rows.append(jnp.exp(away * away * -0.125))
    basis_out[i] = jnp.concatenate(rows, axis=0).astype(BF16)


def fill_hidden(target, spread, basis, rows, fan):
    used = rows * (spread.shape[0] // fan)
    target[:used, :] = silu_of_half(dot(spread[:used, :], basis)).astype(BF16)


class Sums:
    def __init__(self, shape, own, rows, fan):
        self.total = jnp.zeros(shape, F32)
        self.lent = jnp.zeros((shape[0], LANES), F32)
        self.own, self.alone = own, 2 * rows - fan

    def add(self, s, terms):
        self.total = self.total + terms
        if s >= self.alone:
            self.lent = self.lent + jnp.where(self.own[s : s + 1] > 0.5, 0.0, terms[:, LANES:])

    def done(self):
        first, second = self.total[:, :LANES], self.total[:, LANES:]
        return jnp.concatenate([first + self.lent, second - self.lent], axis=1)


def update_of(feats, summed, mix_half, fan):
    scaled = (summed * (1.0 / math.sqrt(fan))).astype(BF16)
    return (feats.astype(F32) + silu_of_half(dot(mix_half, scaled))).astype(BF16)


def first_block(rows, kinds, basis, own, seated, lo, width, weights, hid):
    embed_t, first, mix_half, spread = weights
    fan = kinds.shape[0]
    kinds_count = embed_t.shape[1]
    units = spread.shape[0] // fan
    species = first.shape[1] // units
    fill_hidden(hid, spread, basis, rows, fan)
    kinds = kinds.astype(BF16)
    zero = jnp.zeros((), BF16)
    sums = Sums((mix_half.shape[0], width), own, rows, fan)
    for s in range(rows):
        mine = hid[s * units : (s + 1) * units, :]
        kind = jnp.broadcast_to(kinds[s : s + 1], (units, width))
        sorted_out = [
            jnp.where(kind == jnp.full((), k, BF16), mine, zero) for k in range(species)
        ]
        sums.add(s, dot(first[...], jnp.concatenate(sorted_out, axis=0)))
    rows_of = lax.broadcasted_iota(I32, (kinds_count, width), 0).astype(F32)
    same = rows_of == seated[SPECIES_ROW : SPECIES_ROW + 1, pl.ds(lo, width)]
    feats = dot(embed_t[...], jnp.where(same, 1.0, 0.0).astype(BF16))
    return update_of(feats, sums.done(), mix_half[...], fan)


def turned(matrix):
    size = matrix.shape[1]
    row = lax.broadcasted_iota(I32, (size, size), 0)
    column = lax.broadcasted_iota(I32, (size, size), 1)
    identity = jnp.where(row == column, 1.0, 0.0).astype(BF16)
    return lax.dot_general(
        identity, matrix, (((1,), (1,)), ((), ())), preferred_element_type=F32
    )


def prepare(embed, rad_in, rad_out, mixing, embed_t, first, spread, out_t, mix_half):
    layers, count, units = rad_in.shape
    fan = spread.shape[1] // units
    for layer in range(layers):
        half = rad_in[layer].astype(F32) * 0.5
        weight = turned(jnp.concatenate([half] * fan, axis=0).astype(BF16))
        owner = lax.broadcasted_iota(I32, weight.shape, 1) // count
        for s in range(fan):
            only = jnp.where(owner == s, weight, 0.0).astype(BF16)
            spread[layer, s * units : (s + 1) * units, :] = only
        out_t[layer] = turned(rad_out[layer]).astype(BF16)
    for layer in range(mixing.shape[0]):
        mix_half[layer] = (turned(mixing[layer]) * 0.5).astype(BF16)
    out = rad_out[0].astype(F32)
    table = embed[...].astype(F32)
    species = table.shape[0]
    padded = jnp.concatenate(
        [table, jnp.zeros((embed_t.shape[1] - species, table.shape[1]), F32)], axis=0
    )
    embed_t[...] = turned(padded.astype(BF16)).astype(BF16)
    scaled = jnp.concatenate([out * table[k : k + 1] for k in range(species)], axis=0)
    first[...] = turned(scaled.astype(BF16)).astype(BF16)


def seat_tile(width, pk, nbr, table, seated, edges, owns, depth, delta_out, basis_out, kinds_out, place_out, index):
    atoms = pk.shape[1]
    blocks = atoms // width
    index[...] = nbr[...].astype(F32)
    table[...] = pk[...]
    for b in range(blocks):
        seat = seat_block(b, pk, index, b * width, width, seated, edges, owns, depth)
        table[SEAT_ROW : SEAT_ROW + 1, b * width : (b + 1) * width] = seat
    for part in halves(2 * width):
        wanted = jnp.broadcast_to(pk[SEND_ROW : SEND_ROW + 1, part].astype(I32), (PACK_ROWS, LANES))
        seats = lane_lookup([table[SEAT_ROW : SEAT_ROW + 1, p] for p in halves(atoms)], wanted)
        seats = seats + (wanted // width).astype(F32) * float(width)
        table[SEND_ROW : SEND_ROW + 1, part] = seats[:1]

    def body(i, carry):
        lo = aligned((i + 1) * width, width)
        locate_block(
            i, table, lo - width, seated, edges[i + 1], owns[i + 1], lo, width,
            delta_out, basis_out, kinds_out, place_out,
        )
        return carry

    lax.fori_loop(0, blocks - 2, body, 0)


def first_inner(width, ref_energy, pk, seated, owns, depth, basis, kinds, embed, rad_in, rad_out, mixing, w_in, feats_out, embed_t, first, spread, out_t, mix_half, w_row, ref_row, hid):
    prepare(embed, rad_in, rad_out, mixing, embed_t, first, spread, out_t, mix_half)
    weights = (embed_t, first, mix_half.at[0], spread.at[0])
    w_row[...] = w_in[...]
    kinds_row = pk[SPECIES_ROW : SPECIES_ROW + 1, :]
    energy = jnp.zeros(kinds_row.shape, F32)
    for k in range(ref_energy.shape[0]):
        energy = jnp.where(kinds_row == float(k), ref_energy[k], energy)
    ref_row[...] = energy

    def body(i, carry):
        lo = aligned((i + 1) * width, width)

        def run(rows):
            feats_out[:, pl.ds(aligned(i * width, width), width)] = first_block(
                rows, kinds[i], basis[i], owns.at[i + 1], seated, lo, width, weights, hid
            )

        by_depth(depth[i + 1], kinds.shape[1], run)
        return carry

    lax.fori_loop(0, kinds.shape[0], body, 0)


def pack_halo(feats, table, core, width, to_mate, to_cross):
    atoms = feats.shape[1]
    rows = lax.broadcasted_iota(I32, (width, width), 0).astype(F32).astype(BF16)
    one, zero = jnp.ones((), BF16), jnp.zeros((), BF16)
    for ref, start in ((to_mate, (1 - core) * width), (to_cross, core * width)):
        wanted = table[SEND_ROW : SEND_ROW + 1, pl.ds(aligned(start, width), width)]
        picks = []
        for k in range(atoms // width):
            place = jnp.clip(wanted - float(k * width), -1.0, float(width)).astype(BF16)
            picks.append(jnp.where(rows == place, one, zero))
        ref[...] = dot(feats[...], jnp.concatenate(picks, axis=0)).astype(BF16)


def halo_places(core, atoms, width):
    top = atoms + width
    return aligned((1 - core) * top, width), aligned(core * top, width)


def edge_block(i, blocks, width):
    block = i * (blocks - 1)
    return block, aligned(block * width, width)


def first_outer(width, core_ref, pk, own_table, seated, mate, cross, edges, owns, depth, embed_t, first, spread, mix_half, inner, delta_out, basis_out, place_out, feats_out, to_mate, to_cross, pair_out, table, hid, kinds):
    core = core_ref[0]
    atoms = pk.shape[1]
    blocks = atoms // width
    fan = edges.shape[1]
    weights = (embed_t, first, mix_half.at[0], spread.at[0])
    table[:, width : width + atoms] = own_table[...]
    at_mate, at_cross = halo_places(core, atoms, width)
    for ref, start, at in ((mate, core * width, at_mate), (cross, (1 - core) * width, at_cross)):
        spans = [ref[:, part] for part in halves(atoms)]
        for k in range(width // LANES):
            wanted = ref[SEND_ROW : SEND_ROW + 1, pl.ds(aligned(start + k * LANES, LANES), LANES)]
            wanted = jnp.broadcast_to(wanted.astype(I32), (PACK_ROWS, LANES))
            place = pl.ds(aligned(at + k * LANES, LANES), LANES)
            table[:, place] = lane_lookup(spans, wanted)
            lane = lax.broadcasted_iota(I32, (1, LANES), 1) + k * LANES
            table[SEAT_ROW : SEAT_ROW + 1, place] = lane.astype(F32)
    feats_out[:, width : atoms - width] = inner[...]
    pair_out[0:4, :] = pk[0:4, :]
    pair_out[4:8, :] = mate[0:4, :]

    def body(i, carry):
        b, lo = edge_block(i, blocks, width)
        locate_block(
            i, table, lo, seated, edges[b], owns[b], lo, width,
            delta_out, basis_out, kinds, place_out,
        )

        def run(rows):
            feats_out[:, pl.ds(lo, width)] = first_block(
                rows, kinds[i], basis_out[i], owns.at[b], seated, lo, width, weights, hid
            )

        by_depth(depth[b], fan, run)
        return carry

    lax.fori_loop(0, 2, body, 0)
    pack_halo(feats_out, own_table, core, width, to_mate, to_cross)


def places_of(place, width):
    return [jnp.clip(place - float(k * width), -1.0, float(width)).astype(BF16) for k in range(3)]


def fetch_rows(window, places, s, width):
    rows = lax.broadcasted_iota(I32, (width, width), 0).astype(F32).astype(BF16)
    one, zero = jnp.ones((), BF16), jnp.zeros((), BF16)
    picks = [jnp.where(rows == place[s : s + 1], one, zero) for place in places]
    return dot(window, jnp.concatenate(picks, axis=0))


def layer_block(rows, window, place, own, hid, out_t, mix_half, feats):
    fan, width = place.shape
    units = out_t.shape[1]
    places = places_of(place, width)
    sums = Sums(feats.shape, own, rows, fan)
    for s in range(rows):
        far = fetch_rows(window, places, s, width)
        sums.add(s, far * dot(out_t, hid[s * units : (s + 1) * units, :]))
    return update_of(feats, sums.done(), mix_half, fan)


def hidden_edges(depth, spread, basis, hid_edge, blocks, fan):
    def body(i, carry):
        by_depth(
            depth[i * (blocks - 1)], fan,
            lambda rows: fill_hidden(hid_edge.at[i], spread, basis[i], rows, fan),
        )
        return carry

    lax.fori_loop(0, 2, body, 0)


def layer_inner(width, layer, owns, depth, spreads, outs_t, mixes, feats, basis, place, basis_edge, pair, feats_out, hid_edge, pair_out, hid):
    spread, out_t, mix_half = spreads.at[layer], outs_t[layer], mixes[layer]
    fan = place.shape[1]
    pair_out[...] = pair[...]

    def body(i, carry):
        lo = aligned((i + 1) * width, width)

        def run(rows):
            fill_hidden(hid, spread, basis[i], rows, fan)
            feats_out[:, pl.ds(aligned(i * width, width), width)] = layer_block(
                rows, feats[:, pl.ds(aligned(lo - width, width), 3 * width)], place[i],
                owns.at[i + 1], hid, out_t, mix_half, feats[:, pl.ds(lo, width)],
            )

        by_depth(depth[i + 1], fan, run)
        return carry

    lax.fori_loop(0, place.shape[0], body, 0)
    hidden_edges(depth, spread, basis_edge, hid_edge, place.shape[0] + 2, fan)


def fill_table(table, feats, mate, cross, core, width):
    atoms = feats.shape[1]
    at_mate, at_cross = halo_places(core, atoms, width)
    table[:, width : width + atoms] = feats[...]
    table[:, pl.ds(at_mate, width)] = mate[...]
    table[:, pl.ds(at_cross, width)] = cross[...]


def layer_outer(width, layer, core_ref, own_table, owns, depth, outs_t, mixes, feats, place, mate, cross, hid_edge, inner, feats_out, to_mate, to_cross, table):
    core = core_ref[0]
    atoms = feats.shape[1]
    fan = place.shape[1]
    out_t, mix_half = outs_t[layer], mixes[layer]
    fill_table(table, feats, mate, cross, core, width)
    feats_out[:, width : atoms - width] = inner[...]

    def body(i, carry):
        b, lo = edge_block(i, atoms // width, width)

        def run(rows):
            feats_out[:, pl.ds(lo, width)] = layer_block(
                rows, table[:, pl.ds(lo, 3 * width)], place[i], owns.at[b],
                hid_edge.at[i], out_t, mix_half, feats[:, pl.ds(lo, width)],
            )

        by_depth(depth[b], fan, run)
        return carry

    lax.fori_loop(0, 2, body, 0)
    pack_halo(feats_out, own_table, core, width, to_mate, to_cross)


def head_block(rows, window, place, own, hid, out_t, feats, delta, seat):
    fan, width = place.shape
    chans, units = out_t.shape
    places = places_of(place, width)
    near = feats.astype(F32)
    pairs = []
    for s in range(rows):
        far = fetch_rows(window, places, s, width)
        here = near
        if s >= 2 * rows - fan:
            lower = jnp.where(own[s : s + 1] > 0.5, near[:, LANES:], near[:, :LANES])
            here = jnp.concatenate([near[:, :LANES], lower], axis=1)
        terms = far * (dot(out_t, hid[s * units : (s + 1) * units, :]) * here)
        pairs.append(jnp.sum(terms, axis=0, keepdims=True))
    if rows < fan:
        pairs.append(jnp.zeros((fan - rows, width), F32))
    pair = jnp.concatenate(pairs, axis=0) * (1.0 / math.sqrt(chans))
    mine = own[...] > 0.5
    out = []
    for c in range(3):
        terms = pair * delta[c * fan : (c + 1) * fan, :]
        second = terms[:, LANES:]
        lent = jnp.where(mine, 0.0, second)
        out.append(
            jnp.concatenate(
                [
                    jnp.sum(terms[:, :LANES] + lent, axis=0, keepdims=True),
                    jnp.sum(jnp.where(mine, second, 0.0), axis=0, keepdims=True),
                ],
                axis=1,
            )
        )
    seated = jnp.concatenate(out + [jnp.zeros((PACK_ROWS - 3, width), F32)], axis=0)
    spans = [seated[:, part] for part in halves(width)]
    seat = seat.astype(I32)
    return jnp.concatenate(
        [
            lane_lookup(spans, jnp.broadcast_to(seat[:, part], (PACK_ROWS, LANES)))
            for part in halves(width)
        ],
        axis=1,
    )


def head_inner(width, layer, own_table, owns, depth, spreads, outs_t, feats, basis, place, delta, basis_edge, force_out, hid_edge, hid):
    spread, out_t = spreads.at[layer], outs_t[layer]
    fan = place.shape[1]

    def body(i, carry):
        lo = aligned((i + 1) * width, width)

        def run(rows):
            fill_hidden(hid, spread, basis[i], rows, fan)
            force_out[:, pl.ds(aligned(i * width, width), width)] = head_block(
                rows, feats[:, pl.ds(aligned(lo - width, width), 3 * width)], place[i],
                owns.at[i + 1], hid, out_t, feats[:, pl.ds(lo, width)], delta.at[i],
                own_table[SEAT_ROW : SEAT_ROW + 1, pl.ds(lo, width)],
            )

        by_depth(depth[i + 1], fan, run)
        return carry

    lax.fori_loop(0, place.shape[0], body, 0)
    hidden_edges(depth, spread, basis_edge, hid_edge, place.shape[0] + 2, fan)


def lane_sum(values):
    total = values[:, :LANES]
    for part in halves(values.shape[1])[1:]:
        total = total + values[:, part]
    return jnp.sum(total, axis=0, keepdims=True)


def head_outer(width, layer, core_ref, pk, own_table, received, relayed, owns, depth, outs_t, w_row, ref_row, feats, place, delta, mate, cross, hid_edge, inner, force_out, band_out, sums_out, table):
    core = core_ref[0]
    atoms = feats.shape[1]
    fan = place.shape[1]
    out_t = outs_t[layer]
    fill_table(table, feats, mate, cross, core, width)
    force_out[:, width : atoms - width] = inner[...]

    def body(i, carry):
        b, lo = edge_block(i, atoms // width, width)

        def run(rows):
            force_out[:, pl.ds(lo, width)] = head_block(
                rows, table[:, pl.ds(lo, 3 * width)], place[i], owns.at[b],
                hid_edge.at[i], out_t, feats[:, pl.ds(lo, width)], delta.at[i],
                own_table[SEAT_ROW : SEAT_ROW + 1, pl.ds(lo, width)],
            )

        by_depth(depth[b], fan, run)
        return carry

    lax.fori_loop(0, 2, body, 0)
    energy = dot(w_row[...], feats[...]) + ref_row[...]
    back = pk[0:4, :] - jnp.where(core == 0, relayed[0:4, :], received[4:8, :])
    fore = jnp.where(core == 0, received[4:8, :], relayed[0:4, :]) - pk[0:4, :]
    band_out[0:4, :] = back
    band_out[4:8, :] = fore
    back, fore, force = back[:3], fore[:3], force_out[0:3, :]
    rows = [energy, back * back, fore * fore, back * fore, force * back, force * fore]
    sums = [lane_sum(row) for row in rows]
    sums.append(jnp.zeros((SUM_ROWS - len(sums), LANES), F32))
    sums_out[...] = jnp.concatenate(sums, axis=0)


def add_sums(mine, other, out):
    out[...] = mine[...] + other[...]


def finish(count, flags, band, force, *rest):
    *parts, result, energy_out = rest
    total = parts[0][...]
    for part in parts[1:]:
        total = total + part[...]
    total = jnp.sum(total, axis=1, keepdims=True)
    energy, back_sq, fore_sq, cross, along_back, along_fore = (total[i : i + 1] for i in range(6))
    back_len = jnp.sqrt(back_sq + 1e-06)
    fore_len = jnp.sqrt(fore_sq + 1e-06)
    by_back, by_fore = 1.0 / back_len, 1.0 / fore_len
    tau_sq = (
        back_sq * by_back * by_back + fore_sq * by_fore * by_fore + 2.0 * cross * by_back * by_fore
    )
    proj = (along_back * by_back + along_fore * by_fore) / tau_sq
    spring = SPRING * (fore_len - back_len) / jnp.sqrt(tau_sq)
    climbing = flags[1] == 1
    is_end = flags[0] == 1
    factor = jnp.where(climbing, -2.0 * proj, spring - proj)
    tangent = band[0:3, :] * by_back + band[4:7, :] * by_fore
    moved = jnp.where(is_end, force[0:3, :], force[0:3, :] + factor * tangent)
    for c in range(3):
        result[c] = moved[c : c + 1]
    energy_out[...] = energy * (1.0 / count)


def swap_pairs(count, offset):
    pairs = []
    for low in range(offset, count, 2):
        high = (low + 1) % count
        pairs += [(low, high), (high, low)]
    return pairs


def image_pairs(images, tiles):
    pairs = []
    for low in range(images):
        high = (low + 1) % images
        for tile in range(0, tiles, 2):
            a, b = low * tiles + tile, high * tiles + tile + 1
            pairs += [(a, b), (b, a)]
    return pairs


def on_device(positions, species, counts, neighbours, send_list, climb, embed, ref_energy, rad_in, rad_out, mixing, w_energy):
    atoms = species.shape[0]
    width = send_list.shape[0] // 2
    fan = neighbours.shape[0]
    chans = embed.shape[1]
    layers = mixing.shape[0]
    basis_count, units = rad_in.shape[1:]
    blocks = atoms // width
    inner_atoms = (blocks - 2) * width
    tiles = lax.axis_size("atom")
    images = lax.axis_size("img")
    core = lax.rem(lax.axis_index("atom"), 2)
    image = lax.axis_index("img")
    core_arr = core.reshape(1).astype(I32)
    is_end = jnp.logical_or(image == 0, image == images - 1)
    flags = jnp.stack([is_end.astype(I32), climb[0]])

    def call(body, operands, outs, scratch=(), flops=0):
        scalars = {id(x) for x in (core_arr, flags, ref_energy)}
        return pl.pallas_call(
            body,
            out_shape=[jax.ShapeDtypeStruct(shape, dtype) for shape, dtype in outs],
            in_specs=[SMEM if id(x) in scalars else VMEM for x in operands],
            out_specs=[VMEM] * len(outs),
            scratch_shapes=[pltpu.VMEM(*x) for x in scratch],
            cost_estimate=pl.CostEstimate(flops=flops, bytes_accessed=2**20, transcendentals=0),
            compiler_params=pltpu.CompilerParams(vmem_limit_bytes=40 * 2**20),
        )(*operands)

    def swap(block, offset):
        return lax.ppermute(block, "atom", swap_pairs(tiles, offset))

    pack_type = ((PACK_ROWS, atoms), F32)
    feats_type = ((chans, atoms), BF16)
    halo_type = ((chans, width), BF16)
    hid_type = ((2, fan * units, width), BF16)
    hid_scratch = ((fan * units, width), BF16)
    table_scratch = [((chans, atoms + 2 * width), BF16)]

    def block_outs(count):
        return [
            ((count, 3 * fan, width), F32),
            ((count, fan * basis_count, width), BF16),
            ((count, fan, width), F32),
        ]

    row = lax.broadcasted_iota(I32, (PACK_ROWS, atoms), 0)
    sends = jnp.pad(send_list, (0, atoms - 2 * width))
    pk = jnp.zeros((PACK_ROWS, atoms), F32)
    lines = [positions[0, c] for c in range(3)] + [species, counts, sends]
    for place, line in enumerate(lines):
        pk = jnp.where(row == place, lax.broadcast_in_dim(line, pk.shape, (1,)).astype(F32), pk)
    mate = swap(pk, 0)
    cross = swap(pk, 1)
    kinds_type = ((blocks - 2, fan, width), F32)
    own_table, seated, edges, owns, depth, delta_in, basis_in, kinds_in, place_in = call(
        functools.partial(seat_tile, width),
        (pk, neighbours),
        [
            pack_type,
            pack_type,
            ((blocks, fan, width), F32),
            ((blocks, fan, LANES), F32),
            ((blocks, PACK_ROWS, LANES), F32),
        ]
        + block_outs(blocks - 2)[:2]
        + [kinds_type, kinds_type],
        [((fan, atoms), F32)],
        flops=2**32,
    )
    inner, embed_t, first, spread, out_t, mix_half, w_row, ref_row = call(
        functools.partial(first_inner, width),
        (ref_energy, pk, seated, owns, depth, basis_in, kinds_in, embed, rad_in, rad_out, mixing, w_energy[None]),
        [
            ((chans, inner_atoms), BF16),
            ((chans, -(-embed.shape[0] // 16) * 16), BF16),
            ((chans, embed.shape[0] * units), BF16),
            ((layers + 1, fan * units, fan * basis_count), BF16),
            ((layers + 1, chans, units), BF16),
            ((layers, chans, chans), BF16),
            ((1, chans), BF16),
            ((1, atoms), F32),
        ],
        [hid_scratch],
        flops=2**32,
    )
    delta_out, basis_out, place_out, feats, to_mate, to_cross, pair = call(
        functools.partial(first_outer, width),
        (core_arr, pk, own_table, seated, mate, cross, edges, owns, depth, embed_t, first, spread, mix_half, inner),
        block_outs(2) + [feats_type, halo_type, halo_type, pack_type],
        [((PACK_ROWS, atoms + 2 * width), F32), hid_scratch, ((2, fan, width), F32)],
    )
    for layer in range(1, layers):
        mate = swap(to_mate, 0)
        cross = swap(to_cross, 1)
        inner, hid_edge, pair = call(
            functools.partial(layer_inner, width, layer),
            (owns, depth, spread, out_t, mix_half, feats, basis_in, place_in, basis_out, pair),
            [((chans, inner_atoms), BF16), hid_type, pack_type],
            [hid_scratch],
        )
        feats, to_mate, to_cross = call(
            functools.partial(layer_outer, width, layer),
            (core_arr, own_table, owns, depth, out_t, mix_half, feats, place_out, mate, cross, hid_edge, inner),
            [feats_type, halo_type, halo_type],
            table_scratch,
        )
    received = lax.ppermute(pair, ("img", "atom"), image_pairs(images, tiles))
    relayed = swap(received, 0)
    mate = swap(to_mate, 0)
    cross = swap(to_cross, 1)
    inner, hid_edge = call(
        functools.partial(head_inner, width, layers),
        (own_table, owns, depth, spread, out_t, feats, basis_in, place_in, delta_in, basis_out),
        [((PACK_ROWS, inner_atoms), F32), hid_type],
        [hid_scratch],
    )
    force, band, sums = call(
        functools.partial(head_outer, width, layers),
        (core_arr, pk, own_table, received, relayed, owns, depth, out_t, w_row, ref_row, feats, place_out, delta_out, mate, cross, hid_edge, inner),
        [pack_type, pack_type, ((SUM_ROWS, LANES), F32)],
        table_scratch,
    )
    step = 2 * REDUCE_CHIPS
    while step < tiles:
        sums = sums + lax.ppermute(sums, "atom", [(i, i ^ step) for i in range(tiles)])
        step *= 2
    (both,) = call(add_sums, (sums, swap(sums, 0)), [((SUM_ROWS, LANES), F32)])
    near = lax.ppermute(both, "atom", [(i, i ^ 2 if i % 2 == 0 else i ^ 6) for i in range(tiles)])
    far = lax.ppermute(both, "atom", [(i, i ^ 4) for i in range(tiles)])
    other = swap(near, 0)
    result, energy = call(
        functools.partial(finish, atoms * tiles),
        (flags, band, force, both, near, far, other),
        [((3, 1, atoms), F32), ((1, 1), F32)],
    )
    return jnp.transpose(result, (1, 0, 2)), energy.reshape(1)


def solution(mesh):
    return jax.shard_map(
        on_device,
        mesh=mesh,
        in_specs=(
            P("img", None, "atom"),
            P("atom"),
            P("atom"),
            P(None, "atom"),
            P("atom"),
            P("img"),
            P(),
            P(),
            P(),
            P(),
            P(),
            P(),
        ),
        out_specs=(P("img", None, "atom"), P("img")),
        check_vma=False,
    )
```

```python
import functools
import math

import jax
import jax.numpy as jnp
from jax import lax
from jax.experimental import pallas as pl
from jax.experimental.pallas import tpu as pltpu
from jax.sharding import PartitionSpec as P

F32 = jnp.float32
BF16 = jnp.bfloat16
I32 = jnp.int32
LANES = 128
SPRING = 5.0
SPECIES_ROW = 3
COUNT_ROW = 4
SEND_ROW = 5
SEAT_ROW = 6
PACK_ROWS = 8
SUM_ROWS = 8
REDUCE_CHIPS = 4
VMEM = pl.BlockSpec(memory_space=pltpu.VMEM)
SMEM = pl.BlockSpec(memory_space=pltpu.SMEM)


def dot(a, b):
    return jnp.dot(a, b, preferred_element_type=F32)


def silu_of_half(half):
    return half + half * jnp.tanh(half)


def aligned(start, step):
    return pl.multiple_of(start, step)


def halves(width):
    return [slice(k * LANES, (k + 1) * LANES) for k in range(width // LANES)]


def short_rows(fan):
    return -(-5 * fan // 8)


def lane_fetch(windows, group, place):
    found = jnp.zeros(place.shape, F32)
    for k, window in enumerate(windows):
        rows = jnp.broadcast_to(window, place.shape)
        picked = jnp.take_along_axis(rows, place, axis=1, mode="promise_in_bounds")
        found = jnp.where(group == k, picked, found)
    return found


def lane_lookup(windows, index):
    return lane_fetch(windows, index // LANES, index & (LANES - 1))


def seat_atoms(pk, lo, width, most):
    counts = pk[COUNT_ROW : COUNT_ROW + 1, lo : lo + width]
    value = lax.broadcasted_iota(I32, (most, width), 0).astype(F32) + 1.0
    same = counts == value
    row = lax.broadcasted_iota(I32, (width, width), 0)
    lane = lax.broadcasted_iota(I32, (width, width), 1)
    earlier = dot(jnp.where(same, 1.0, 0.0).astype(BF16), jnp.where(row < lane, 1.0, 0.0).astype(BF16))
    larger = jnp.sum(jnp.where(counts > value, 1.0, 0.0), axis=1, keepdims=True)
    rank = jnp.sum(jnp.where(same, earlier + larger, 0.0), axis=0, keepdims=True)
    seat = jnp.where(rank < width // 2, rank, 1.5 * width - 1.0 - rank)
    taken = jnp.where(row.astype(F32) == seat, 1.0, 0.0).astype(BF16)
    atoms = lax.broadcasted_iota(I32, (PACK_ROWS, width), 1).astype(F32).astype(BF16)
    taker = lax.dot_general(
        atoms, taken, (((1,), (1,)), ((), ())), preferred_element_type=F32
    )
    return seat, taker[:1]


def seat_block(pk, nbr, lo, width, seated):
    fan = nbr.shape[0]
    seat, taker = seat_atoms(pk, lo, width, fan)
    pieces, tables = [], []
    for part in halves(width):
        who = taker[:, part].astype(I32)
        spans = [nbr[:, lo + p.start : lo + p.stop] for p in halves(width)]
        pieces.append(lane_lookup(spans, jnp.broadcast_to(who, (fan, LANES))) - float(lo))
        spans = [pk[:, lo + p.start : lo + p.stop] for p in halves(width)]
        tables.append(lane_lookup(spans, jnp.broadcast_to(who, (PACK_ROWS, LANES))))
    seated[:, lo : lo + width] = jnp.concatenate(tables, axis=1)
    return seat, pieces, [x[COUNT_ROW : COUNT_ROW + 1] for x in tables]


def fill_rows(pieces, counts, fits):
    first, second = pieces
    fan = first.shape[0]
    short = short_rows(fan)
    limit = jnp.where(fits, float(short), float(fan))
    row = lax.broadcasted_iota(I32, (fan, LANES), 0).astype(F32)
    mine = row < counts[1]
    over = [2 * short - 1 - r if 0 <= 2 * short - 1 - r < fan else 0 for r in range(fan)]
    over = jnp.concatenate([first[r : r + 1] for r in over], axis=0)
    spilled = jnp.logical_and(fits, 2.0 * short - 1.0 - row < counts[0])
    spilled = jnp.logical_and(spilled, row < float(short))
    spilled = jnp.logical_and(spilled, row >= float(2 * short - fan))
    spilled = jnp.logical_and(spilled, jnp.logical_not(mine))
    first = jnp.where(row < jnp.minimum(counts[0], limit), first, -1.0)
    second = jnp.where(mine, second, jnp.where(spilled, over, -1.0))
    return jnp.concatenate([first, second], axis=1), jnp.where(spilled, 0.0, 1.0)


def by_depth(depth, fan, run):
    shallow = jnp.max(depth[...]) < float(short_rows(fan)) + 0.5

    @pl.when(shallow)
    def _():
        run(short_rows(fan))

    @pl.when(jnp.logical_not(shallow))
    def _():
        run(fan)


def locate_block(i, table, table_lo, seated, edges, own, lo, width, delta_out, basis_out, kinds_out, place_out):
    fan = edges.shape[0]
    spans = [
        table[:, table_lo + p.start : table_lo + p.stop] for p in halves(3 * width)
    ]
    mine = own > 0.5
    home = seated[:, lo : lo + width]
    parts = []
    for part in halves(width):
        rel = edges[:, part].astype(I32)
        live = rel >= 0
        group, place = rel >> 7, rel & (LANES - 1)
        fetch = lambda r: lane_fetch([span[r : r + 1] for span in spans], group, place)
        values = []
        for c in range(3):
            here = home[c : c + 1, part]
            if part.start > 0:
                here = jnp.where(mine, here, home[c : c + 1, :LANES])
            values.append(fetch(c) - here)
        values.append(jnp.where(live, fetch(SPECIES_ROW), -1.0))
        tile = (rel // width).astype(F32) * float(width)
        values.append(jnp.where(live, fetch(SEAT_ROW) + tile, -1.0))
        parts.append(values)
    joined = [jnp.concatenate(list(piece), axis=1) for piece in zip(*parts)]
    for c in range(3):
        delta_out[i, c * fan : (c + 1) * fan, :] = joined[c]
    kinds_out[i] = joined[3]
    place_out[i] = joined[4]
    dist_sq = joined[0] * joined[0] + joined[1] * joined[1] + joined[2] * joined[2]
    count = basis_out.shape[1] // fan
    centres = 2.0 * lax.broadcasted_iota(I32, (count, width), 0).astype(F32)
    rows = []
    for s in range(fan):
        away = jnp.broadcast_to(dist_sq[s : s + 1], (count, width)) - centres
        rows.append(jnp.exp(away * away * -0.125))
    basis_out[i] = jnp.concatenate(rows, axis=0).astype(BF16)


def fill_hidden(target, spread, basis, rows, fan):
    used = rows * (spread.shape[0] // fan)
    target[:used, :] = silu_of_half(dot(spread[:used, :], basis)).astype(BF16)


class Sums:
    def __init__(self, shape, own, rows, fan):
        self.total = jnp.zeros(shape, F32)
        self.lent = jnp.zeros((shape[0], LANES), F32)
        self.own, self.alone = own, 2 * rows - fan

    def add(self, s, terms):
        self.total = self.total + terms
        if s >= self.alone:
            self.lent = self.lent + jnp.where(self.own[s : s + 1] > 0.5, 0.0, terms[:, LANES:])

    def done(self):
        first, second = self.total[:, :LANES], self.total[:, LANES:]
        return jnp.concatenate([first + self.lent, second - self.lent], axis=1)


def update_of(feats, summed, mix_half, fan):
    scaled = (summed * (1.0 / math.sqrt(fan))).astype(BF16)
    return (feats.astype(F32) + silu_of_half(dot(mix_half, scaled))).astype(BF16)


def first_block(rows, kinds, hid, own, seated, lo, width, weights):
    embed_t, first, mix_half, spread = weights
    fan = kinds.shape[0]
    kinds_count = embed_t.shape[1]
    units = spread.shape[0] // fan
    species = first.shape[1] // units
    kinds = kinds.astype(BF16)
    zero = jnp.zeros((), BF16)
    sums = Sums((mix_half.shape[0], width), own, rows, fan)
    for s in range(rows):
        mine = hid[s * units : (s + 1) * units, :]
        kind = jnp.broadcast_to(kinds[s : s + 1], (units, width))
        sorted_out = [
            jnp.where(kind == jnp.full((), k, BF16), mine, zero) for k in range(species)
        ]
        sums.add(s, dot(first[...], jnp.concatenate(sorted_out, axis=0)))
    rows_of = lax.broadcasted_iota(I32, (kinds_count, width), 0).astype(F32)
    same = rows_of == seated[SPECIES_ROW : SPECIES_ROW + 1, lo : lo + width]
    feats = dot(embed_t[...], jnp.where(same, 1.0, 0.0).astype(BF16))
    return update_of(feats, sums.done(), mix_half[...], fan)


def turned(matrix):
    size = matrix.shape[1]
    row = lax.broadcasted_iota(I32, (size, size), 0)
    column = lax.broadcasted_iota(I32, (size, size), 1)
    identity = jnp.where(row == column, 1.0, 0.0).astype(BF16)
    return lax.dot_general(
        identity, matrix, (((1,), (1,)), ((), ())), preferred_element_type=F32
    )


def prepare(embed, rad_in, rad_out, mixing, embed_t, first, spread, out_t, mix_half):
    layers, count, units = rad_in.shape
    fan = spread.shape[1] // units
    for layer in range(layers):
        half = rad_in[layer].astype(F32) * 0.5
        weight = turned(jnp.concatenate([half] * fan, axis=0).astype(BF16))
        owner = lax.broadcasted_iota(I32, weight.shape, 1) // count
        for s in range(fan):
            only = jnp.where(owner == s, weight, 0.0).astype(BF16)
            spread[layer, s * units : (s + 1) * units, :] = only
        out_t[layer] = turned(rad_out[layer]).astype(BF16)
    for layer in range(mixing.shape[0]):
        mix_half[layer] = (turned(mixing[layer]) * 0.5).astype(BF16)
    out = rad_out[0].astype(F32)
    table = embed[...].astype(F32)
    species = table.shape[0]
    padded = jnp.concatenate(
        [table, jnp.zeros((embed_t.shape[1] - species, table.shape[1]), F32)], axis=0
    )
    embed_t[...] = turned(padded.astype(BF16)).astype(BF16)
    scaled = jnp.concatenate([out * table[k : k + 1] for k in range(species)], axis=0)
    first[...] = turned(scaled.astype(BF16)).astype(BF16)


def seat_tile(width, pk, nbr, table, seated, edges, owns, depth, delta_out, basis_out, kinds_out, place_out, index):
    atoms = pk.shape[1]
    blocks = atoms // width
    index[...] = nbr[...].astype(F32)
    table[...] = pk[...]
    found = [seat_block(pk, index, b * width, width, seated) for b in range(blocks)]
    both = [counts[0] + counts[1] for _, _, counts in found]
    most = functools.reduce(jnp.maximum, both)
    fits = jnp.max(most, axis=1, keepdims=True) <= float(2 * short_rows(nbr.shape[0]))
    depth[...] = jnp.where(
        jnp.broadcast_to(fits, depth.shape), float(short_rows(nbr.shape[0])), float(nbr.shape[0])
    )
    for b, (seat, pieces, counts) in enumerate(found):
        table[SEAT_ROW : SEAT_ROW + 1, b * width : (b + 1) * width] = seat
        edges[b], owns[b] = fill_rows(pieces, counts, fits)
    for part in halves(2 * width):
        wanted = jnp.broadcast_to(pk[SEND_ROW : SEND_ROW + 1, part].astype(I32), (PACK_ROWS, LANES))
        seats = lane_lookup([table[SEAT_ROW : SEAT_ROW + 1, p] for p in halves(atoms)], wanted)
        seats = seats + (wanted // width).astype(F32) * float(width)
        table[SEND_ROW : SEND_ROW + 1, part] = seats[:1]

    for i in range(blocks - 2):
        lo = (i + 1) * width
        locate_block(
            i, table, lo - width, seated, edges[i + 1], owns[i + 1], lo, width,
            delta_out, basis_out, kinds_out, place_out,
        )


def first_inner(width, ref_energy, pk, seated, owns, depth, basis, kinds, embed, rad_in, rad_out, mixing, w_in, feats_out, embed_t, first, spread, out_t, mix_half, w_row, ref_row, hid):
    prepare(embed, rad_in, rad_out, mixing, embed_t, first, spread, out_t, mix_half)
    weights = (embed_t, first, mix_half.at[0], spread.at[0])
    w_row[...] = w_in[...]
    kinds_row = pk[SPECIES_ROW : SPECIES_ROW + 1, :]
    energy = jnp.zeros(kinds_row.shape, F32)
    for k in range(ref_energy.shape[0]):
        energy = jnp.where(kinds_row == float(k), ref_energy[k], energy)
    ref_row[...] = energy

    def run(rows):
        for i in range(kinds.shape[0]):
            fill_hidden(hid.at[i], spread.at[0], basis[i], rows, kinds.shape[1])
        for i in range(kinds.shape[0]):
            feats_out[:, i * width : (i + 1) * width] = first_block(
                rows, kinds[i], hid.at[i], owns.at[i + 1], seated, (i + 1) * width, width, weights
            )

    by_depth(depth, kinds.shape[1], run)


def pack_halo(feats, table, core, width, to_mate, to_cross):
    atoms = feats.shape[1]
    rows = lax.broadcasted_iota(I32, (width, width), 0).astype(F32).astype(BF16)
    one, zero = jnp.ones((), BF16), jnp.zeros((), BF16)
    for ref, start in ((to_mate, (1 - core) * width), (to_cross, core * width)):
        wanted = table[SEND_ROW : SEND_ROW + 1, pl.ds(aligned(start, width), width)]
        picks = []
        for k in range(atoms // width):
            place = jnp.clip(wanted - float(k * width), -1.0, float(width)).astype(BF16)
            picks.append(jnp.where(rows == place, one, zero))
        ref[...] = dot(feats[...], jnp.concatenate(picks, axis=0)).astype(BF16)


def halo_places(core, atoms, width):
    top = atoms + width
    return aligned((1 - core) * top, width), aligned(core * top, width)


def edge_blocks(blocks, width):
    return [(0, 0, 0), (1, blocks - 1, (blocks - 1) * width)]


def first_outer(width, core_ref, pk, own_table, seated, mate, cross, edges, owns, depth, embed_t, first, spread, mix_half, inner, delta_out, basis_out, place_out, feats_out, to_mate, to_cross, pair_out, table, kinds, hid):
    core = core_ref[0]
    atoms = pk.shape[1]
    blocks = atoms // width
    fan = edges.shape[1]
    weights = (embed_t, first, mix_half.at[0], spread.at[0])
    table[:, width : width + atoms] = own_table[...]
    at_mate, at_cross = halo_places(core, atoms, width)
    for ref, start, at in ((mate, core * width, at_mate), (cross, (1 - core) * width, at_cross)):
        spans = [ref[:, part] for part in halves(atoms)]
        for k in range(width // LANES):
            wanted = ref[SEND_ROW : SEND_ROW + 1, pl.ds(aligned(start + k * LANES, LANES), LANES)]
            wanted = jnp.broadcast_to(wanted.astype(I32), (PACK_ROWS, LANES))
            place = pl.ds(aligned(at + k * LANES, LANES), LANES)
            table[:, place] = lane_lookup(spans, wanted)
            lane = lax.broadcasted_iota(I32, (1, LANES), 1) + k * LANES
            table[SEAT_ROW : SEAT_ROW + 1, place] = lane.astype(F32)
    feats_out[:, width : atoms - width] = inner[...]
    pair_out[0:4, :] = pk[0:4, :]
    pair_out[4:8, :] = mate[0:4, :]

    for i, b, lo in edge_blocks(blocks, width):
        locate_block(
            i, table, lo, seated, edges[b], owns[b], lo, width,
            delta_out, basis_out, kinds, place_out,
        )

    def run(rows):
        for i in range(2):
            fill_hidden(hid.at[i], spread.at[0], basis_out[i], rows, fan)
        for i, b, lo in edge_blocks(blocks, width):
            feats_out[:, lo : lo + width] = first_block(
                rows, kinds[i], hid.at[i], owns.at[b], seated, lo, width, weights
            )

    by_depth(depth, fan, run)
    pack_halo(feats_out, own_table, core, width, to_mate, to_cross)


def places_of(place, width):
    return [jnp.clip(place - float(k * width), -1.0, float(width)).astype(BF16) for k in range(3)]


def fetch_rows(window, places, s, width):
    rows = lax.broadcasted_iota(I32, (width, width), 0).astype(F32).astype(BF16)
    one, zero = jnp.ones((), BF16), jnp.zeros((), BF16)
    picks = [jnp.where(rows == place[s : s + 1], one, zero) for place in places]
    return dot(window, jnp.concatenate(picks, axis=0))


def layer_block(rows, window, place, own, hid, out_t, mix_half, feats):
    fan, width = place.shape
    places = places_of(place, width)
    sums = Sums(feats.shape, own, rows, fan)
    for s in range(rows):
        far = fetch_rows(window, places, s, width)
        sums.add(s, far * dot(out_t, hid(s)))
    return update_of(feats, sums.done(), mix_half, fan)


def stored(hid_edge, i, units):
    return lambda s: hid_edge[i, s * units : (s + 1) * units, :]


def hidden_edges(rows, spread, basis, hid_edge, fan):
    for i in range(2):
        fill_hidden(hid_edge.at[i], spread, basis[i], rows, fan)


def layer_inner(width, layer, owns, depth, spreads, outs_t, mixes, feats, basis, place, basis_edge, pair, feats_out, hid_edge, pair_out, hid):
    spread, out_t, mix_half = spreads.at[layer], outs_t[layer], mixes[layer]
    units = out_t.shape[1]
    pair_out[...] = pair[...]

    def run(rows):
        for i in range(place.shape[0]):
            fill_hidden(hid.at[i], spread, basis[i], rows, place.shape[1])
        for i in range(place.shape[0]):
            lo = (i + 1) * width
            feats_out[:, lo - width : lo] = layer_block(
                rows, feats[:, lo - width : lo + 2 * width], place[i], owns.at[i + 1],
                stored(hid, i, units), out_t, mix_half,
                feats[:, lo : lo + width],
            )
        hidden_edges(rows, spread, basis_edge, hid_edge, place.shape[1])

    by_depth(depth, place.shape[1], run)


def fill_table(table, feats, mate, cross, core, width):
    atoms = feats.shape[1]
    at_mate, at_cross = halo_places(core, atoms, width)
    table[:, width : width + atoms] = feats[...]
    table[:, pl.ds(at_mate, width)] = mate[...]
    table[:, pl.ds(at_cross, width)] = cross[...]


def layer_outer(width, layer, core_ref, own_table, owns, depth, outs_t, mixes, feats, place, mate, cross, hid_edge, inner, feats_out, to_mate, to_cross, table):
    core = core_ref[0]
    atoms = feats.shape[1]
    fan = place.shape[1]
    out_t, mix_half = outs_t[layer], mixes[layer]
    fill_table(table, feats, mate, cross, core, width)
    feats_out[:, width : atoms - width] = inner[...]

    def run(rows):
        for i, b, lo in edge_blocks(atoms // width, width):
            feats_out[:, lo : lo + width] = layer_block(
                rows, table[:, lo : lo + 3 * width], place[i], owns.at[b],
                stored(hid_edge, i, out_t.shape[1]), out_t, mix_half, feats[:, lo : lo + width],
            )

    by_depth(depth, fan, run)
    pack_halo(feats_out, own_table, core, width, to_mate, to_cross)


def head_block(rows, window, place, own, hid, out_t, feats, delta, seat):
    fan, width = place.shape
    chans = out_t.shape[0]
    places = places_of(place, width)
    near = feats.astype(F32)
    pairs = []
    for s in range(rows):
        far = fetch_rows(window, places, s, width)
        here = near
        if s >= 2 * rows - fan:
            lower = jnp.where(own[s : s + 1] > 0.5, near[:, LANES:], near[:, :LANES])
            here = jnp.concatenate([near[:, :LANES], lower], axis=1)
        terms = far * (dot(out_t, hid(s)) * here)
        pairs.append(jnp.sum(terms, axis=0, keepdims=True))
    if rows < fan:
        pairs.append(jnp.zeros((fan - rows, width), F32))
    pair = jnp.concatenate(pairs, axis=0) * (1.0 / math.sqrt(chans))
    mine = own[...] > 0.5
    out = []
    for c in range(3):
        terms = pair * delta[c * fan : (c + 1) * fan, :]
        second = terms[:, LANES:]
        lent = jnp.where(mine, 0.0, second)
        out.append(
            jnp.concatenate(
                [
                    jnp.sum(terms[:, :LANES] + lent, axis=0, keepdims=True),
                    jnp.sum(jnp.where(mine, second, 0.0), axis=0, keepdims=True),
                ],
                axis=1,
            )
        )
    seated = jnp.concatenate(out + [jnp.zeros((PACK_ROWS - 3, width), F32)], axis=0)
    spans = [seated[:, part] for part in halves(width)]
    seat = seat.astype(I32)
    return jnp.concatenate(
        [
            lane_lookup(spans, jnp.broadcast_to(seat[:, part], (PACK_ROWS, LANES)))
            for part in halves(width)
        ],
        axis=1,
    )


def head_inner(width, layer, own_table, owns, depth, spreads, outs_t, feats, basis, place, delta, basis_edge, force_out, hid_edge, hid):
    spread, out_t = spreads.at[layer], outs_t[layer]
    units = out_t.shape[1]

    def run(rows):
        for i in range(place.shape[0]):
            fill_hidden(hid.at[i], spread, basis[i], rows, place.shape[1])
        for i in range(place.shape[0]):
            lo = (i + 1) * width
            force_out[:, lo - width : lo] = head_block(
                rows, feats[:, lo - width : lo + 2 * width], place[i], owns.at[i + 1],
                stored(hid, i, units), out_t, feats[:, lo : lo + width],
                delta.at[i], own_table[SEAT_ROW : SEAT_ROW + 1, lo : lo + width],
            )
        hidden_edges(rows, spread, basis_edge, hid_edge, place.shape[1])

    by_depth(depth, place.shape[1], run)


def lane_sum(values):
    total = values[:, :LANES]
    for part in halves(values.shape[1])[1:]:
        total = total + values[:, part]
    return jnp.sum(total, axis=0, keepdims=True)


def head_outer(width, layer, core_ref, pk, own_table, received, relayed, owns, depth, outs_t, w_row, ref_row, feats, place, delta, mate, cross, hid_edge, inner, force_out, band_out, sums_out, table):
    core = core_ref[0]
    atoms = feats.shape[1]
    fan = place.shape[1]
    out_t = outs_t[layer]
    fill_table(table, feats, mate, cross, core, width)
    force_out[:, width : atoms - width] = inner[...]

    def run(rows):
        for i, b, lo in edge_blocks(atoms // width, width):
            force_out[:, lo : lo + width] = head_block(
                rows, table[:, lo : lo + 3 * width], place[i], owns.at[b],
                stored(hid_edge, i, out_t.shape[1]), out_t, feats[:, lo : lo + width],
                delta.at[i], own_table[SEAT_ROW : SEAT_ROW + 1, lo : lo + width],
            )

    by_depth(depth, fan, run)
    energy = dot(w_row[...], feats[...]) + ref_row[...]
    back = pk[0:4, :] - jnp.where(core == 0, relayed[0:4, :], received[4:8, :])
    fore = jnp.where(core == 0, received[4:8, :], relayed[0:4, :]) - pk[0:4, :]
    band_out[0:4, :] = back
    band_out[4:8, :] = fore
    back, fore, force = back[:3], fore[:3], force_out[0:3, :]
    rows = [energy, back * back, fore * fore, back * fore, force * back, force * fore]
    sums = [lane_sum(row) for row in rows]
    sums.append(jnp.zeros((SUM_ROWS - len(sums), LANES), F32))
    sums_out[...] = jnp.concatenate(sums, axis=0)


def add_sums(mine, other, out):
    out[...] = mine[...] + other[...]


def finish(count, flags, band, force, *rest):
    *parts, result, energy_out = rest
    total = parts[0][...]
    for part in parts[1:]:
        total = total + part[...]
    total = jnp.sum(total, axis=1, keepdims=True)
    energy, back_sq, fore_sq, cross, along_back, along_fore = (total[i : i + 1] for i in range(6))
    back_len = jnp.sqrt(back_sq + 1e-06)
    fore_len = jnp.sqrt(fore_sq + 1e-06)
    by_back, by_fore = 1.0 / back_len, 1.0 / fore_len
    tau_sq = (
        back_sq * by_back * by_back + fore_sq * by_fore * by_fore + 2.0 * cross * by_back * by_fore
    )
    proj = (along_back * by_back + along_fore * by_fore) / tau_sq
    spring = SPRING * (fore_len - back_len) / jnp.sqrt(tau_sq)
    climbing = flags[1] == 1
    is_end = flags[0] == 1
    factor = jnp.where(climbing, -2.0 * proj, spring - proj)
    tangent = band[0:3, :] * by_back + band[4:7, :] * by_fore
    moved = jnp.where(is_end, force[0:3, :], force[0:3, :] + factor * tangent)
    for c in range(3):
        result[c] = moved[c : c + 1]
    energy_out[...] = energy * (1.0 / count)


def swap_pairs(count, offset):
    pairs = []
    for low in range(offset, count, 2):
        high = (low + 1) % count
        pairs += [(low, high), (high, low)]
    return pairs


def image_pairs(images, tiles):
    pairs = []
    for low in range(images):
        high = (low + 1) % images
        for tile in range(0, tiles, 2):
            a, b = low * tiles + tile, high * tiles + tile + 1
            pairs += [(a, b), (b, a)]
    return pairs


def on_device(positions, species, counts, neighbours, send_list, climb, embed, ref_energy, rad_in, rad_out, mixing, w_energy):
    atoms = species.shape[0]
    width = send_list.shape[0] // 2
    fan = neighbours.shape[0]
    chans = embed.shape[1]
    layers = mixing.shape[0]
    basis_count, units = rad_in.shape[1:]
    blocks = atoms // width
    inner_atoms = (blocks - 2) * width
    tiles = lax.axis_size("atom")
    images = lax.axis_size("img")
    core = lax.rem(lax.axis_index("atom"), 2)
    image = lax.axis_index("img")
    core_arr = core.reshape(1).astype(I32)
    is_end = jnp.logical_or(image == 0, image == images - 1)
    flags = jnp.stack([is_end.astype(I32), climb[0]])

    def call(body, operands, outs, scratch=(), flops=0):
        scalars = {id(x) for x in (core_arr, flags, ref_energy)}
        return pl.pallas_call(
            body,
            out_shape=[jax.ShapeDtypeStruct(shape, dtype) for shape, dtype in outs],
            in_specs=[SMEM if id(x) in scalars else VMEM for x in operands],
            out_specs=[VMEM] * len(outs),
            scratch_shapes=[pltpu.VMEM(*x) for x in scratch],
            cost_estimate=pl.CostEstimate(flops=flops, bytes_accessed=2**20, transcendentals=0),
            compiler_params=pltpu.CompilerParams(vmem_limit_bytes=40 * 2**20),
        )(*operands)

    def swap(block, offset):
        return lax.ppermute(block, "atom", swap_pairs(tiles, offset))

    pack_type = ((PACK_ROWS, atoms), F32)
    feats_type = ((chans, atoms), BF16)
    halo_type = ((chans, width), BF16)
    hid_type = ((2, fan * units, width), BF16)
    hid_scratch = ((blocks - 2, fan * units, width), BF16)
    table_scratch = [((chans, atoms + 2 * width), BF16)]

    def block_outs(count):
        return [
            ((count, 3 * fan, width), F32),
            ((count, fan * basis_count, width), BF16),
            ((count, fan, width), F32),
        ]

    row = lax.broadcasted_iota(I32, (PACK_ROWS, atoms), 0)
    sends = jnp.pad(send_list, (0, atoms - 2 * width))
    pk = jnp.zeros((PACK_ROWS, atoms), F32)
    lines = [positions[0, c] for c in range(3)] + [species, counts, sends]
    for place, line in enumerate(lines):
        pk = jnp.where(row == place, lax.broadcast_in_dim(line, pk.shape, (1,)).astype(F32), pk)
    mate = swap(pk, 0)
    cross = swap(pk, 1)
    kinds_type = ((blocks - 2, fan, width), F32)
    own_table, seated, edges, owns, depth, delta_in, basis_in, kinds_in, place_in = call(
        functools.partial(seat_tile, width),
        (pk, neighbours),
        [
            pack_type,
            pack_type,
            ((blocks, fan, width), F32),
            ((blocks, fan, LANES), F32),
            ((PACK_ROWS, LANES), F32),
        ]
        + block_outs(blocks - 2)[:2]
        + [kinds_type, kinds_type],
        [((fan, atoms), F32)],
        flops=2**32,
    )
    inner, embed_t, first, spread, out_t, mix_half, w_row, ref_row = call(
        functools.partial(first_inner, width),
        (ref_energy, pk, seated, owns, depth, basis_in, kinds_in, embed, rad_in, rad_out, mixing, w_energy[None]),
        [
            ((chans, inner_atoms), BF16),
            ((chans, -(-embed.shape[0] // 16) * 16), BF16),
            ((chans, embed.shape[0] * units), BF16),
            ((layers + 1, fan * units, fan * basis_count), BF16),
            ((layers + 1, chans, units), BF16),
            ((layers, chans, chans), BF16),
            ((1, chans), BF16),
            ((1, atoms), F32),
        ],
        [hid_scratch],
        flops=2**32,
    )
    delta_out, basis_out, place_out, feats, to_mate, to_cross, pair = call(
        functools.partial(first_outer, width),
        (core_arr, pk, own_table, seated, mate, cross, edges, owns, depth, embed_t, first, spread, mix_half, inner),
        block_outs(2) + [feats_type, halo_type, halo_type, pack_type],
        [((PACK_ROWS, atoms + 2 * width), F32), ((2, fan, width), F32), hid_type],
    )
    for layer in range(1, layers):
        mate = swap(to_mate, 0)
        cross = swap(to_cross, 1)
        inner, hid_edge, pair = call(
            functools.partial(layer_inner, width, layer),
            (owns, depth, spread, out_t, mix_half, feats, basis_in, place_in, basis_out, pair),
            [((chans, inner_atoms), BF16), hid_type, pack_type],
            [hid_scratch],
        )
        feats, to_mate, to_cross = call(
            functools.partial(layer_outer, width, layer),
            (core_arr, own_table, owns, depth, out_t, mix_half, feats, place_out, mate, cross, hid_edge, inner),
            [feats_type, halo_type, halo_type],
            table_scratch,
        )
    received = lax.ppermute(pair, ("img", "atom"), image_pairs(images, tiles))
    relayed = swap(received, 0)
    mate = swap(to_mate, 0)
    cross = swap(to_cross, 1)
    inner, hid_edge = call(
        functools.partial(head_inner, width, layers),
        (own_table, owns, depth, spread, out_t, feats, basis_in, place_in, delta_in, basis_out),
        [((PACK_ROWS, inner_atoms), F32), hid_type],
        [hid_scratch],
    )
    force, band, sums = call(
        functools.partial(head_outer, width, layers),
        (core_arr, pk, own_table, received, relayed, owns, depth, out_t, w_row, ref_row, feats, place_out, delta_out, mate, cross, hid_edge, inner),
        [pack_type, pack_type, ((SUM_ROWS, LANES), F32)],
        table_scratch,
    )
    step = 2 * REDUCE_CHIPS
    while step < tiles:
        sums = sums + lax.ppermute(sums, "atom", [(i, i ^ step) for i in range(tiles)])
        step *= 2
    (both,) = call(add_sums, (sums, swap(sums, 0)), [((SUM_ROWS, LANES), F32)])
    near = lax.ppermute(both, "atom", [(i, i ^ 2 if i % 2 == 0 else i ^ 6) for i in range(tiles)])
    far = lax.ppermute(both, "atom", [(i, i ^ 4) for i in range(tiles)])
    other = swap(near, 0)
    result, energy = call(
        functools.partial(finish, atoms * tiles),
        (flags, band, force, both, near, far, other),
        [((3, 1, atoms), F32), ((1, 1), F32)],
    )
    return jnp.transpose(result, (1, 0, 2)), energy.reshape(1)


def solution(mesh):
    return jax.shard_map(
        on_device,
        mesh=mesh,
        in_specs=(
            P("img", None, "atom"),
            P("atom"),
            P("atom"),
            P(None, "atom"),
            P("atom"),
            P("img"),
            P(),
            P(),
            P(),
            P(),
            P(),
            P(),
        ),
        out_specs=(P("img", None, "atom"), P("img")),
        check_vma=False,
    )
```

```python
import functools
import math

import jax
import jax.numpy as jnp
from jax import lax
from jax.experimental import pallas as pl
from jax.experimental.pallas import tpu as pltpu
from jax.sharding import PartitionSpec as P

F32 = jnp.float32
BF16 = jnp.bfloat16
I32 = jnp.int32
LANES = 128
SPRING = 5.0
SPECIES_ROW = 3
COUNT_ROW = 4
SEND_ROW = 5
SEAT_ROW = 6
PACK_ROWS = 8
SUM_ROWS = 8
REDUCE_CHIPS = 4
VMEM = pl.BlockSpec(memory_space=pltpu.VMEM)
SMEM = pl.BlockSpec(memory_space=pltpu.SMEM)


def dot(a, b):
    return jnp.dot(a, b, preferred_element_type=F32)


def silu_of_half(half):
    return half + half * jnp.tanh(half)


def aligned(start, step):
    return pl.multiple_of(start, step)


def halves(width):
    return [slice(k * LANES, (k + 1) * LANES) for k in range(width // LANES)]


def short_rows(fan):
    return -(-5 * fan // 8)


def lane_fetch(windows, group, place):
    found = jnp.zeros(place.shape, F32)
    for k, window in enumerate(windows):
        rows = jnp.broadcast_to(window, place.shape)
        picked = jnp.take_along_axis(rows, place, axis=1, mode="promise_in_bounds")
        found = jnp.where(group == k, picked, found)
    return found


def lane_lookup(windows, index):
    return lane_fetch(windows, index // LANES, index & (LANES - 1))


def blank(out):
    out[...] = jnp.zeros(out.shape, F32)


def seat_atoms(pk, lo, width, most):
    counts = pk[COUNT_ROW : COUNT_ROW + 1, lo : lo + width]
    value = lax.broadcasted_iota(I32, (most, width), 0).astype(F32) + 1.0
    same = counts == value
    row = lax.broadcasted_iota(I32, (width, width), 0)
    lane = lax.broadcasted_iota(I32, (width, width), 1)
    earlier = dot(jnp.where(same, 1.0, 0.0).astype(BF16), jnp.where(row < lane, 1.0, 0.0).astype(BF16))
    larger = jnp.sum(jnp.where(counts > value, 1.0, 0.0), axis=1, keepdims=True)
    rank = jnp.sum(jnp.where(same, earlier + larger, 0.0), axis=0, keepdims=True)
    seat = jnp.where(rank < width // 2, rank, 1.5 * width - 1.0 - rank)
    taken = jnp.where(row.astype(F32) == seat, 1.0, 0.0).astype(BF16)
    atoms = lax.broadcasted_iota(I32, (PACK_ROWS, width), 1).astype(F32).astype(BF16)
    taker = lax.dot_general(
        atoms, taken, (((1,), (1,)), ((), ())), preferred_element_type=F32
    )
    return seat, taker[:1]


def seat_block(pk, nbr, lo, width, seated):
    fan = nbr.shape[0]
    seat, taker = seat_atoms(pk, lo, width, fan)
    pieces, tables = [], []
    for part in halves(width):
        who = taker[:, part].astype(I32)
        spans = [nbr[:, lo + p.start : lo + p.stop] for p in halves(width)]
        pieces.append(lane_lookup(spans, jnp.broadcast_to(who, (fan, LANES))) - float(lo))
        spans = [pk[:, lo + p.start : lo + p.stop] for p in halves(width)]
        tables.append(lane_lookup(spans, jnp.broadcast_to(who, (PACK_ROWS, LANES))))
    seated[:, lo : lo + width] = jnp.concatenate(tables, axis=1)
    return seat, pieces, [x[COUNT_ROW : COUNT_ROW + 1] for x in tables]


def fill_rows(pieces, counts, fits):
    first, second = pieces
    fan = first.shape[0]
    short = short_rows(fan)
    limit = jnp.where(fits, float(short), float(fan))
    row = lax.broadcasted_iota(I32, (fan, LANES), 0).astype(F32)
    mine = row < counts[1]
    over = [2 * short - 1 - r if 0 <= 2 * short - 1 - r < fan else 0 for r in range(fan)]
    over = jnp.concatenate([first[r : r + 1] for r in over], axis=0)
    spilled = jnp.logical_and(fits, 2.0 * short - 1.0 - row < counts[0])
    spilled = jnp.logical_and(spilled, row < float(short))
    spilled = jnp.logical_and(spilled, row >= float(2 * short - fan))
    spilled = jnp.logical_and(spilled, jnp.logical_not(mine))
    first = jnp.where(row < jnp.minimum(counts[0], limit), first, -1.0)
    second = jnp.where(mine, second, jnp.where(spilled, over, -1.0))
    return jnp.concatenate([first, second], axis=1), jnp.where(spilled, 0.0, 1.0)


def by_depth(depth, fan, run):
    shallow = jnp.max(depth[...]) < float(short_rows(fan)) + 0.5

    @pl.when(shallow)
    def _():
        run(short_rows(fan))

    @pl.when(jnp.logical_not(shallow))
    def _():
        run(fan)


def locate_block(i, table, table_lo, seated, edges, own, lo, width, delta_out, basis_out, kinds_out, place_out):
    fan = edges.shape[0]
    spans = [
        table[:, table_lo + p.start : table_lo + p.stop] for p in halves(3 * width)
    ]
    mine = own > 0.5
    home = seated[:, lo : lo + width]
    parts = []
    for part in halves(width):
        rel = edges[:, part].astype(I32)
        live = rel >= 0
        group, place = rel >> 7, rel & (LANES - 1)
        fetch = lambda r: lane_fetch([span[r : r + 1] for span in spans], group, place)
        values = []
        for c in range(3):
            here = home[c : c + 1, part]
            if part.start > 0:
                here = jnp.where(mine, here, home[c : c + 1, :LANES])
            values.append(fetch(c) - here)
        values.append(jnp.where(live, fetch(SPECIES_ROW), -1.0))
        tile = (rel // width).astype(F32) * float(width)
        values.append(jnp.where(live, fetch(SEAT_ROW) + tile, -1.0))
        parts.append(values)
    joined = [jnp.concatenate(list(piece), axis=1) for piece in zip(*parts)]
    for c in range(3):
        delta_out[i, c * fan : (c + 1) * fan, :] = joined[c]
    kinds_out[i] = joined[3]
    place_out[i] = joined[4]
    dist_sq = joined[0] * joined[0] + joined[1] * joined[1] + joined[2] * joined[2]
    count = basis_out.shape[1] // fan
    centres = 2.0 * lax.broadcasted_iota(I32, (count, width), 0).astype(F32)
    rows = []
    for s in range(fan):
        away = jnp.broadcast_to(dist_sq[s : s + 1], (count, width)) - centres
        rows.append(jnp.exp(away * away * -0.125))
    basis_out[i] = jnp.concatenate(rows, axis=0).astype(BF16)


def fill_hidden(target, spread, basis, rows, fan):
    used = rows * (spread.shape[0] // fan)
    target[:used, :] = silu_of_half(dot(spread[:used, :], basis)).astype(BF16)


class Sums:
    def __init__(self, shape, own, rows, fan, total=None, lent=None):
        self.total = jnp.zeros(shape, F32) if total is None else total
        self.lent = jnp.zeros((shape[0], LANES), F32) if lent is None else lent
        self.own, self.alone = own, 2 * rows - fan

    def add(self, s, terms):
        self.total = self.total + terms
        if s >= self.alone:
            self.lent = self.lent + jnp.where(self.own[s : s + 1] > 0.5, 0.0, terms[:, LANES:])

    def done(self):
        first, second = self.total[:, :LANES], self.total[:, LANES:]
        return jnp.concatenate([first + self.lent, second - self.lent], axis=1)


def update_of(feats, summed, mix_half, fan):
    scaled = (summed * (1.0 / math.sqrt(fan))).astype(BF16)
    return (feats.astype(F32) + silu_of_half(dot(mix_half, scaled))).astype(BF16)


def first_block(rows, kinds, hid, own, seated, lo, width, weights):
    embed_t, first, mix_half, spread = weights
    fan = kinds.shape[0]
    kinds_count = embed_t.shape[1]
    units = spread.shape[0] // fan
    species = first.shape[1] // units
    kinds = kinds.astype(BF16)
    zero = jnp.zeros((), BF16)
    sums = Sums((mix_half.shape[0], width), own, rows, fan)
    for s in range(rows):
        mine = hid[s * units : (s + 1) * units, :]
        kind = jnp.broadcast_to(kinds[s : s + 1], (units, width))
        sorted_out = [
            jnp.where(kind == jnp.full((), k, BF16), mine, zero) for k in range(species)
        ]
        sums.add(s, dot(first[...], jnp.concatenate(sorted_out, axis=0)))
    rows_of = lax.broadcasted_iota(I32, (kinds_count, width), 0).astype(F32)
    same = rows_of == seated[SPECIES_ROW : SPECIES_ROW + 1, lo : lo + width]
    feats = dot(embed_t[...], jnp.where(same, 1.0, 0.0).astype(BF16))
    return update_of(feats, sums.done(), mix_half[...], fan)


def turned(matrix):
    size = matrix.shape[1]
    row = lax.broadcasted_iota(I32, (size, size), 0)
    column = lax.broadcasted_iota(I32, (size, size), 1)
    identity = jnp.where(row == column, 1.0, 0.0).astype(BF16)
    return lax.dot_general(
        identity, matrix, (((1,), (1,)), ((), ())), preferred_element_type=F32
    )


def prepare(embed, rad_in, rad_out, mixing, embed_t, first, spread, out_t, mix_half):
    layers, count, units = rad_in.shape
    fan = spread.shape[1] // units
    for layer in range(layers):
        half = rad_in[layer].astype(F32) * 0.5
        weight = turned(jnp.concatenate([half] * fan, axis=0).astype(BF16))
        owner = lax.broadcasted_iota(I32, weight.shape, 1) // count
        for s in range(fan):
            only = jnp.where(owner == s, weight, 0.0).astype(BF16)
            spread[layer, s * units : (s + 1) * units, :] = only
        out_t[layer] = turned(rad_out[layer]).astype(BF16)
    for layer in range(mixing.shape[0]):
        mix_half[layer] = (turned(mixing[layer]) * 0.5).astype(BF16)
    out = rad_out[0].astype(F32)
    table = embed[...].astype(F32)
    species = table.shape[0]
    padded = jnp.concatenate(
        [table, jnp.zeros((embed_t.shape[1] - species, table.shape[1]), F32)], axis=0
    )
    embed_t[...] = turned(padded.astype(BF16)).astype(BF16)
    scaled = jnp.concatenate([out * table[k : k + 1] for k in range(species)], axis=0)
    first[...] = turned(scaled.astype(BF16)).astype(BF16)


def seat_tile(width, pk, nbr, table, seated, edges, owns, depth, delta_out, basis_out, kinds_out, place_out, index):
    atoms = pk.shape[1]
    blocks = atoms // width
    index[...] = nbr[...].astype(F32)
    table[...] = pk[...]
    found = [seat_block(pk, index, b * width, width, seated) for b in range(blocks)]
    both = [counts[0] + counts[1] for _, _, counts in found]
    most = functools.reduce(jnp.maximum, both)
    fits = jnp.max(most, axis=1, keepdims=True) <= float(2 * short_rows(nbr.shape[0]))
    depth[...] = jnp.where(
        jnp.broadcast_to(fits, depth.shape), float(short_rows(nbr.shape[0])), float(nbr.shape[0])
    )
    for b, (seat, pieces, counts) in enumerate(found):
        table[SEAT_ROW : SEAT_ROW + 1, b * width : (b + 1) * width] = seat
        edges[b], owns[b] = fill_rows(pieces, counts, fits)
    for part in halves(2 * width):
        wanted = jnp.broadcast_to(pk[SEND_ROW : SEND_ROW + 1, part].astype(I32), (PACK_ROWS, LANES))
        seats = lane_lookup([table[SEAT_ROW : SEAT_ROW + 1, p] for p in halves(atoms)], wanted)
        seats = seats + (wanted // width).astype(F32) * float(width)
        table[SEND_ROW : SEND_ROW + 1, part] = seats[:1]

    for i in range(blocks - 2):
        lo = (i + 1) * width
        locate_block(
            i, table, lo - width, seated, edges[i + 1], owns[i + 1], lo, width,
            delta_out, basis_out, kinds_out, place_out,
        )


def first_inner(width, ref_energy, pk, seated, owns, depth, basis, kinds, embed, rad_in, rad_out, mixing, w_in, feats_out, embed_t, first, spread, out_t, mix_half, w_row, ref_row, hid):
    prepare(embed, rad_in, rad_out, mixing, embed_t, first, spread, out_t, mix_half)
    weights = (embed_t, first, mix_half.at[0], spread.at[0])
    w_row[...] = w_in[...]
    kinds_row = pk[SPECIES_ROW : SPECIES_ROW + 1, :]
    energy = jnp.zeros(kinds_row.shape, F32)
    for k in range(ref_energy.shape[0]):
        energy = jnp.where(kinds_row == float(k), ref_energy[k], energy)
    ref_row[...] = energy
    def run(rows):
        for i in range(kinds.shape[0]):
            fill_hidden(hid.at[i], spread.at[0], basis[i], rows, kinds.shape[1])
        for i in range(kinds.shape[0]):
            feats_out[:, i * width : (i + 1) * width] = first_block(
                rows, kinds[i], hid.at[i], owns.at[i + 1], seated, (i + 1) * width, width, weights
            )

    by_depth(depth, kinds.shape[1], run)


def pack_halo(feats, table, core, width, to_mate, to_cross):
    atoms = feats.shape[1]
    rows = lax.broadcasted_iota(I32, (width, width), 0).astype(F32).astype(BF16)
    one, zero = jnp.ones((), BF16), jnp.zeros((), BF16)
    for ref, start in ((to_mate, (1 - core) * width), (to_cross, core * width)):
        wanted = table[SEND_ROW : SEND_ROW + 1, pl.ds(aligned(start, width), width)]
        picks = []
        for k in range(atoms // width):
            place = jnp.clip(wanted - float(k * width), -1.0, float(width)).astype(BF16)
            picks.append(jnp.where(rows == place, one, zero))
        ref[...] = dot(feats[...], jnp.concatenate(picks, axis=0)).astype(BF16)


def halo_places(core, atoms, width):
    top = atoms + width
    return aligned((1 - core) * top, width), aligned(core * top, width)


def edge_blocks(blocks, width):
    return [(0, 0, 0), (1, blocks - 1, (blocks - 1) * width)]


def first_outer(width, core_ref, pk, own_table, seated, mate, cross, edges, owns, depth, embed_t, first, spread, mix_half, inner, delta_out, basis_out, place_out, feats_out, to_mate, to_cross, pair_out, table, kinds, hid):
    core = core_ref[0]
    atoms = pk.shape[1]
    blocks = atoms // width
    fan = edges.shape[1]
    weights = (embed_t, first, mix_half.at[0], spread.at[0])
    table[:, width : width + atoms] = own_table[...]
    at_mate, at_cross = halo_places(core, atoms, width)
    for ref, start, at in ((mate, core * width, at_mate), (cross, (1 - core) * width, at_cross)):
        spans = [ref[:, part] for part in halves(atoms)]
        for k in range(width // LANES):
            wanted = ref[SEND_ROW : SEND_ROW + 1, pl.ds(aligned(start + k * LANES, LANES), LANES)]
            wanted = jnp.broadcast_to(wanted.astype(I32), (PACK_ROWS, LANES))
            place = pl.ds(aligned(at + k * LANES, LANES), LANES)
            table[:, place] = lane_lookup(spans, wanted)
            lane = lax.broadcasted_iota(I32, (1, LANES), 1) + k * LANES
            table[SEAT_ROW : SEAT_ROW + 1, place] = lane.astype(F32)
    feats_out[:, width : atoms - width] = inner[...]
    pair_out[0:4, :] = pk[0:4, :]
    pair_out[4:8, :] = mate[0:4, :]

    for i, b, lo in edge_blocks(blocks, width):
        locate_block(
            i, table, lo, seated, edges[b], owns[b], lo, width,
            delta_out, basis_out, kinds, place_out,
        )

    def run(rows):
        for i in range(2):
            fill_hidden(hid.at[i], spread.at[0], basis_out[i], rows, fan)
        for i, b, lo in edge_blocks(blocks, width):
            feats_out[:, lo : lo + width] = first_block(
                rows, kinds[i], hid.at[i], owns.at[b], seated, lo, width, weights
            )

    by_depth(depth, fan, run)
    pack_halo(feats_out, own_table, core, width, to_mate, to_cross)


def places_of(place, width, tiles=(0, 1, 2)):
    return [jnp.clip(place - float(k * width), -1.0, float(width)).astype(BF16) for k in tiles]


def fetch_rows(window, places, s, width):
    rows = lax.broadcasted_iota(I32, (width, width), 0).astype(F32).astype(BF16)
    one, zero = jnp.ones((), BF16), jnp.zeros((), BF16)
    picks = [jnp.where(rows == place[s : s + 1], one, zero) for place in places]
    return dot(window, jnp.concatenate(picks, axis=0))


def layer_block(rows, window, place, own, hid, out_t, mix_half, feats):
    fan, width = place.shape
    places = places_of(place, width)
    sums = Sums(feats.shape, own, rows, fan)
    for s in range(rows):
        far = fetch_rows(window, places, s, width)
        sums.add(s, far * dot(out_t, hid(s)))
    return update_of(feats, sums.done(), mix_half, fan)


def stored(hid_edge, i, units):
    return lambda s: hid_edge[i, s * units : (s + 1) * units, :]


def layer_inner(width, layer, owns, depth, spreads, outs_t, mixes, feats, basis, place, basis_edge, place_edge, pair, feats_out, field_edge, total_edge, lent_edge, pair_out, hid):
    pair_out[...] = pair[...]
    spread, out_t, mix_half = spreads.at[layer], outs_t[layer], mixes[layer]
    units = out_t.shape[1]
    fan = place.shape[1]
    inner = place.shape[0]

    def run(rows):
        for i in range(inner):
            fill_hidden(hid.at[i], spread, basis[i], rows, fan)
        for i in range(2):
            fill_hidden(hid.at[inner + i], spread, basis_edge[i], rows, fan)
        for i in range(inner):
            lo = (i + 1) * width
            feats_out[:, lo - width : lo] = layer_block(
                rows, feats[:, lo - width : lo + 2 * width], place[i], owns.at[i + 1],
                stored(hid, i, units), out_t, mix_half, feats[:, lo : lo + width],
            )
        for i, b, lo in edge_blocks(inner + 2, width):
            near = max(lo - width, 0)
            window = feats[:, near : near + 2 * width]
            places = places_of(place_edge[i], width, (0, 1) if i else (1, 2))
            sums = Sums(total_edge.shape[1:], owns.at[b], rows, fan)
            for s in range(rows):
                field = dot(out_t, stored(hid, inner + i, units)(s))
                field_edge[i, s] = field
                sums.add(s, fetch_rows(window, places, s, width) * field)
            total_edge[i] = sums.total
            lent_edge[i] = sums.lent

    by_depth(depth, fan, run)


def halo_of(i, core, mate, cross):
    lower_by_mate = core == (0 if i else 1)
    return jnp.where(lower_by_mate, mate[...], cross[...])


def layer_outer(width, layer, core_ref, own_table, owns, depth, mixes, feats, place, mate, cross, field_edge, total_edge, lent_edge, inner, feats_out, to_mate, to_cross):
    core = core_ref[0]
    atoms = feats.shape[1]
    fan = place.shape[1]
    mix_half = mixes[layer]
    feats_out[:, width : atoms - width] = inner[...]

    def run(rows):
        for i, b, lo in edge_blocks(atoms // width, width):
            halo = halo_of(i, core, mate, cross)
            places = places_of(place[i], width, (2,) if i else (0,))
            sums = Sums(None, owns.at[b], rows, fan, total_edge[i], lent_edge[i])
            for s in range(rows):
                sums.add(s, fetch_rows(halo, places, s, width) * field_edge[i, s])
            feats_out[:, lo : lo + width] = update_of(
                feats[:, lo : lo + width], sums.done(), mix_half, fan
            )

    by_depth(depth, fan, run)
    pack_halo(feats_out, own_table, core, width, to_mate, to_cross)


def near_of(near, own, s, alone):
    if s < alone:
        return near
    lower = jnp.where(own[s : s + 1] > 0.5, near[:, LANES:], near[:, :LANES])
    return jnp.concatenate([near[:, :LANES], lower], axis=1)


def filled(pairs, fan):
    if len(pairs) < fan:
        pairs.append(jnp.zeros((fan - len(pairs), pairs[0].shape[1]), F32))
    return jnp.concatenate(pairs, axis=0)


def force_of(pair, own, delta, seat, chans):
    fan, width = pair.shape
    pair = pair * (1.0 / math.sqrt(chans))
    mine = own[...] > 0.5
    out = []
    for c in range(3):
        terms = pair * delta[c * fan : (c + 1) * fan, :]
        second = terms[:, LANES:]
        lent = jnp.where(mine, 0.0, second)
        out.append(
            jnp.concatenate(
                [
                    jnp.sum(terms[:, :LANES] + lent, axis=0, keepdims=True),
                    jnp.sum(jnp.where(mine, second, 0.0), axis=0, keepdims=True),
                ],
                axis=1,
            )
        )
    seated = jnp.concatenate(out + [jnp.zeros((PACK_ROWS - 3, width), F32)], axis=0)
    spans = [seated[:, part] for part in halves(width)]
    seat = seat.astype(I32)
    return jnp.concatenate(
        [
            lane_lookup(spans, jnp.broadcast_to(seat[:, part], (PACK_ROWS, LANES)))
            for part in halves(width)
        ],
        axis=1,
    )


def head_inner(width, layer, own_table, owns, depth, spreads, outs_t, feats, basis, place, delta, basis_edge, place_edge, force_out, field_edge, pair_edge, hid):
    spread, out_t = spreads.at[layer], outs_t[layer]
    chans, units = out_t.shape
    fan = place.shape[1]
    inner = place.shape[0]

    def run(rows):
        for i in range(inner):
            fill_hidden(hid.at[i], spread, basis[i], rows, fan)
        for i in range(2):
            fill_hidden(hid.at[inner + i], spread, basis_edge[i], rows, fan)
        alone = 2 * rows - fan
        for i in range(inner):
            lo = (i + 1) * width
            window = feats[:, lo - width : lo + 2 * width]
            near = feats[:, lo : lo + width].astype(F32)
            places = places_of(place[i], width)
            pairs = []
            for s in range(rows):
                field = dot(out_t, stored(hid, i, units)(s))
                field = field * near_of(near, owns.at[i + 1], s, alone)
                terms = fetch_rows(window, places, s, width) * field
                pairs.append(jnp.sum(terms, axis=0, keepdims=True))
            force_out[:, lo - width : lo] = force_of(
                filled(pairs, fan), owns.at[i + 1], delta.at[i],
                own_table[SEAT_ROW : SEAT_ROW + 1, lo : lo + width], chans,
            )
        for i, b, lo in edge_blocks(inner + 2, width):
            start = max(lo - width, 0)
            window = feats[:, start : start + 2 * width]
            near = feats[:, lo : lo + width].astype(F32)
            places = places_of(place_edge[i], width, (0, 1) if i else (1, 2))
            pairs = []
            for s in range(rows):
                field = dot(out_t, stored(hid, inner + i, units)(s))
                field = field * near_of(near, owns.at[b], s, alone)
                field_edge[i, s] = field
                terms = fetch_rows(window, places, s, width) * field
                pairs.append(jnp.sum(terms, axis=0, keepdims=True))
            pair_edge[i] = filled(pairs, fan)

    by_depth(depth, fan, run)


def lane_sum(values):
    total = values[:, :LANES]
    for part in halves(values.shape[1])[1:]:
        total = total + values[:, part]
    return jnp.sum(total, axis=0, keepdims=True)


def head_outer(width, core_ref, own_table, owns, depth, place, delta, mate, cross, field_edge, pair_edge, inner, force_out):
    core = core_ref[0]
    chans = mate.shape[0]
    atoms = own_table.shape[1]
    fan = place.shape[1]
    force_out[:, width : atoms - width] = inner[...]

    def run(rows):
        for i, b, lo in edge_blocks(atoms // width, width):
            halo = halo_of(i, core, mate, cross)
            places = places_of(place[i], width, (2,) if i else (0,))
            pairs = []
            for s in range(rows):
                terms = fetch_rows(halo, places, s, width) * field_edge[i, s]
                pairs.append(jnp.sum(terms, axis=0, keepdims=True))
            force_out[:, lo : lo + width] = force_of(
                pair_edge[i] + filled(pairs, fan), owns.at[b], delta.at[i],
                own_table[SEAT_ROW : SEAT_ROW + 1, lo : lo + width], chans,
            )

    by_depth(depth, fan, run)


def pass_on(received, _, out):
    out[...] = received[...]


def tail(core_ref, pk, received, relayed, w_row, ref_row, feats, force_in, band_out, sums_out):
    core = core_ref[0]
    energy = dot(w_row[...], feats[...]) + ref_row[...]
    back = pk[0:4, :] - jnp.where(core == 0, relayed[0:4, :], received[4:8, :])
    fore = jnp.where(core == 0, received[4:8, :], relayed[0:4, :]) - pk[0:4, :]
    band_out[0:4, :] = back
    band_out[4:8, :] = fore
    back, fore, force = back[:3], fore[:3], force_in[0:3, :]
    rows = [energy, back * back, fore * fore, back * fore, force * back, force * fore]
    sums = [lane_sum(row) for row in rows]
    sums.append(jnp.zeros((SUM_ROWS - len(sums), LANES), F32))
    sums_out[...] = jnp.concatenate(sums, axis=0)


def add_sums(mine, other, out):
    out[...] = mine[...] + other[...]


def finish(count, flags, band, force, *rest):
    *parts, result, energy_out = rest
    total = parts[0][...]
    for part in parts[1:]:
        total = total + part[...]
    total = jnp.sum(total, axis=1, keepdims=True)
    energy, back_sq, fore_sq, cross, along_back, along_fore = (total[i : i + 1] for i in range(6))
    back_len = jnp.sqrt(back_sq + 1e-06)
    fore_len = jnp.sqrt(fore_sq + 1e-06)
    by_back, by_fore = 1.0 / back_len, 1.0 / fore_len
    tau_sq = (
        back_sq * by_back * by_back + fore_sq * by_fore * by_fore + 2.0 * cross * by_back * by_fore
    )
    proj = (along_back * by_back + along_fore * by_fore) / tau_sq
    spring = SPRING * (fore_len - back_len) / jnp.sqrt(tau_sq)
    climbing = flags[1] == 1
    is_end = flags[0] == 1
    factor = jnp.where(climbing, -2.0 * proj, spring - proj)
    tangent = band[0:3, :] * by_back + band[4:7, :] * by_fore
    moved = jnp.where(is_end, force[0:3, :], force[0:3, :] + factor * tangent)
    for c in range(3):
        result[c] = moved[c : c + 1]
    energy_out[...] = energy * (1.0 / count)


def swap_pairs(count, offset):
    pairs = []
    for low in range(offset, count, 2):
        high = (low + 1) % count
        pairs += [(low, high), (high, low)]
    return pairs


def image_pairs(images, tiles):
    pairs = []
    for low in range(images):
        high = (low + 1) % images
        for tile in range(0, tiles, 2):
            a, b = low * tiles + tile, high * tiles + tile + 1
            pairs += [(a, b), (b, a)]
    return pairs


def on_device(positions, species, counts, neighbours, send_list, climb, embed, ref_energy, rad_in, rad_out, mixing, w_energy):
    atoms = species.shape[0]
    width = send_list.shape[0] // 2
    fan = neighbours.shape[0]
    chans = embed.shape[1]
    layers = mixing.shape[0]
    basis_count, units = rad_in.shape[1:]
    blocks = atoms // width
    inner_atoms = (blocks - 2) * width
    tiles = lax.axis_size("atom")
    images = lax.axis_size("img")
    core = lax.rem(lax.axis_index("atom"), 2)
    image = lax.axis_index("img")
    core_arr = core.reshape(1).astype(I32)
    is_end = jnp.logical_or(image == 0, image == images - 1)
    flags = jnp.stack([is_end.astype(I32), climb[0]])

    def call(body, operands, outs, scratch=(), flops=0):
        scalars = {id(x) for x in (core_arr, flags, ref_energy)}
        return pl.pallas_call(
            body,
            out_shape=[jax.ShapeDtypeStruct(shape, dtype) for shape, dtype in outs],
            in_specs=[SMEM if id(x) in scalars else VMEM for x in operands],
            out_specs=[VMEM] * len(outs),
            scratch_shapes=[pltpu.VMEM(*x) for x in scratch],
            cost_estimate=pl.CostEstimate(flops=flops, bytes_accessed=2**20, transcendentals=0),
            compiler_params=pltpu.CompilerParams(vmem_limit_bytes=16 * 2**20),
        )(*operands)

    def swap(block, offset):
        return lax.ppermute(block, "atom", swap_pairs(tiles, offset))

    pack_type = ((PACK_ROWS, atoms), F32)
    feats_type = ((chans, atoms), BF16)
    halo_type = ((chans, width), BF16)
    hid_type = ((2, fan * units, width), BF16)
    hid_scratch = ((blocks - 2, fan * units, width), BF16)

    def block_outs(count):
        return [
            ((count, 3 * fan, width), F32),
            ((count, fan * basis_count, width), BF16),
            ((count, fan, width), F32),
        ]

    row = lax.broadcasted_iota(I32, (PACK_ROWS, atoms), 0)
    sends = jnp.pad(send_list, (0, atoms - 2 * width))
    (pk,) = call(blank, (), [pack_type], flops=2**33)
    lines = [positions[0, c] for c in range(3)] + [species, counts, sends]
    for place, line in enumerate(lines):
        pk = jnp.where(row == place, lax.broadcast_in_dim(line, pk.shape, (1,)).astype(F32), pk)
    mate = swap(pk, 0)
    cross = swap(pk, 1)
    kinds_type = ((blocks - 2, fan, width), F32)
    own_table, seated, edges, owns, depth, delta_in, basis_in, kinds_in, place_in = call(
        functools.partial(seat_tile, width),
        (pk, neighbours),
        [
            pack_type,
            pack_type,
            ((blocks, fan, width), F32),
            ((blocks, fan, LANES), F32),
            ((PACK_ROWS, LANES), F32),
        ]
        + block_outs(blocks - 2)[:2]
        + [kinds_type, kinds_type],
        [((fan, atoms), F32)],
        flops=2**32,
    )
    inner, embed_t, first, spread, out_t, mix_half, w_row, ref_row = call(
        functools.partial(first_inner, width),
        (ref_energy, pk, seated, owns, depth, basis_in, kinds_in, embed, rad_in, rad_out, mixing, w_energy[None]),
        [
            ((chans, inner_atoms), BF16),
            ((chans, -(-embed.shape[0] // 16) * 16), BF16),
            ((chans, embed.shape[0] * units), BF16),
            ((layers + 1, fan * units, fan * basis_count), BF16),
            ((layers + 1, chans, units), BF16),
            ((layers, chans, chans), BF16),
            ((1, chans), BF16),
            ((1, atoms), F32),
        ],
        [hid_scratch],
        flops=2**32,
    )
    delta_out, basis_out, place_out, feats, to_mate, to_cross, pair = call(
        functools.partial(first_outer, width),
        (core_arr, pk, own_table, seated, mate, cross, edges, owns, depth, embed_t, first, spread, mix_half, inner),
        block_outs(2) + [feats_type, halo_type, halo_type, pack_type],
        [((PACK_ROWS, atoms + 2 * width), F32), ((2, fan, width), F32), hid_type],
    )
    for layer in range(1, layers):
        cross = swap(to_cross, 1)
        mate = swap(to_mate, 0)
        inner, field_edge, total_edge, lent_edge, pair = call(
            functools.partial(layer_inner, width, layer),
            (owns, depth, spread, out_t, mix_half, feats, basis_in, place_in, basis_out, place_out, pair),
            [
                ((chans, inner_atoms), BF16),
                ((2, fan, chans, width), F32),
                ((2, chans, width), F32),
                ((2, chans, LANES), F32),
                pack_type,
            ],
            [((blocks, fan * units, width), BF16)],
            flops=2**32,
        )
        feats, to_mate, to_cross = call(
            functools.partial(layer_outer, width, layer),
            (core_arr, own_table, owns, depth, mix_half, feats, place_out, mate, cross, field_edge, total_edge, lent_edge, inner),
            [feats_type, halo_type, halo_type],
        )
    received = lax.ppermute(pair, ("img", "atom"), image_pairs(images, tiles))
    cross = swap(to_cross, 1)
    mate = swap(to_mate, 0)
    inner, field_edge, pair_edge = call(
        functools.partial(head_inner, width, layers),
        (own_table, owns, depth, spread, out_t, feats, basis_in, place_in, delta_in, basis_out, place_out),
        [((PACK_ROWS, inner_atoms), F32), ((2, fan, chans, width), F32), ((2, fan, width), F32)],
        [((blocks, fan * units, width), BF16)],
        flops=2**32,
    )
    (late,) = call(pass_on, (received, inner), [pack_type])
    relayed = swap(late, 0)
    (force,) = call(
        functools.partial(head_outer, width),
        (core_arr, own_table, owns, depth, place_out, delta_out, mate, cross, field_edge, pair_edge, inner),
        [pack_type],
        flops=2**32,
    )
    band, sums = call(
        tail,
        (core_arr, pk, received, relayed, w_row, ref_row, feats, force),
        [pack_type, ((SUM_ROWS, LANES), F32)],
    )
    step = 2 * REDUCE_CHIPS
    while step < tiles:
        sums = sums + lax.ppermute(sums, "atom", [(i, i ^ step) for i in range(tiles)])
        step *= 2
    (both,) = call(add_sums, (sums, swap(sums, 0)), [((SUM_ROWS, LANES), F32)])
    near = lax.ppermute(both, "atom", [(i, i ^ 2 if i % 2 == 0 else i ^ 6) for i in range(tiles)])
    far = lax.ppermute(both, "atom", [(i, i ^ 4) for i in range(tiles)])
    other = swap(near, 0)
    result, energy = call(
        functools.partial(finish, atoms * tiles),
        (flags, band, force, both, near, far, other),
        [((3, 1, atoms), F32), ((1, 1), F32)],
    )
    return jnp.transpose(result, (1, 0, 2)), energy.reshape(1)


def solution(mesh):
    return jax.shard_map(
        on_device,
        mesh=mesh,
        in_specs=(
            P("img", None, "atom"),
            P("atom"),
            P("atom"),
            P(None, "atom"),
            P("atom"),
            P("img"),
            P(),
            P(),
            P(),
            P(),
            P(),
            P(),
        ),
        out_specs=(P("img", None, "atom"), P("img")),
        check_vma=False,
    )
```

```python
import functools
import math

import jax
import jax.numpy as jnp
from jax import lax
from jax.experimental import pallas as pl
from jax.experimental.pallas import tpu as pltpu
from jax.sharding import PartitionSpec as P

F32 = jnp.float32
BF16 = jnp.bfloat16
I32 = jnp.int32
LANES = 128
SPRING = 5.0
SPECIES_ROW = 3
COUNT_ROW = 4
SEND_ROW = 5
SEAT_ROW = 6
CLIMB_ROW = 7
PACK_ROWS = 8
SUM_ROWS = 8
REDUCE_CHIPS = 4
VMEM = pl.BlockSpec(memory_space=pltpu.VMEM)


def core_index():
    return lax.rem(lax.axis_index("atom"), 2)


def dot(a, b):
    return jnp.dot(a, b, preferred_element_type=F32)


def silu_of_half(half):
    return half + half * jnp.tanh(half)


def aligned(start, step):
    return pl.multiple_of(start, step)


def halves(width):
    return [slice(k * LANES, (k + 1) * LANES) for k in range(width // LANES)]


def short_rows(fan):
    return -(-5 * fan // 8)


def lane_fetch(windows, group, place):
    found = jnp.zeros(place.shape, F32)
    for k, window in enumerate(windows):
        rows = jnp.broadcast_to(window, place.shape)
        picked = jnp.take_along_axis(rows, place, axis=1, mode="promise_in_bounds")
        found = jnp.where(group == k, picked, found)
    return found


def lane_lookup(windows, index):
    return lane_fetch(windows, index // LANES, index & (LANES - 1))


def blank(out):
    out[...] = jnp.zeros(out.shape, F32)


def seat_atoms(pk, lo, width, most):
    counts = pk[COUNT_ROW : COUNT_ROW + 1, lo : lo + width]
    value = lax.broadcasted_iota(I32, (most, width), 0).astype(F32) + 1.0
    same = counts == value
    row = lax.broadcasted_iota(I32, (width, width), 0)
    lane = lax.broadcasted_iota(I32, (width, width), 1)
    earlier = dot(jnp.where(same, 1.0, 0.0).astype(BF16), jnp.where(row < lane, 1.0, 0.0).astype(BF16))
    larger = jnp.sum(jnp.where(counts > value, 1.0, 0.0), axis=1, keepdims=True)
    rank = jnp.sum(jnp.where(same, earlier + larger, 0.0), axis=0, keepdims=True)
    seat = jnp.where(rank < width // 2, rank, 1.5 * width - 1.0 - rank)
    taken = jnp.where(row.astype(F32) == seat, 1.0, 0.0).astype(BF16)
    atoms = lax.broadcasted_iota(I32, (PACK_ROWS, width), 1).astype(F32).astype(BF16)
    taker = lax.dot_general(
        atoms, taken, (((1,), (1,)), ((), ())), preferred_element_type=F32
    )
    return seat, taker[:1]


def seat_block(pk, nbr, lo, width, seated):
    fan = nbr.shape[0]
    seat, taker = seat_atoms(pk, lo, width, fan)
    pieces, tables = [], []
    for part in halves(width):
        who = taker[:, part].astype(I32)
        spans = [nbr[:, lo + p.start : lo + p.stop] for p in halves(width)]
        pieces.append(lane_lookup(spans, jnp.broadcast_to(who, (fan, LANES))) - float(lo))
        spans = [pk[:, lo + p.start : lo + p.stop] for p in halves(width)]
        tables.append(lane_lookup(spans, jnp.broadcast_to(who, (PACK_ROWS, LANES))))
    seated[:, lo : lo + width] = jnp.concatenate(tables, axis=1)
    return seat, pieces, [x[COUNT_ROW : COUNT_ROW + 1] for x in tables]


def fill_rows(pieces, counts, fits):
    first, second = pieces
    fan = first.shape[0]
    short = short_rows(fan)
    limit = jnp.where(fits, float(short), float(fan))
    row = lax.broadcasted_iota(I32, (fan, LANES), 0).astype(F32)
    mine = row < counts[1]
    over = [2 * short - 1 - r if 0 <= 2 * short - 1 - r < fan else 0 for r in range(fan)]
    over = jnp.concatenate([first[r : r + 1] for r in over], axis=0)
    spilled = jnp.logical_and(fits, 2.0 * short - 1.0 - row < counts[0])
    spilled = jnp.logical_and(spilled, row < float(short))
    spilled = jnp.logical_and(spilled, row >= float(2 * short - fan))
    spilled = jnp.logical_and(spilled, jnp.logical_not(mine))
    first = jnp.where(row < jnp.minimum(counts[0], limit), first, -1.0)
    second = jnp.where(mine, second, jnp.where(spilled, over, -1.0))
    return jnp.concatenate([first, second], axis=1), jnp.where(spilled, 0.0, 1.0)


def by_depth(depth, fan, run):
    shallow = jnp.max(depth[...]) < float(short_rows(fan)) + 0.5

    @pl.when(shallow)
    def _():
        run(short_rows(fan))

    @pl.when(jnp.logical_not(shallow))
    def _():
        run(fan)


def locate_block(i, table, table_lo, seated, edges, own, lo, width, delta_out, basis_out, kinds_out, place_out):
    fan = edges.shape[0]
    spans = [
        table[:, table_lo + p.start : table_lo + p.stop] for p in halves(3 * width)
    ]
    mine = own > 0.5
    home = seated[:, lo : lo + width]
    parts = []
    for part in halves(width):
        rel = edges[:, part].astype(I32)
        live = rel >= 0
        group, place = rel >> 7, rel & (LANES - 1)
        fetch = lambda r: lane_fetch([span[r : r + 1] for span in spans], group, place)
        values = []
        for c in range(3):
            here = home[c : c + 1, part]
            if part.start > 0:
                here = jnp.where(mine, here, home[c : c + 1, :LANES])
            values.append(fetch(c) - here)
        values.append(jnp.where(live, fetch(SPECIES_ROW), -1.0))
        tile = (rel // width).astype(F32) * float(width)
        values.append(jnp.where(live, fetch(SEAT_ROW) + tile, -1.0))
        parts.append(values)
    joined = [jnp.concatenate(list(piece), axis=1) for piece in zip(*parts)]
    for c in range(3):
        delta_out[i, c * fan : (c + 1) * fan, :] = joined[c]
    kinds_out[i] = joined[3]
    place_out[i] = joined[4]
    dist_sq = joined[0] * joined[0] + joined[1] * joined[1] + joined[2] * joined[2]
    count = basis_out.shape[1] // fan
    centres = 2.0 * lax.broadcasted_iota(I32, (count, width), 0).astype(F32)
    rows = []
    for s in range(fan):
        away = jnp.broadcast_to(dist_sq[s : s + 1], (count, width)) - centres
        rows.append(jnp.exp(away * away * -0.125))
    basis_out[i] = jnp.concatenate(rows, axis=0).astype(BF16)


def fill_hidden(target, spread, basis, rows, fan):
    used = rows * (spread.shape[0] // fan)
    target[:used, :] = silu_of_half(dot(spread[:used, :], basis)).astype(BF16)


class Sums:
    def __init__(self, shape, own, rows, fan, total=None, lent=None):
        self.total = jnp.zeros(shape, F32) if total is None else total
        self.lent = jnp.zeros((shape[0], LANES), F32) if lent is None else lent
        self.own, self.alone = own, 2 * rows - fan

    def add(self, s, terms):
        self.total = self.total + terms
        if s >= self.alone:
            self.lent = self.lent + jnp.where(self.own[s : s + 1] > 0.5, 0.0, terms[:, LANES:])

    def done(self):
        first, second = self.total[:, :LANES], self.total[:, LANES:]
        return jnp.concatenate([first + self.lent, second - self.lent], axis=1)


def update_of(feats, summed, mix_half, fan):
    scaled = (summed * (1.0 / math.sqrt(fan))).astype(BF16)
    return (feats.astype(F32) + silu_of_half(dot(mix_half, scaled))).astype(BF16)


def first_block(rows, kinds, hid, own, seated, lo, width, weights):
    embed_t, first, mix_half, spread = weights
    fan = kinds.shape[0]
    kinds_count = embed_t.shape[1]
    units = spread.shape[0] // fan
    species = first.shape[1] // units
    kinds = kinds.astype(BF16)
    zero = jnp.zeros((), BF16)
    sums = Sums((mix_half.shape[0], width), own, rows, fan)
    for s in range(rows):
        mine = hid[s * units : (s + 1) * units, :]
        kind = jnp.broadcast_to(kinds[s : s + 1], (units, width))
        sorted_out = [
            jnp.where(kind == jnp.full((), k, BF16), mine, zero) for k in range(species)
        ]
        sums.add(s, dot(first[...], jnp.concatenate(sorted_out, axis=0)))
    rows_of = lax.broadcasted_iota(I32, (kinds_count, width), 0).astype(F32)
    same = rows_of == seated[SPECIES_ROW : SPECIES_ROW + 1, lo : lo + width]
    feats = dot(embed_t[...], jnp.where(same, 1.0, 0.0).astype(BF16))
    return update_of(feats, sums.done(), mix_half[...], fan)


def turned(matrix):
    size = matrix.shape[1]
    row = lax.broadcasted_iota(I32, (size, size), 0)
    column = lax.broadcasted_iota(I32, (size, size), 1)
    identity = jnp.where(row == column, 1.0, 0.0).astype(BF16)
    return lax.dot_general(
        identity, matrix, (((1,), (1,)), ((), ())), preferred_element_type=F32
    )


def prepare(embed, rad_in, rad_out, mixing, embed_t, first, spread, out_t, mix_half):
    layers, count, units = rad_in.shape
    fan = spread.shape[1] // units
    for layer in range(layers):
        half = rad_in[layer].astype(F32) * 0.5
        weight = turned(jnp.concatenate([half] * fan, axis=0).astype(BF16))
        owner = lax.broadcasted_iota(I32, weight.shape, 1) // count
        for s in range(fan):
            only = jnp.where(owner == s, weight, 0.0).astype(BF16)
            spread[layer, s * units : (s + 1) * units, :] = only
        out_t[layer] = turned(rad_out[layer]).astype(BF16)
    for layer in range(mixing.shape[0]):
        mix_half[layer] = (turned(mixing[layer]) * 0.5).astype(BF16)
    out = rad_out[0].astype(F32)
    table = embed[...].astype(F32)
    species = table.shape[0]
    padded = jnp.concatenate(
        [table, jnp.zeros((embed_t.shape[1] - species, table.shape[1]), F32)], axis=0
    )
    embed_t[...] = turned(padded.astype(BF16)).astype(BF16)
    scaled = jnp.concatenate([out * table[k : k + 1] for k in range(species)], axis=0)
    first[...] = turned(scaled.astype(BF16)).astype(BF16)


def seat_tile(width, pk, nbr, table, seated, edges, owns, depth, delta_out, basis_out, kinds_out, place_out, index):
    atoms = pk.shape[1]
    blocks = atoms // width
    index[...] = nbr[...].astype(F32)
    table[...] = pk[...]
    found = [seat_block(pk, index, b * width, width, seated) for b in range(blocks)]
    both = [counts[0] + counts[1] for _, _, counts in found]
    most = functools.reduce(jnp.maximum, both)
    fits = jnp.max(most, axis=1, keepdims=True) <= float(2 * short_rows(nbr.shape[0]))
    depth[...] = jnp.where(
        jnp.broadcast_to(fits, depth.shape), float(short_rows(nbr.shape[0])), float(nbr.shape[0])
    )
    for b, (seat, pieces, counts) in enumerate(found):
        table[SEAT_ROW : SEAT_ROW + 1, b * width : (b + 1) * width] = seat
        edges[b], owns[b] = fill_rows(pieces, counts, fits)
    for part in halves(2 * width):
        wanted = jnp.broadcast_to(pk[SEND_ROW : SEND_ROW + 1, part].astype(I32), (PACK_ROWS, LANES))
        seats = lane_lookup([table[SEAT_ROW : SEAT_ROW + 1, p] for p in halves(atoms)], wanted)
        seats = seats + (wanted // width).astype(F32) * float(width)
        table[SEND_ROW : SEND_ROW + 1, part] = seats[:1]

    for i in range(blocks - 2):
        lo = (i + 1) * width
        locate_block(
            i, table, lo - width, seated, edges[i + 1], owns[i + 1], lo, width,
            delta_out, basis_out, kinds_out, place_out,
        )


def first_inner(width, ref_energy, pk, seated, owns, depth, basis, kinds, embed, rad_in, rad_out, mixing, w_in, feats_out, embed_t, first, spread, out_t, mix_half, w_row, ref_row, hid):
    prepare(embed, rad_in, rad_out, mixing, embed_t, first, spread, out_t, mix_half)
    weights = (embed_t, first, mix_half.at[0], spread.at[0])
    w_row[...] = w_in[...]
    kinds_row = pk[SPECIES_ROW : SPECIES_ROW + 1, :]
    energy = jnp.zeros(kinds_row.shape, F32)
    for k in range(ref_energy.shape[1]):
        energy = jnp.where(kinds_row == float(k), ref_energy[0:1, k : k + 1], energy)
    ref_row[...] = energy
    def run(rows):
        for i in range(kinds.shape[0]):
            fill_hidden(hid.at[i], spread.at[0], basis[i], rows, kinds.shape[1])
        for i in range(kinds.shape[0]):
            feats_out[:, i * width : (i + 1) * width] = first_block(
                rows, kinds[i], hid.at[i], owns.at[i + 1], seated, (i + 1) * width, width, weights
            )

    by_depth(depth, kinds.shape[1], run)


def pack_halo(feats, table, core, width, to_mate, to_cross):
    atoms = feats.shape[1]
    rows = lax.broadcasted_iota(I32, (width, width), 0).astype(F32).astype(BF16)
    one, zero = jnp.ones((), BF16), jnp.zeros((), BF16)
    for ref, start in ((to_mate, (1 - core) * width), (to_cross, core * width)):
        wanted = table[SEND_ROW : SEND_ROW + 1, pl.ds(aligned(start, width), width)]
        picks = []
        for k in range(atoms // width):
            place = jnp.clip(wanted - float(k * width), -1.0, float(width)).astype(BF16)
            picks.append(jnp.where(rows == place, one, zero))
        ref[...] = dot(feats[...], jnp.concatenate(picks, axis=0)).astype(BF16)


def halo_places(core, atoms, width):
    top = atoms + width
    return aligned((1 - core) * top, width), aligned(core * top, width)


def edge_blocks(blocks, width):
    return [(0, 0, 0), (1, blocks - 1, (blocks - 1) * width)]


def first_outer(width, pk, own_table, seated, mate, cross, edges, owns, depth, embed_t, first, spread, mix_half, inner, delta_out, basis_out, place_out, feats_out, to_mate, to_cross, pair_out, table, kinds, hid):
    core = core_index()
    atoms = pk.shape[1]
    blocks = atoms // width
    fan = edges.shape[1]
    weights = (embed_t, first, mix_half.at[0], spread.at[0])
    table[:, width : width + atoms] = own_table[...]
    at_mate, at_cross = halo_places(core, atoms, width)
    for ref, start, at in ((mate, core * width, at_mate), (cross, (1 - core) * width, at_cross)):
        spans = [ref[:, part] for part in halves(atoms)]
        for k in range(width // LANES):
            wanted = ref[SEND_ROW : SEND_ROW + 1, pl.ds(aligned(start + k * LANES, LANES), LANES)]
            wanted = jnp.broadcast_to(wanted.astype(I32), (PACK_ROWS, LANES))
            place = pl.ds(aligned(at + k * LANES, LANES), LANES)
            table[:, place] = lane_lookup(spans, wanted)
            lane = lax.broadcasted_iota(I32, (1, LANES), 1) + k * LANES
            table[SEAT_ROW : SEAT_ROW + 1, place] = lane.astype(F32)
    feats_out[:, width : atoms - width] = inner[...]
    pair_out[0:4, :] = pk[0:4, :]
    pair_out[4:8, :] = mate[0:4, :]

    for i, b, lo in edge_blocks(blocks, width):
        locate_block(
            i, table, lo, seated, edges[b], owns[b], lo, width,
            delta_out, basis_out, kinds, place_out,
        )

    def run(rows):
        for i in range(2):
            fill_hidden(hid.at[i], spread.at[0], basis_out[i], rows, fan)
        for i, b, lo in edge_blocks(blocks, width):
            feats_out[:, lo : lo + width] = first_block(
                rows, kinds[i], hid.at[i], owns.at[b], seated, lo, width, weights
            )

    by_depth(depth, fan, run)
    pack_halo(feats_out, own_table, core, width, to_mate, to_cross)


def places_of(place, width, tiles=(0, 1, 2)):
    return [jnp.clip(place - float(k * width), -1.0, float(width)).astype(BF16) for k in tiles]


def fetch_rows(window, places, s, width):
    rows = lax.broadcasted_iota(I32, (width, width), 0).astype(F32).astype(BF16)
    one, zero = jnp.ones((), BF16), jnp.zeros((), BF16)
    picks = [jnp.where(rows == place[s : s + 1], one, zero) for place in places]
    return dot(window, jnp.concatenate(picks, axis=0))


def layer_block(rows, window, place, own, hid, out_t, mix_half, feats):
    fan, width = place.shape
    places = places_of(place, width)
    sums = Sums(feats.shape, own, rows, fan)
    for s in range(rows):
        far = fetch_rows(window, places, s, width)
        sums.add(s, far * dot(out_t, hid(s)))
    return update_of(feats, sums.done(), mix_half, fan)


def stored(hid_edge, i, units):
    return lambda s: hid_edge[i, s * units : (s + 1) * units, :]


def layer_inner(width, layer, owns, depth, spreads, outs_t, mixes, feats, basis, place, basis_edge, place_edge, pair, feats_out, field_edge, total_edge, lent_edge, pair_out, hid):
    pair_out[...] = pair[...]
    spread, out_t, mix_half = spreads.at[layer], outs_t[layer], mixes[layer]
    units = out_t.shape[1]
    fan = place.shape[1]
    inner = place.shape[0]

    def run(rows):
        for i in range(inner):
            fill_hidden(hid.at[i], spread, basis[i], rows, fan)
        for i in range(2):
            fill_hidden(hid.at[inner + i], spread, basis_edge[i], rows, fan)
        for i in range(inner):
            lo = (i + 1) * width
            feats_out[:, lo - width : lo] = layer_block(
                rows, feats[:, lo - width : lo + 2 * width], place[i], owns.at[i + 1],
                stored(hid, i, units), out_t, mix_half, feats[:, lo : lo + width],
            )
        for i, b, lo in edge_blocks(inner + 2, width):
            near = max(lo - width, 0)
            window = feats[:, near : near + 2 * width]
            places = places_of(place_edge[i], width, (0, 1) if i else (1, 2))
            sums = Sums(total_edge.shape[1:], owns.at[b], rows, fan)
            for s in range(rows):
                field = dot(out_t, stored(hid, inner + i, units)(s))
                field_edge[i, s] = field
                sums.add(s, fetch_rows(window, places, s, width) * field)
            total_edge[i] = sums.total
            lent_edge[i] = sums.lent

    by_depth(depth, fan, run)


def halo_of(i, core, mate, cross):
    lower_by_mate = core == (0 if i else 1)
    return jnp.where(lower_by_mate, mate[...], cross[...])


def layer_outer(width, layer, own_table, owns, depth, mixes, feats, place, mate, cross, field_edge, total_edge, lent_edge, inner, feats_out, to_mate, to_cross):
    core = core_index()
    atoms = feats.shape[1]
    fan = place.shape[1]
    mix_half = mixes[layer]
    feats_out[:, width : atoms - width] = inner[...]

    def run(rows):
        for i, b, lo in edge_blocks(atoms // width, width):
            halo = halo_of(i, core, mate, cross)
            places = places_of(place[i], width, (2,) if i else (0,))
            sums = Sums(None, owns.at[b], rows, fan, total_edge[i], lent_edge[i])
            for s in range(rows):
                sums.add(s, fetch_rows(halo, places, s, width) * field_edge[i, s])
            feats_out[:, lo : lo + width] = update_of(
                feats[:, lo : lo + width], sums.done(), mix_half, fan
            )

    by_depth(depth, fan, run)
    pack_halo(feats_out, own_table, core, width, to_mate, to_cross)


def near_of(near, own, s, alone):
    if s < alone:
        return near
    lower = jnp.where(own[s : s + 1] > 0.5, near[:, LANES:], near[:, :LANES])
    return jnp.concatenate([near[:, :LANES], lower], axis=1)


def filled(pairs, fan):
    if len(pairs) < fan:
        pairs.append(jnp.zeros((fan - len(pairs), pairs[0].shape[1]), F32))
    return jnp.concatenate(pairs, axis=0)


def force_of(pair, own, delta, seat, chans):
    fan, width = pair.shape
    pair = pair * (1.0 / math.sqrt(chans))
    mine = own[...] > 0.5
    out = []
    for c in range(3):
        terms = pair * delta[c * fan : (c + 1) * fan, :]
        second = terms[:, LANES:]
        lent = jnp.where(mine, 0.0, second)
        out.append(
            jnp.concatenate(
                [
                    jnp.sum(terms[:, :LANES] + lent, axis=0, keepdims=True),
                    jnp.sum(jnp.where(mine, second, 0.0), axis=0, keepdims=True),
                ],
                axis=1,
            )
        )
    seated = jnp.concatenate(out + [jnp.zeros((PACK_ROWS - 3, width), F32)], axis=0)
    spans = [seated[:, part] for part in halves(width)]
    seat = seat.astype(I32)
    return jnp.concatenate(
        [
            lane_lookup(spans, jnp.broadcast_to(seat[:, part], (PACK_ROWS, LANES)))
            for part in halves(width)
        ],
        axis=1,
    )


def head_inner(width, layer, own_table, owns, depth, spreads, outs_t, feats, basis, place, delta, basis_edge, place_edge, force_out, field_edge, pair_edge, hid):
    spread, out_t = spreads.at[layer], outs_t[layer]
    chans, units = out_t.shape
    fan = place.shape[1]
    inner = place.shape[0]

    def run(rows):
        for i in range(inner):
            fill_hidden(hid.at[i], spread, basis[i], rows, fan)
        for i in range(2):
            fill_hidden(hid.at[inner + i], spread, basis_edge[i], rows, fan)
        alone = 2 * rows - fan
        for i in range(inner):
            lo = (i + 1) * width
            window = feats[:, lo - width : lo + 2 * width]
            near = feats[:, lo : lo + width].astype(F32)
            places = places_of(place[i], width)
            pairs = []
            for s in range(rows):
                field = dot(out_t, stored(hid, i, units)(s))
                field = field * near_of(near, owns.at[i + 1], s, alone)
                terms = fetch_rows(window, places, s, width) * field
                pairs.append(jnp.sum(terms, axis=0, keepdims=True))
            force_out[:, lo - width : lo] = force_of(
                filled(pairs, fan), owns.at[i + 1], delta.at[i],
                own_table[SEAT_ROW : SEAT_ROW + 1, lo : lo + width], chans,
            )
        for i, b, lo in edge_blocks(inner + 2, width):
            start = max(lo - width, 0)
            window = feats[:, start : start + 2 * width]
            near = feats[:, lo : lo + width].astype(F32)
            places = places_of(place_edge[i], width, (0, 1) if i else (1, 2))
            pairs = []
            for s in range(rows):
                field = dot(out_t, stored(hid, inner + i, units)(s))
                field = field * near_of(near, owns.at[b], s, alone)
                field_edge[i, s] = field
                terms = fetch_rows(window, places, s, width) * field
                pairs.append(jnp.sum(terms, axis=0, keepdims=True))
            pair_edge[i] = filled(pairs, fan)

    by_depth(depth, fan, run)


def lane_sum(values):
    total = values[:, :LANES]
    for part in halves(values.shape[1])[1:]:
        total = total + values[:, part]
    return jnp.sum(total, axis=0, keepdims=True)


def head_outer(width, own_table, owns, depth, place, delta, mate, cross, field_edge, pair_edge, inner, force_out):
    core = core_index()
    chans = mate.shape[0]
    atoms = own_table.shape[1]
    fan = place.shape[1]
    force_out[:, width : atoms - width] = inner[...]

    def run(rows):
        for i, b, lo in edge_blocks(atoms // width, width):
            halo = halo_of(i, core, mate, cross)
            places = places_of(place[i], width, (2,) if i else (0,))
            pairs = []
            for s in range(rows):
                terms = fetch_rows(halo, places, s, width) * field_edge[i, s]
                pairs.append(jnp.sum(terms, axis=0, keepdims=True))
            force_out[:, lo : lo + width] = force_of(
                pair_edge[i] + filled(pairs, fan), owns.at[b], delta.at[i],
                own_table[SEAT_ROW : SEAT_ROW + 1, lo : lo + width], chans,
            )

    by_depth(depth, fan, run)


def pass_on(received, _, out):
    out[...] = received[...]


def tail(pk, received, relayed, w_row, ref_row, feats, force_in, band_out, sums_out):
    core = core_index()
    energy = dot(w_row[...], feats[...]) + ref_row[...]
    direct, by_mate = received[0:4, :], relayed[4:8, :]
    direct_ahead = lax.rem(core + lax.axis_index("img"), 2) == 0
    back = pk[0:4, :] - jnp.where(direct_ahead, by_mate, direct)
    fore = jnp.where(direct_ahead, direct, by_mate) - pk[0:4, :]
    band_out[0:4, :] = back
    band_out[4:8, :] = fore
    back, fore, force = back[:3], fore[:3], force_in[0:3, :]
    rows = [energy, back * back, fore * fore, back * fore, force * back, force * fore]
    sums = [lane_sum(row) for row in rows]
    sums.append(jnp.zeros((SUM_ROWS - len(sums), LANES), F32))
    sums_out[...] = jnp.concatenate(sums, axis=0)


def add_sums(mine, other, out):
    out[...] = mine[...] + other[...]


def finish(count, pk, band, force, *rest):
    *parts, result, energy_out = rest
    total = parts[0][...]
    for part in parts[1:]:
        total = total + part[...]
    total = jnp.sum(total, axis=1, keepdims=True)
    energy, back_sq, fore_sq, cross, along_back, along_fore = (total[i : i + 1] for i in range(6))
    back_len = jnp.sqrt(back_sq + 1e-06)
    fore_len = jnp.sqrt(fore_sq + 1e-06)
    by_back, by_fore = 1.0 / back_len, 1.0 / fore_len
    tau_sq = (
        back_sq * by_back * by_back + fore_sq * by_fore * by_fore + 2.0 * cross * by_back * by_fore
    )
    proj = (along_back * by_back + along_fore * by_fore) / tau_sq
    spring = SPRING * (fore_len - back_len) / jnp.sqrt(tau_sq)
    image = lax.axis_index("img")
    is_end = jnp.logical_or(image == 0, image == lax.axis_size("img") - 1)
    factor = jnp.where(pk[CLIMB_ROW : CLIMB_ROW + 1, 0:1] == 1.0, -2.0 * proj, spring - proj)
    tangent = band[0:3, :] * by_back + band[4:7, :] * by_fore
    moved = jnp.where(is_end, force[0:3, :], force[0:3, :] + factor * tangent)
    for c in range(3):
        result[c] = moved[c : c + 1]
    energy_out[...] = energy * (1.0 / count)


def swap_pairs(count, offset):
    pairs = []
    for low in range(offset, count, 2):
        high = (low + 1) % count
        pairs += [(low, high), (high, low)]
    return pairs


def image_pairs(images, tiles):
    pairs = []
    for tile in range(tiles):
        pairs += [(a * tiles + tile, b * tiles + tile) for a, b in swap_pairs(images, tile % 2)]
    return pairs


def on_device(positions, species, counts, neighbours, send_list, climb, embed, ref_energy, rad_in, rad_out, mixing, w_energy):
    atoms = species.shape[0]
    width = send_list.shape[0] // 2
    fan = neighbours.shape[0]
    chans = embed.shape[1]
    layers = mixing.shape[0]
    basis_count, units = rad_in.shape[1:]
    blocks = atoms // width
    inner_atoms = (blocks - 2) * width
    tiles = lax.axis_size("atom")
    images = lax.axis_size("img")
    def call(body, operands, outs, scratch=(), flops=0):
        return pl.pallas_call(
            body,
            out_shape=[jax.ShapeDtypeStruct(shape, dtype) for shape, dtype in outs],
            in_specs=[VMEM] * len(operands),
            out_specs=[VMEM] * len(outs),
            scratch_shapes=[pltpu.VMEM(*x) for x in scratch],
            cost_estimate=pl.CostEstimate(flops=flops, bytes_accessed=2**20, transcendentals=0),
            compiler_params=pltpu.CompilerParams(vmem_limit_bytes=16 * 2**20),
        )(*operands)

    def swap(block, offset):
        return lax.ppermute(block, "atom", swap_pairs(tiles, offset))

    pack_type = ((PACK_ROWS, atoms), F32)
    feats_type = ((chans, atoms), BF16)
    halo_type = ((chans, width), BF16)
    hid_type = ((2, fan * units, width), BF16)
    hid_scratch = ((blocks - 2, fan * units, width), BF16)

    def block_outs(count):
        return [
            ((count, 3 * fan, width), F32),
            ((count, fan * basis_count, width), BF16),
            ((count, fan, width), F32),
        ]

    row = lax.broadcasted_iota(I32, (PACK_ROWS, atoms), 0)
    sends = jnp.pad(send_list, (0, atoms - 2 * width))
    (pk,) = call(blank, (), [pack_type], flops=2**33)
    lines = [positions[0, c] for c in range(3)] + [species, counts, sends, climb]
    for place, line in zip((0, 1, 2, SPECIES_ROW, COUNT_ROW, SEND_ROW, CLIMB_ROW), lines):
        pk = jnp.where(row == place, lax.broadcast_in_dim(line, pk.shape, (1,)).astype(F32), pk)
    mate = swap(pk, 0)
    cross = swap(pk, 1)
    kinds_type = ((blocks - 2, fan, width), F32)
    own_table, seated, edges, owns, depth, delta_in, basis_in, kinds_in, place_in = call(
        functools.partial(seat_tile, width),
        (pk, neighbours),
        [
            pack_type,
            pack_type,
            ((blocks, fan, width), F32),
            ((blocks, fan, LANES), F32),
            ((PACK_ROWS, LANES), F32),
        ]
        + block_outs(blocks - 2)[:2]
        + [kinds_type, kinds_type],
        [((fan, atoms), F32)],
        flops=2**32,
    )
    inner, embed_t, first, spread, out_t, mix_half, w_row, ref_row = call(
        functools.partial(first_inner, width),
        (ref_energy[None], pk, seated, owns, depth, basis_in, kinds_in, embed, rad_in, rad_out, mixing, w_energy[None]),
        [
            ((chans, inner_atoms), BF16),
            ((chans, -(-embed.shape[0] // 16) * 16), BF16),
            ((chans, embed.shape[0] * units), BF16),
            ((layers + 1, fan * units, fan * basis_count), BF16),
            ((layers + 1, chans, units), BF16),
            ((layers, chans, chans), BF16),
            ((1, chans), BF16),
            ((1, atoms), F32),
        ],
        [hid_scratch],
        flops=2**32,
    )
    delta_out, basis_out, place_out, feats, to_mate, to_cross, pair = call(
        functools.partial(first_outer, width),
        (pk, own_table, seated, mate, cross, edges, owns, depth, embed_t, first, spread, mix_half, inner),
        block_outs(2) + [feats_type, halo_type, halo_type, pack_type],
        [((PACK_ROWS, atoms + 2 * width), F32), ((2, fan, width), F32), hid_type],
    )
    for layer in range(1, layers):
        cross = swap(to_cross, 1)
        mate = swap(to_mate, 0)
        inner, field_edge, total_edge, lent_edge, pair = call(
            functools.partial(layer_inner, width, layer),
            (owns, depth, spread, out_t, mix_half, feats, basis_in, place_in, basis_out, place_out, pair),
            [
                ((chans, inner_atoms), BF16),
                ((2, fan, chans, width), F32),
                ((2, chans, width), F32),
                ((2, chans, LANES), F32),
                pack_type,
            ],
            [((blocks, fan * units, width), BF16)],
            flops=2**32,
        )
        feats, to_mate, to_cross = call(
            functools.partial(layer_outer, width, layer),
            (own_table, owns, depth, mix_half, feats, place_out, mate, cross, field_edge, total_edge, lent_edge, inner),
            [feats_type, halo_type, halo_type],
        )
    received = lax.ppermute(pair, ("img", "atom"), image_pairs(images, tiles))
    cross = swap(to_cross, 1)
    mate = swap(to_mate, 0)
    inner, field_edge, pair_edge = call(
        functools.partial(head_inner, width, layers),
        (own_table, owns, depth, spread, out_t, feats, basis_in, place_in, delta_in, basis_out, place_out),
        [((PACK_ROWS, inner_atoms), F32), ((2, fan, chans, width), F32), ((2, fan, width), F32)],
        [((blocks, fan * units, width), BF16)],
        flops=2**32,
    )
    (late,) = call(pass_on, (received, inner), [pack_type])
    relayed = swap(late, 0)
    (force,) = call(
        functools.partial(head_outer, width),
        (own_table, owns, depth, place_out, delta_out, mate, cross, field_edge, pair_edge, inner),
        [pack_type],
        flops=2**32,
    )
    band, sums = call(
        tail,
        (pk, received, relayed, w_row, ref_row, feats, force),
        [pack_type, ((SUM_ROWS, LANES), F32)],
    )
    step = 2 * REDUCE_CHIPS
    while step < tiles:
        sums = sums + lax.ppermute(sums, "atom", [(i, i ^ step) for i in range(tiles)])
        step *= 2
    (both,) = call(add_sums, (sums, swap(sums, 0)), [((SUM_ROWS, LANES), F32)])
    near = lax.ppermute(both, "atom", [(i, i ^ 2 if i % 2 == 0 else i ^ 6) for i in range(tiles)])
    far = lax.ppermute(both, "atom", [(i, i ^ 4) for i in range(tiles)])
    other = swap(near, 0)
    result, energy = call(
        functools.partial(finish, atoms * tiles),
        (pk, band, force, both, near, far, other),
        [((3, 1, atoms), F32), ((1, 1), F32)],
    )
    return jnp.transpose(result, (1, 0, 2)), energy.reshape(1)


def solution(mesh):
    return jax.shard_map(
        on_device,
        mesh=mesh,
        in_specs=(
            P("img", None, "atom"),
            P("atom"),
            P("atom"),
            P(None, "atom"),
            P("atom"),
            P("img"),
            P(),
            P(),
            P(),
            P(),
            P(),
            P(),
        ),
        out_specs=(P("img", None, "atom"), P("img")),
        check_vma=False,
    )
```

```python
import functools
import math

import jax
import jax.numpy as jnp
from jax import lax
from jax.experimental import pallas as pl
from jax.experimental.pallas import tpu as pltpu
from jax.sharding import PartitionSpec as P

F32 = jnp.float32
BF16 = jnp.bfloat16
I32 = jnp.int32
LANES = 128
SPRING = 5.0
SPECIES_ROW = 3
COUNT_ROW = 4
SEND_ROW = 5
SEAT_ROW = 6
CLIMB_ROW = 7
PACK_ROWS = 8
SUM_ROWS = 8
REDUCE_CHIPS = 4
VMEM = pl.BlockSpec(memory_space=pltpu.VMEM)


def core_index():
    return lax.rem(lax.axis_index("atom"), 2)


def dot(a, b):
    return jnp.dot(a, b, preferred_element_type=F32)


def silu_of_half(half):
    return half + half * jnp.tanh(half)


def aligned(start, step):
    return pl.multiple_of(start, step)


def halves(width):
    return [slice(k * LANES, (k + 1) * LANES) for k in range(width // LANES)]


def depths(fan):
    short = -(-5 * fan // 8)
    return [short, short + 1, short + 2, fan]


def lane_fetch(windows, group, place):
    found = jnp.zeros(place.shape, F32)
    for k, window in enumerate(windows):
        rows = jnp.broadcast_to(window, place.shape)
        picked = jnp.take_along_axis(rows, place, axis=1, mode="promise_in_bounds")
        found = jnp.where(group == k, picked, found)
    return found


def lane_lookup(windows, index):
    return lane_fetch(windows, index // LANES, index & (LANES - 1))


def blank(out):
    out[...] = jnp.zeros(out.shape, F32)


def seat_atoms(pk, lo, width, most):
    counts = pk[COUNT_ROW : COUNT_ROW + 1, lo : lo + width]
    value = lax.broadcasted_iota(I32, (most, width), 0).astype(F32) + 1.0
    same = counts == value
    row = lax.broadcasted_iota(I32, (width, width), 0)
    lane = lax.broadcasted_iota(I32, (width, width), 1)
    earlier = dot(jnp.where(same, 1.0, 0.0).astype(BF16), jnp.where(row < lane, 1.0, 0.0).astype(BF16))
    larger = jnp.sum(jnp.where(counts > value, 1.0, 0.0), axis=1, keepdims=True)
    rank = jnp.sum(jnp.where(same, earlier + larger, 0.0), axis=0, keepdims=True)
    seat = jnp.where(rank < width // 2, rank, 1.5 * width - 1.0 - rank)
    taken = jnp.where(row.astype(F32) == seat, 1.0, 0.0).astype(BF16)
    atoms = lax.broadcasted_iota(I32, (PACK_ROWS, width), 1).astype(F32).astype(BF16)
    taker = lax.dot_general(
        atoms, taken, (((1,), (1,)), ((), ())), preferred_element_type=F32
    )
    return seat, taker[:1]


def seat_block(pk, nbr, lo, width, seated):
    fan = nbr.shape[0]
    seat, taker = seat_atoms(pk, lo, width, fan)
    pieces, tables = [], []
    for part in halves(width):
        who = taker[:, part].astype(I32)
        spans = [nbr[:, lo + p.start : lo + p.stop] for p in halves(width)]
        pieces.append(lane_lookup(spans, jnp.broadcast_to(who, (fan, LANES))) - float(lo))
        spans = [pk[:, lo + p.start : lo + p.stop] for p in halves(width)]
        tables.append(lane_lookup(spans, jnp.broadcast_to(who, (PACK_ROWS, LANES))))
    seated[:, lo : lo + width] = jnp.concatenate(tables, axis=1)
    return seat, pieces, [x[COUNT_ROW : COUNT_ROW + 1] for x in tables]


def fill_rows(pieces, counts, limit):
    first, second = pieces
    fan = first.shape[0]
    row = lax.broadcasted_iota(I32, (fan, LANES), 0).astype(F32)
    mine = row < counts[1]
    spilled, over = jnp.zeros((fan, LANES), F32), first
    for rows in depths(fan)[:-1]:
        slots = [2 * rows - 1 - r if 0 <= 2 * rows - 1 - r < fan else 0 for r in range(fan)]
        here = jnp.logical_and(limit == float(rows), 2.0 * rows - 1.0 - row < counts[0])
        here = jnp.logical_and(here, row < float(rows))
        here = jnp.logical_and(here, row >= float(2 * rows - fan))
        here = jnp.logical_and(here, jnp.logical_not(mine))
        over = jnp.where(here, jnp.concatenate([first[r : r + 1] for r in slots], axis=0), over)
        spilled = jnp.where(here, 1.0, spilled)
    spilled = spilled > 0.5
    first = jnp.where(row < jnp.minimum(counts[0], limit), first, -1.0)
    second = jnp.where(mine, second, jnp.where(spilled, over, -1.0))
    return jnp.concatenate([first, second], axis=1), jnp.where(spilled, 0.0, 1.0)


def by_depth(depth, fan, run):
    limit = jnp.max(depth[...])
    short = depths(fan)[0]

    @pl.when(limit < short + 0.5)
    def _():
        run(short)

    @pl.when(limit > short + 0.5)
    def _():
        run(limit.astype(I32))


def over_rows(rows, step, carry):
    if isinstance(rows, int):
        for s in range(rows):
            carry = step(s, carry)
        return carry
    return lax.fori_loop(0, rows, step, carry)


def spill_from(rows, fan):
    return 2 * rows - fan if isinstance(rows, int) else 0


def may_spill(s, first):
    return not isinstance(s, int) or s >= first


def locate_block(i, table, table_lo, seated, edges, own, lo, width, delta_out, basis_out, kinds_out, place_out):
    fan = edges.shape[0]
    spans = [
        table[:, table_lo + p.start : table_lo + p.stop] for p in halves(3 * width)
    ]
    mine = own > 0.5
    home = seated[:, lo : lo + width]
    parts = []
    for part in halves(width):
        rel = edges[:, part].astype(I32)
        live = rel >= 0
        group, place = rel >> 7, rel & (LANES - 1)
        fetch = lambda r: lane_fetch([span[r : r + 1] for span in spans], group, place)
        values = []
        for c in range(3):
            here = home[c : c + 1, part]
            if part.start > 0:
                here = jnp.where(mine, here, home[c : c + 1, :LANES])
            values.append(fetch(c) - here)
        values.append(jnp.where(live, fetch(SPECIES_ROW), -1.0))
        tile = (rel // width).astype(F32) * float(width)
        values.append(jnp.where(live, fetch(SEAT_ROW) + tile, -1.0))
        parts.append(values)
    joined = [jnp.concatenate(list(piece), axis=1) for piece in zip(*parts)]
    for c in range(3):
        delta_out[i, c * fan : (c + 1) * fan, :] = joined[c]
    kinds_out[i] = joined[3]
    place_out[i] = joined[4]
    dist_sq = joined[0] * joined[0] + joined[1] * joined[1] + joined[2] * joined[2]
    count = basis_out.shape[1] // fan
    centres = 2.0 * lax.broadcasted_iota(I32, (count, width), 0).astype(F32)
    rows = []
    for s in range(fan):
        away = jnp.broadcast_to(dist_sq[s : s + 1], (count, width)) - centres
        rows.append(jnp.exp(away * away * -0.125))
    basis_out[i] = jnp.concatenate(rows, axis=0).astype(BF16)


def fill_hidden(target, spread, basis, rows, fan):
    units = spread.shape[0] // fan

    def part(start, used):
        place = pl.ds(start, used)
        target[place, :] = silu_of_half(dot(spread[place, :], basis[...])).astype(BF16)

    if isinstance(rows, int):
        part(0, rows * units)
    else:

        def step(s, carry):
            part(aligned(s * units, units), units)
            return carry

        lax.fori_loop(0, fan, step, 0)


def add_terms(carry, own, s, terms, first):
    total, lent = carry
    if may_spill(s, first):
        lent = lent + jnp.where(own[pl.ds(s, 1), :] > 0.5, 0.0, terms[:, LANES:])
    return total + terms, lent


def no_sums(chans, width):
    return jnp.zeros((chans, width), F32), jnp.zeros((chans, LANES), F32)


def summed_of(carry):
    total, lent = carry
    return jnp.concatenate([total[:, :LANES] + lent, total[:, LANES:] - lent], axis=1)


def update_of(feats, summed, mix_half, fan):
    scaled = (summed * (1.0 / math.sqrt(fan))).astype(BF16)
    return (feats.astype(F32) + silu_of_half(dot(mix_half, scaled))).astype(BF16)


def first_block(rows, kinds, hid, own, seated, lo, width, weights):
    embed_t, first, first_rest, mix_half, spread = weights
    fan = kinds.shape[0]
    units = spread.shape[0] // fan
    species = first.shape[1] // units
    zero = jnp.zeros((), BF16)

    def step(s, carry):
        sums, whole, away = carry
        mine = hid[pl.ds(s * units, units), :]
        kind = jnp.broadcast_to(kinds[pl.ds(s, 1), :].astype(BF16), (units, width))
        sorted_out = [
            jnp.where(kind == jnp.full((), k, BF16), mine, zero) for k in range(species)
        ]
        sorted_out = jnp.concatenate(sorted_out, axis=0)
        whole = whole + sorted_out
        if may_spill(s, spill_from(rows, fan)):
            mine = jnp.broadcast_to(own[pl.ds(s, 1), :].astype(BF16), away.shape)
            away = away + jnp.where(mine > jnp.full((), 0.5, BF16), zero, sorted_out[:, LANES:])
        sums = add_terms(sums, own, s, dot(first[...], sorted_out), spill_from(rows, fan))
        return sums, whole, away

    whole = jnp.zeros((species * units, width), BF16)
    carry = no_sums(mix_half.shape[0], width), whole, whole[:, :LANES]
    (total, lent), whole, away = over_rows(rows, step, carry)
    sums = total + dot(first_rest[...], whole), lent + dot(first_rest[...], away)
    rows_of = lax.broadcasted_iota(I32, (embed_t.shape[1], width), 0).astype(F32)
    same = rows_of == seated[SPECIES_ROW : SPECIES_ROW + 1, lo : lo + width]
    feats = dot(embed_t[...], jnp.where(same, 1.0, 0.0).astype(BF16))
    return update_of(feats, summed_of(sums), mix_half[...], fan)


def turned(matrix):
    size = matrix.shape[1]
    row = lax.broadcasted_iota(I32, (size, size), 0)
    column = lax.broadcasted_iota(I32, (size, size), 1)
    identity = jnp.where(row == column, 1.0, 0.0).astype(BF16)
    return lax.dot_general(
        identity, matrix, (((1,), (1,)), ((), ())), preferred_element_type=F32
    )


def prepare(embed, rad_in, rad_out, mixing, embed_t, first, first_rest, spread, out_t, mix_half):
    layers, count, units = rad_in.shape
    fan = spread.shape[1] // units
    for layer in range(layers):
        half = rad_in[layer].astype(F32) * 0.5
        weight = turned(jnp.concatenate([half] * fan, axis=0).astype(BF16))
        owner = lax.broadcasted_iota(I32, weight.shape, 1) // count
        for s in range(fan):
            only = jnp.where(owner == s, weight, 0.0).astype(BF16)
            spread[layer, s * units : (s + 1) * units, :] = only
        out_t[layer] = turned(rad_out[layer]).astype(BF16)
    for layer in range(mixing.shape[0]):
        mix_half[layer] = (turned(mixing[layer]) * 0.5).astype(BF16)
    out = rad_out[0].astype(F32)
    table = embed[...].astype(F32)
    species = table.shape[0]
    padded = jnp.concatenate(
        [table, jnp.zeros((embed_t.shape[1] - species, table.shape[1]), F32)], axis=0
    )
    embed_t[...] = turned(padded.astype(BF16)).astype(BF16)
    scaled = jnp.concatenate([out * table[k : k + 1] for k in range(species)], axis=0)
    first[...] = turned(scaled.astype(BF16)).astype(BF16)
    rest = scaled - scaled.astype(BF16).astype(F32)
    first_rest[...] = turned(rest.astype(BF16)).astype(BF16)


def seat_tile(width, pk, nbr, table, seated, edges, owns, depth, delta_out, basis_out, kinds_out, place_out, index):
    atoms = pk.shape[1]
    blocks = atoms // width
    index[...] = nbr[...].astype(F32)
    table[...] = pk[...]
    found = [seat_block(pk, index, b * width, width, seated) for b in range(blocks)]
    both = [counts[0] + counts[1] for _, _, counts in found]
    most = functools.reduce(jnp.maximum, both)
    most = jnp.max(most, axis=1, keepdims=True)
    fan = nbr.shape[0]
    limit = jnp.full(most.shape, float(fan), F32)
    for rows in depths(fan)[-2::-1]:
        limit = jnp.where(most <= float(2 * rows), float(rows), limit)
    depth[...] = jnp.broadcast_to(limit, depth.shape)
    for b, (seat, pieces, counts) in enumerate(found):
        table[SEAT_ROW : SEAT_ROW + 1, b * width : (b + 1) * width] = seat
        edges[b], owns[b] = fill_rows(pieces, counts, limit)
    for part in halves(2 * width):
        wanted = jnp.broadcast_to(pk[SEND_ROW : SEND_ROW + 1, part].astype(I32), (PACK_ROWS, LANES))
        seats = lane_lookup([table[SEAT_ROW : SEAT_ROW + 1, p] for p in halves(atoms)], wanted)
        seats = seats + (wanted // width).astype(F32) * float(width)
        table[SEND_ROW : SEND_ROW + 1, part] = seats[:1]

    for i in range(blocks - 2):
        lo = (i + 1) * width
        locate_block(
            i, table, lo - width, seated, edges[i + 1], owns[i + 1], lo, width,
            delta_out, basis_out, kinds_out, place_out,
        )


def first_inner(width, ref_energy, pk, seated, owns, depth, basis, kinds, embed, rad_in, rad_out, mixing, w_in, feats_out, embed_t, first, first_rest, spread, out_t, mix_half, w_row, ref_row, hid):
    prepare(embed, rad_in, rad_out, mixing, embed_t, first, first_rest, spread, out_t, mix_half)
    weights = (embed_t, first, first_rest, mix_half.at[0], spread.at[0])
    w_row[...] = w_in[...]
    kinds_row = pk[SPECIES_ROW : SPECIES_ROW + 1, :]
    energy = jnp.zeros(kinds_row.shape, F32)
    for k in range(ref_energy.shape[1]):
        energy = jnp.where(kinds_row == float(k), ref_energy[0:1, k : k + 1], energy)
    ref_row[...] = energy
    def run(rows):
        for i in range(kinds.shape[0]):
            fill_hidden(hid.at[i], spread.at[0], basis.at[i], rows, kinds.shape[1])
        for i in range(kinds.shape[0]):
            feats_out[:, i * width : (i + 1) * width] = first_block(
                rows, kinds.at[i], hid.at[i], owns.at[i + 1], seated, (i + 1) * width, width, weights
            )

    by_depth(depth, kinds.shape[1], run)


def pack_halo(feats, table, start, width, out):
    atoms = feats.shape[1]
    rows = lax.broadcasted_iota(I32, (width, width), 0).astype(F32).astype(BF16)
    one, zero = jnp.ones((), BF16), jnp.zeros((), BF16)
    wanted = table[SEND_ROW : SEND_ROW + 1, pl.ds(aligned(start, width), width)]
    picks = []
    for k in range(atoms // width):
        place = jnp.clip(wanted - float(k * width), -1.0, float(width)).astype(BF16)
        picks.append(jnp.where(rows == place, one, zero))
    out[...] = dot(feats[...], jnp.concatenate(picks, axis=0)).astype(BF16)


def halo_places(core, atoms, width):
    top = atoms + width
    return aligned((1 - core) * top, width), aligned(core * top, width)


def edge_blocks(blocks, width):
    return [(0, 0, 0), (1, blocks - 1, (blocks - 1) * width)]


def first_outer(width, pk, own_table, seated, mate, cross, edges, owns, depth, embed_t, first, first_rest, spread, mix_half, inner, delta_out, basis_out, place_out, feats_out, to_mate, to_cross, pair_out, table, kinds, hid):
    core = core_index()
    atoms = pk.shape[1]
    blocks = atoms // width
    fan = edges.shape[1]
    weights = (embed_t, first, first_rest, mix_half.at[0], spread.at[0])
    table[:, width : width + atoms] = own_table[...]
    at_mate, at_cross = halo_places(core, atoms, width)
    for ref, start, at in ((mate, core * width, at_mate), (cross, (1 - core) * width, at_cross)):
        spans = [ref[:, part] for part in halves(atoms)]
        for k in range(width // LANES):
            wanted = ref[SEND_ROW : SEND_ROW + 1, pl.ds(aligned(start + k * LANES, LANES), LANES)]
            wanted = jnp.broadcast_to(wanted.astype(I32), (PACK_ROWS, LANES))
            place = pl.ds(aligned(at + k * LANES, LANES), LANES)
            table[:, place] = lane_lookup(spans, wanted)
            lane = lax.broadcasted_iota(I32, (1, LANES), 1) + k * LANES
            table[SEAT_ROW : SEAT_ROW + 1, place] = lane.astype(F32)
    feats_out[:, width : atoms - width] = inner[...]
    pair_out[0:4, :] = pk[0:4, :]
    pair_out[4:8, :] = mate[0:4, :]

    for i, b, lo in edge_blocks(blocks, width):
        locate_block(
            i, table, lo, seated, edges[b], owns[b], lo, width,
            delta_out, basis_out, kinds, place_out,
        )

    def run(rows):
        for i in range(2):
            fill_hidden(hid.at[i], spread.at[0], basis_out.at[i], rows, fan)
        for i, b, lo in edge_blocks(blocks, width):
            feats_out[:, lo : lo + width] = first_block(
                rows, kinds.at[i], hid.at[i], owns.at[b], seated, lo, width, weights
            )

    by_depth(depth, fan, run)
    pack_halo(feats_out, own_table, core * width, width, to_cross)
    pack_halo(feats_out, own_table, (1 - core) * width, width, to_mate)


class Places:
    def __init__(self, place, width, tiles):
        self.place, self.width, self.tiles = place, width, tiles
        self.known = self.rows(place[...])

    def rows(self, place):
        width = float(self.width)
        return [jnp.clip(place - k * width, -1.0, width).astype(BF16) for k in self.tiles]

    def fetch(self, window, s):
        if isinstance(s, int):
            lines = [x[s : s + 1] for x in self.known]
        else:
            lines = self.rows(self.place[pl.ds(s, 1), :])
        rows = lax.broadcasted_iota(I32, (self.width, self.width), 0).astype(F32).astype(BF16)
        one, zero = jnp.ones((), BF16), jnp.zeros((), BF16)
        return dot(window, jnp.concatenate([jnp.where(rows == x, one, zero) for x in lines], axis=0))


def stored(hid, s, units):
    return hid[pl.ds(s * units, units), :]


def layer_inner(width, layer, owns, depth, spreads, outs_t, mixes, feats, basis, place, basis_edge, place_edge, pair, feats_out, field_edge, total_edge, lent_edge, pair_out, hid):
    spread, out_t, mix_half = spreads.at[layer], outs_t[layer], mixes[layer]
    chans, units = out_t.shape
    fan = place.shape[1]
    inner = place.shape[0]
    pair_out[...] = pair[...]

    def run(rows):
        first = spill_from(rows, fan)
        for i in range(inner):
            fill_hidden(hid.at[i], spread, basis.at[i], rows, fan)
        for i in range(2):
            fill_hidden(hid.at[inner + i], spread, basis_edge.at[i], rows, fan)
        for i in range(inner):
            lo = (i + 1) * width
            window = feats[:, lo - width : lo + 2 * width]
            places = Places(place.at[i], width, (0, 1, 2))

            def step(s, carry):
                terms = places.fetch(window, s) * dot(out_t, stored(hid.at[i], s, units))
                return add_terms(carry, owns.at[i + 1], s, terms, first)

            sums = over_rows(rows, step, no_sums(chans, width))
            feats_out[:, lo - width : lo] = update_of(
                feats[:, lo : lo + width], summed_of(sums), mix_half, fan
            )
        for i, b, lo in edge_blocks(inner + 2, width):
            start = max(lo - width, 0)
            window = feats[:, start : start + 2 * width]
            places = Places(place_edge.at[i], width, (0, 1) if i else (1, 2))

            def step(s, carry):
                field = dot(out_t, stored(hid.at[inner + i], s, units))
                field_edge[i, s] = field
                return add_terms(carry, owns.at[b], s, places.fetch(window, s) * field, first)

            total_edge[i], lent_edge[i] = over_rows(rows, step, no_sums(chans, width))

    by_depth(depth, fan, run)


def halo_of(i, core, mate, cross):
    lower_by_mate = core == (0 if i else 1)
    return jnp.where(lower_by_mate, mate[...], cross[...])


def layer_outer(width, layer, own_table, owns, depth, mixes, feats, place, mate, cross, field_edge, total_edge, lent_edge, inner, feats_out, to_mate, to_cross):
    core = core_index()
    atoms = feats.shape[1]
    fan = place.shape[1]
    mix_half = mixes[layer]
    feats_out[:, width : atoms - width] = inner[...]

    def run(rows):
        for i, b, lo in edge_blocks(atoms // width, width):
            halo = halo_of(i, core, mate, cross)
            places = Places(place.at[i], width, (2,) if i else (0,))

            def step(s, carry):
                terms = places.fetch(halo, s) * field_edge[i, s]
                return add_terms(carry, owns.at[b], s, terms, spill_from(rows, fan))

            sums = over_rows(rows, step, (total_edge[i], lent_edge[i]))
            feats_out[:, lo : lo + width] = update_of(
                feats[:, lo : lo + width], summed_of(sums), mix_half, fan
            )

    by_depth(depth, fan, run)
    pack_halo(feats_out, own_table, core * width, width, to_cross)
    pack_halo(feats_out, own_table, (1 - core) * width, width, to_mate)


def near_of(near, own, s, first):
    if not may_spill(s, first):
        return near
    lower = jnp.where(own[pl.ds(s, 1), :] > 0.5, near[:, LANES:], near[:, :LANES])
    return jnp.concatenate([near[:, :LANES], lower], axis=1)


def put_pair(pairs, s, terms):
    pairs[pl.ds(s, 1), :] = jnp.sum(terms, axis=0, keepdims=True)


def force_of(pair, own, delta, seat, chans):
    fan, width = pair.shape
    pair = pair * (1.0 / math.sqrt(chans))
    mine = own[...] > 0.5
    out = []
    for c in range(3):
        terms = pair * delta[c * fan : (c + 1) * fan, :]
        second = terms[:, LANES:]
        lent = jnp.where(mine, 0.0, second)
        out.append(
            jnp.concatenate(
                [
                    jnp.sum(terms[:, :LANES] + lent, axis=0, keepdims=True),
                    jnp.sum(jnp.where(mine, second, 0.0), axis=0, keepdims=True),
                ],
                axis=1,
            )
        )
    seated = jnp.concatenate(out + [jnp.zeros((PACK_ROWS - 3, width), F32)], axis=0)
    spans = [seated[:, part] for part in halves(width)]
    seat = seat.astype(I32)
    return jnp.concatenate(
        [
            lane_lookup(spans, jnp.broadcast_to(seat[:, part], (PACK_ROWS, LANES)))
            for part in halves(width)
        ],
        axis=1,
    )


def head_inner(width, layer, own_table, owns, depth, spreads, outs_t, feats, basis, place, delta, basis_edge, place_edge, force_out, field_edge, pair_edge, hid, pairs):
    spread, out_t = spreads.at[layer], outs_t[layer]
    chans, units = out_t.shape
    fan = place.shape[1]
    inner = place.shape[0]
    pairs[...] = jnp.zeros(pairs.shape, F32)
    pair_edge[...] = jnp.zeros(pair_edge.shape, F32)

    def run(rows):
        first = spill_from(rows, fan)
        for i in range(inner):
            fill_hidden(hid.at[i], spread, basis.at[i], rows, fan)
        for i in range(2):
            fill_hidden(hid.at[inner + i], spread, basis_edge.at[i], rows, fan)
        for i in range(inner):
            lo = (i + 1) * width
            window = feats[:, lo - width : lo + 2 * width]
            near = feats[:, lo : lo + width].astype(F32)
            places = Places(place.at[i], width, (0, 1, 2))

            def step(s, carry):
                field = dot(out_t, stored(hid.at[i], s, units))
                field = field * near_of(near, owns.at[i + 1], s, first)
                put_pair(pairs.at[i], s, places.fetch(window, s) * field)
                return carry

            over_rows(rows, step, 0)
            force_out[:, lo - width : lo] = force_of(
                pairs[i], owns.at[i + 1], delta.at[i],
                own_table[SEAT_ROW : SEAT_ROW + 1, lo : lo + width], chans,
            )
        for i, b, lo in edge_blocks(inner + 2, width):
            start = max(lo - width, 0)
            window = feats[:, start : start + 2 * width]
            near = feats[:, lo : lo + width].astype(F32)
            places = Places(place_edge.at[i], width, (0, 1) if i else (1, 2))

            def step(s, carry):
                field = dot(out_t, stored(hid.at[inner + i], s, units))
                field = field * near_of(near, owns.at[b], s, first)
                field_edge[i, s] = field
                put_pair(pair_edge.at[i], s, places.fetch(window, s) * field)
                return carry

            over_rows(rows, step, 0)

    by_depth(depth, fan, run)


def lane_sum(values):
    total = values[:, :LANES]
    for part in halves(values.shape[1])[1:]:
        total = total + values[:, part]
    return jnp.sum(total, axis=0, keepdims=True)


def head_outer(width, own_table, owns, depth, place, delta, mate, cross, field_edge, pair_edge, inner, force_out, pairs):
    core = core_index()
    chans = mate.shape[0]
    atoms = own_table.shape[1]
    fan = place.shape[1]
    force_out[:, width : atoms - width] = inner[...]
    pairs[...] = jnp.zeros(pairs.shape, F32)

    def run(rows):
        for i, b, lo in edge_blocks(atoms // width, width):
            halo = halo_of(i, core, mate, cross)
            places = Places(place.at[i], width, (2,) if i else (0,))

            def step(s, carry):
                put_pair(pairs.at[i], s, places.fetch(halo, s) * field_edge[i, s])
                return carry

            over_rows(rows, step, 0)
            force_out[:, lo : lo + width] = force_of(
                pair_edge[i] + pairs[i], owns.at[b], delta.at[i],
                own_table[SEAT_ROW : SEAT_ROW + 1, lo : lo + width], chans,
            )

    by_depth(depth, fan, run)


def pass_on(received, _, out):
    out[...] = received[...]


def tail(pk, received, relayed, w_row, ref_row, feats, force_in, band_out, sums_out):
    core = core_index()
    energy = dot(w_row[...], feats[...]) + ref_row[...]
    direct, by_mate = received[0:4, :], relayed[4:8, :]
    direct_ahead = lax.rem(core + lax.axis_index("img"), 2) == 0
    back = pk[0:4, :] - jnp.where(direct_ahead, by_mate, direct)
    fore = jnp.where(direct_ahead, direct, by_mate) - pk[0:4, :]
    band_out[0:4, :] = back
    band_out[4:8, :] = fore
    back, fore, force = back[:3], fore[:3], force_in[0:3, :]
    rows = [energy, back * back, fore * fore, back * fore, force * back, force * fore]
    sums = [lane_sum(row) for row in rows]
    sums.append(jnp.zeros((SUM_ROWS - len(sums), LANES), F32))
    sums_out[...] = jnp.concatenate(sums, axis=0)


def add_sums(mine, other, out):
    out[...] = mine[...] + other[...]


def finish(count, pk, band, force, *rest):
    *parts, result, energy_out = rest
    total = parts[0][...]
    for part in parts[1:]:
        total = total + part[...]
    total = jnp.sum(total, axis=1, keepdims=True)
    energy, back_sq, fore_sq, cross, along_back, along_fore = (total[i : i + 1] for i in range(6))
    back_len = jnp.sqrt(back_sq + 1e-06)
    fore_len = jnp.sqrt(fore_sq + 1e-06)
    by_back, by_fore = 1.0 / back_len, 1.0 / fore_len
    tau_sq = (
        back_sq * by_back * by_back + fore_sq * by_fore * by_fore + 2.0 * cross * by_back * by_fore
    )
    proj = (along_back * by_back + along_fore * by_fore) / tau_sq
    spring = SPRING * (fore_len - back_len) / jnp.sqrt(tau_sq)
    image = lax.axis_index("img")
    is_end = jnp.logical_or(image == 0, image == lax.axis_size("img") - 1)
    factor = jnp.where(pk[CLIMB_ROW : CLIMB_ROW + 1, 0:1] == 1.0, -2.0 * proj, spring - proj)
    tangent = band[0:3, :] * by_back + band[4:7, :] * by_fore
    moved = jnp.where(is_end, force[0:3, :], force[0:3, :] + factor * tangent)
    for c in range(3):
        result[c] = moved[c : c + 1]
    energy_out[...] = energy * (1.0 / count)


def swap_pairs(count, offset):
    pairs = []
    for low in range(offset, count, 2):
        high = (low + 1) % count
        pairs += [(low, high), (high, low)]
    return pairs


def image_pairs(images, tiles):
    pairs = []
    for tile in range(tiles):
        pairs += [(a * tiles + tile, b * tiles + tile) for a, b in swap_pairs(images, tile % 2)]
    return pairs


def on_device(positions, species, counts, neighbours, send_list, climb, embed, ref_energy, rad_in, rad_out, mixing, w_energy):
    atoms = species.shape[0]
    width = send_list.shape[0] // 2
    fan = neighbours.shape[0]
    chans = embed.shape[1]
    layers = mixing.shape[0]
    basis_count, units = rad_in.shape[1:]
    blocks = atoms // width
    inner_atoms = (blocks - 2) * width
    tiles = lax.axis_size("atom")
    images = lax.axis_size("img")
    def call(body, operands, outs, scratch=(), flops=0):
        return pl.pallas_call(
            body,
            out_shape=[jax.ShapeDtypeStruct(shape, dtype) for shape, dtype in outs],
            in_specs=[VMEM] * len(operands),
            out_specs=[VMEM] * len(outs),
            scratch_shapes=[pltpu.VMEM(*x) for x in scratch],
            cost_estimate=pl.CostEstimate(flops=flops, bytes_accessed=2**20, transcendentals=0),
            compiler_params=pltpu.CompilerParams(vmem_limit_bytes=16 * 2**20),
        )(*operands)

    def swap(block, offset):
        return lax.ppermute(block, "atom", swap_pairs(tiles, offset))

    pack_type = ((PACK_ROWS, atoms), F32)
    feats_type = ((chans, atoms), BF16)
    halo_type = ((chans, width), BF16)
    hid_type = ((2, fan * units, width), BF16)
    hid_scratch = ((blocks - 2, fan * units, width), BF16)

    def block_outs(count):
        return [
            ((count, 3 * fan, width), F32),
            ((count, fan * basis_count, width), BF16),
            ((count, fan, width), F32),
        ]

    row = lax.broadcasted_iota(I32, (PACK_ROWS, atoms), 0)
    sends = jnp.pad(send_list, (0, atoms - 2 * width))
    (pk,) = call(blank, (), [pack_type], flops=2**33)
    lines = [positions[0, c] for c in range(3)] + [species, counts, sends, climb]
    for place, line in zip((0, 1, 2, SPECIES_ROW, COUNT_ROW, SEND_ROW, CLIMB_ROW), lines):
        pk = jnp.where(row == place, lax.broadcast_in_dim(line, pk.shape, (1,)).astype(F32), pk)
    mate = swap(pk, 0)
    cross = swap(pk, 1)
    kinds_type = ((blocks - 2, fan, width), F32)
    own_table, seated, edges, owns, depth, delta_in, basis_in, kinds_in, place_in = call(
        functools.partial(seat_tile, width),
        (pk, neighbours),
        [
            pack_type,
            pack_type,
            ((blocks, fan, width), F32),
            ((blocks, fan, LANES), F32),
            ((PACK_ROWS, LANES), F32),
        ]
        + block_outs(blocks - 2)[:2]
        + [kinds_type, kinds_type],
        [((fan, atoms), F32)],
        flops=2**32,
    )
    inner, embed_t, first, first_rest, spread, out_t, mix_half, w_row, ref_row = call(
        functools.partial(first_inner, width),
        (ref_energy[None], pk, seated, owns, depth, basis_in, kinds_in, embed, rad_in, rad_out, mixing, w_energy[None]),
        [
            ((chans, inner_atoms), BF16),
            ((chans, -(-embed.shape[0] // 16) * 16), BF16),
            ((chans, embed.shape[0] * units), BF16),
            ((chans, embed.shape[0] * units), BF16),
            ((layers + 1, fan * units, fan * basis_count), BF16),
            ((layers + 1, chans, units), BF16),
            ((layers, chans, chans), BF16),
            ((1, chans), BF16),
            ((1, atoms), F32),
        ],
        [hid_scratch],
        flops=2**32,
    )
    delta_out, basis_out, place_out, feats, to_mate, to_cross, pair = call(
        functools.partial(first_outer, width),
        (pk, own_table, seated, mate, cross, edges, owns, depth, embed_t, first, first_rest, spread, mix_half, inner),
        block_outs(2) + [feats_type, halo_type, halo_type, pack_type],
        [((PACK_ROWS, atoms + 2 * width), F32), ((2, fan, width), F32), hid_type],
    )
    for layer in range(1, layers):
        cross = swap(to_cross, 1)
        mate = swap(to_mate, 0)
        inner, field_edge, total_edge, lent_edge, pair = call(
            functools.partial(layer_inner, width, layer),
            (owns, depth, spread, out_t, mix_half, feats, basis_in, place_in, basis_out, place_out, pair),
            [
                ((chans, inner_atoms), BF16),
                ((2, fan, chans, width), F32),
                ((2, chans, width), F32),
                ((2, chans, LANES), F32),
                pack_type,
            ],
            [((blocks, fan * units, width), BF16)],
            flops=2**32,
        )
        feats, to_mate, to_cross = call(
            functools.partial(layer_outer, width, layer),
            (own_table, owns, depth, mix_half, feats, place_out, mate, cross, field_edge, total_edge, lent_edge, inner),
            [feats_type, halo_type, halo_type],
        )
    received = lax.ppermute(pair, ("img", "atom"), image_pairs(images, tiles))
    cross = swap(to_cross, 1)
    mate = swap(to_mate, 0)
    inner, field_edge, pair_edge = call(
        functools.partial(head_inner, width, layers),
        (own_table, owns, depth, spread, out_t, feats, basis_in, place_in, delta_in, basis_out, place_out),
        [((PACK_ROWS, inner_atoms), F32), ((2, fan, chans, width), F32), ((2, fan, width), F32)],
        [((blocks, fan * units, width), BF16), ((blocks - 2, fan, width), F32)],
        flops=2**32,
    )
    (late,) = call(pass_on, (received, inner), [pack_type])
    relayed = swap(late, 0)
    (force,) = call(
        functools.partial(head_outer, width),
        (own_table, owns, depth, place_out, delta_out, mate, cross, field_edge, pair_edge, inner),
        [pack_type],
        [((2, fan, width), F32)],
        flops=2**32,
    )
    band, sums = call(
        tail,
        (pk, received, relayed, w_row, ref_row, feats, force),
        [pack_type, ((SUM_ROWS, LANES), F32)],
    )
    step = 2 * REDUCE_CHIPS
    while step < tiles:
        sums = sums + lax.ppermute(sums, "atom", [(i, i ^ step) for i in range(tiles)])
        step *= 2
    (both,) = call(add_sums, (sums, swap(sums, 0)), [((SUM_ROWS, LANES), F32)])
    near = lax.ppermute(both, "atom", [(i, i ^ 2 if i % 2 == 0 else i ^ 6) for i in range(tiles)])
    far = lax.ppermute(both, "atom", [(i, i ^ 4) for i in range(tiles)])
    other = swap(near, 0)
    result, energy = call(
        functools.partial(finish, atoms * tiles),
        (pk, band, force, both, near, far, other),
        [((3, 1, atoms), F32), ((1, 1), F32)],
    )
    return jnp.transpose(result, (1, 0, 2)), energy.reshape(1)


def solution(mesh):
    return jax.shard_map(
        on_device,
        mesh=mesh,
        in_specs=(
            P("img", None, "atom"),
            P("atom"),
            P("atom"),
            P(None, "atom"),
            P("atom"),
            P("img"),
            P(),
            P(),
            P(),
            P(),
            P(),
            P(),
        ),
        out_specs=(P("img", None, "atom"), P("img")),
        check_vma=False,
    )
```

```python
import functools
import math

import jax
import jax.numpy as jnp
from jax import lax
from jax.experimental import pallas as pl
from jax.experimental.pallas import tpu as pltpu
from jax.sharding import PartitionSpec as P

F32 = jnp.float32
BF16 = jnp.bfloat16
I32 = jnp.int32
LANES = 128
SPRING = 5.0
SPECIES_ROW = 3
COUNT_ROW = 4
SEND_ROW = 5
SEAT_ROW = 6
CLIMB_ROW = 7
PACK_ROWS = 8
SUM_ROWS = 8
REDUCE_CHIPS = 4
VMEM = pl.BlockSpec(memory_space=pltpu.VMEM)


def core_index():
    return lax.rem(lax.axis_index("atom"), 2)


def dot(a, b):
    return jnp.dot(a, b, preferred_element_type=F32)


def silu_of_half(half):
    return half + half * jnp.tanh(half)


def aligned(start, step):
    return pl.multiple_of(start, step)


def halves(width):
    return [slice(k * LANES, (k + 1) * LANES) for k in range(width // LANES)]


def depths(fan):
    short = -(-5 * fan // 8)
    return [short, short + 1, short + 2, fan]


def lane_fetch(windows, group, place):
    found = jnp.zeros(place.shape, F32)
    for k, window in enumerate(windows):
        rows = jnp.broadcast_to(window, place.shape)
        picked = jnp.take_along_axis(rows, place, axis=1, mode="promise_in_bounds")
        found = jnp.where(group == k, picked, found)
    return found


def lane_lookup(windows, index):
    return lane_fetch(windows, index // LANES, index & (LANES - 1))


def blank(out):
    out[...] = jnp.zeros(out.shape, F32)


def seat_atoms(pk, lo, width, most):
    counts = pk[COUNT_ROW : COUNT_ROW + 1, lo : lo + width]
    value = lax.broadcasted_iota(I32, (most, width), 0).astype(F32) + 1.0
    same = counts == value
    row = lax.broadcasted_iota(I32, (width, width), 0)
    lane = lax.broadcasted_iota(I32, (width, width), 1)
    earlier = dot(jnp.where(same, 1.0, 0.0).astype(BF16), jnp.where(row < lane, 1.0, 0.0).astype(BF16))
    larger = jnp.sum(jnp.where(counts > value, 1.0, 0.0), axis=1, keepdims=True)
    rank = jnp.sum(jnp.where(same, earlier + larger, 0.0), axis=0, keepdims=True)
    seat = jnp.where(rank < width // 2, rank, 1.5 * width - 1.0 - rank)
    taken = jnp.where(row.astype(F32) == seat, 1.0, 0.0).astype(BF16)
    atoms = lax.broadcasted_iota(I32, (PACK_ROWS, width), 1).astype(F32).astype(BF16)
    taker = lax.dot_general(
        atoms, taken, (((1,), (1,)), ((), ())), preferred_element_type=F32
    )
    return seat, taker[:1]


def seat_block(pk, nbr, lo, width, seated):
    fan = nbr.shape[0]
    seat, taker = seat_atoms(pk, lo, width, fan)
    pieces, tables = [], []
    for part in halves(width):
        who = taker[:, part].astype(I32)
        spans = [nbr[:, lo + p.start : lo + p.stop] for p in halves(width)]
        pieces.append(lane_lookup(spans, jnp.broadcast_to(who, (fan, LANES))) - float(lo))
        spans = [pk[:, lo + p.start : lo + p.stop] for p in halves(width)]
        tables.append(lane_lookup(spans, jnp.broadcast_to(who, (PACK_ROWS, LANES))))
    seated[:, lo : lo + width] = jnp.concatenate(tables, axis=1)
    return seat, pieces, [x[COUNT_ROW : COUNT_ROW + 1] for x in tables]


def fill_rows(pieces, counts, limit):
    first, second = pieces
    fan = first.shape[0]
    row = lax.broadcasted_iota(I32, (fan, LANES), 0).astype(F32)
    mine = row < counts[1]
    spilled, over = jnp.zeros((fan, LANES), F32), first
    for rows in depths(fan)[:-1]:
        slots = [2 * rows - 1 - r if 0 <= 2 * rows - 1 - r < fan else 0 for r in range(fan)]
        here = jnp.logical_and(limit == float(rows), 2.0 * rows - 1.0 - row < counts[0])
        here = jnp.logical_and(here, row < float(rows))
        here = jnp.logical_and(here, row >= float(2 * rows - fan))
        here = jnp.logical_and(here, jnp.logical_not(mine))
        over = jnp.where(here, jnp.concatenate([first[r : r + 1] for r in slots], axis=0), over)
        spilled = jnp.where(here, 1.0, spilled)
    spilled = spilled > 0.5
    first = jnp.where(row < jnp.minimum(counts[0], limit), first, -1.0)
    second = jnp.where(mine, second, jnp.where(spilled, over, -1.0))
    return jnp.concatenate([first, second], axis=1), jnp.where(spilled, 0.0, 1.0)


def by_depth(depth, fan, run):
    limit = jnp.max(depth[...])
    short = depths(fan)[0]

    @pl.when(limit < short + 0.5)
    def _():
        run(short)

    @pl.when(limit > short + 0.5)
    def _():
        run(limit.astype(I32))


def over_rows(rows, step, carry):
    if isinstance(rows, int):
        for s in range(rows):
            carry = step(s, carry)
        return carry
    return lax.fori_loop(0, rows, step, carry)


def spill_from(rows, fan):
    return 2 * rows - fan if isinstance(rows, int) else 0


def may_spill(s, first):
    return not isinstance(s, int) or s >= first


def locate_block(i, table, table_lo, seated, edges, own, lo, width, delta_out, basis_out, kinds_out, place_out):
    fan = edges.shape[0]
    spans = [
        table[:, table_lo + p.start : table_lo + p.stop] for p in halves(3 * width)
    ]
    mine = own > 0.5
    home = seated[:, lo : lo + width]
    parts = []
    for part in halves(width):
        rel = edges[:, part].astype(I32)
        live = rel >= 0
        group, place = rel >> 7, rel & (LANES - 1)
        fetch = lambda r: lane_fetch([span[r : r + 1] for span in spans], group, place)
        values = []
        for c in range(3):
            here = home[c : c + 1, part]
            if part.start > 0:
                here = jnp.where(mine, here, home[c : c + 1, :LANES])
            values.append(fetch(c) - here)
        values.append(jnp.where(live, fetch(SPECIES_ROW), -1.0))
        tile = (rel // width).astype(F32) * float(width)
        values.append(jnp.where(live, fetch(SEAT_ROW) + tile, -1.0))
        parts.append(values)
    joined = [jnp.concatenate(list(piece), axis=1) for piece in zip(*parts)]
    for c in range(3):
        delta_out[i, c * fan : (c + 1) * fan, :] = joined[c]
    kinds_out[i] = joined[3]
    place_out[i] = joined[4]
    dist_sq = joined[0] * joined[0] + joined[1] * joined[1] + joined[2] * joined[2]
    count = basis_out.shape[1] // fan
    centres = 2.0 * lax.broadcasted_iota(I32, (count, width), 0).astype(F32)
    rows = []
    for s in range(fan):
        away = jnp.broadcast_to(dist_sq[s : s + 1], (count, width)) - centres
        rows.append(jnp.exp(away * away * -0.125))
    basis_out[i] = jnp.concatenate(rows, axis=0).astype(BF16)


def fill_hidden(target, spread, basis, rows, fan):
    units = spread.shape[0] // fan

    def part(start, used):
        place = pl.ds(start, used)
        target[place, :] = silu_of_half(dot(spread[place, :], basis[...])).astype(BF16)

    if isinstance(rows, int):
        part(0, rows * units)
    else:

        def step(s, carry):
            part(aligned(s * units, units), units)
            return carry

        lax.fori_loop(0, fan, step, 0)


def add_terms(carry, own, s, terms, first):
    total, lent = carry
    if may_spill(s, first):
        lent = lent + jnp.where(own[pl.ds(s, 1), :] > 0.5, 0.0, terms[:, LANES:])
    return total + terms, lent


def no_sums(chans, width):
    return jnp.zeros((chans, width), F32), jnp.zeros((chans, LANES), F32)


def summed_of(carry):
    total, lent = carry
    return jnp.concatenate([total[:, :LANES] + lent, total[:, LANES:] - lent], axis=1)


def update_of(feats, summed, mix_half, fan):
    scaled = (summed * (1.0 / math.sqrt(fan))).astype(BF16)
    return (feats.astype(F32) + silu_of_half(dot(mix_half, scaled))).astype(BF16)


def first_block(rows, kinds, hid, own, seated, lo, width, weights):
    embed_t, first, first_rest, mix_half, spread = weights
    fan = kinds.shape[0]
    units = spread.shape[0] // fan
    species = first.shape[1] // units
    zero = jnp.zeros((), BF16)

    def step(s, carry):
        sums, whole, away = carry
        mine = hid[pl.ds(s * units, units), :]
        kind = jnp.broadcast_to(kinds[pl.ds(s, 1), :].astype(BF16), (units, width))
        sorted_out = [
            jnp.where(kind == jnp.full((), k, BF16), mine, zero) for k in range(species)
        ]
        sorted_out = jnp.concatenate(sorted_out, axis=0)
        whole = whole + sorted_out
        if may_spill(s, spill_from(rows, fan)):
            mine = jnp.broadcast_to(own[pl.ds(s, 1), :].astype(BF16), away.shape)
            away = away + jnp.where(mine > jnp.full((), 0.5, BF16), zero, sorted_out[:, LANES:])
        sums = add_terms(sums, own, s, dot(first[...], sorted_out), spill_from(rows, fan))
        return sums, whole, away

    whole = jnp.zeros((species * units, width), BF16)
    carry = no_sums(mix_half.shape[0], width), whole, whole[:, :LANES]
    (total, lent), whole, away = over_rows(rows, step, carry)
    sums = total + dot(first_rest[...], whole), lent + dot(first_rest[...], away)
    rows_of = lax.broadcasted_iota(I32, (embed_t.shape[1], width), 0).astype(F32)
    same = rows_of == seated[SPECIES_ROW : SPECIES_ROW + 1, lo : lo + width]
    feats = dot(embed_t[...], jnp.where(same, 1.0, 0.0).astype(BF16))
    return update_of(feats, summed_of(sums), mix_half[...], fan)


def turned(matrix):
    size = matrix.shape[1]
    row = lax.broadcasted_iota(I32, (size, size), 0)
    column = lax.broadcasted_iota(I32, (size, size), 1)
    identity = jnp.where(row == column, 1.0, 0.0).astype(BF16)
    return lax.dot_general(
        identity, matrix, (((1,), (1,)), ((), ())), preferred_element_type=F32
    )


def prepare(embed, rad_in, rad_out, mixing, embed_t, first, first_rest, spread, out_t, mix_half):
    layers, count, units = rad_in.shape
    fan = spread.shape[1] // units
    for layer in range(layers):
        half = rad_in[layer].astype(F32) * 0.5
        weight = turned(jnp.concatenate([half] * fan, axis=0).astype(BF16))
        owner = lax.broadcasted_iota(I32, weight.shape, 1) // count
        for s in range(fan):
            only = jnp.where(owner == s, weight, 0.0).astype(BF16)
            spread[layer, s * units : (s + 1) * units, :] = only
        out_t[layer] = turned(rad_out[layer]).astype(BF16)
    for layer in range(mixing.shape[0]):
        mix_half[layer] = (turned(mixing[layer]) * 0.5).astype(BF16)
    out = rad_out[0].astype(F32)
    table = embed[...].astype(F32)
    species = table.shape[0]
    padded = jnp.concatenate(
        [table, jnp.zeros((embed_t.shape[1] - species, table.shape[1]), F32)], axis=0
    )
    embed_t[...] = turned(padded.astype(BF16)).astype(BF16)
    scaled = jnp.concatenate([out * table[k : k + 1] for k in range(species)], axis=0)
    first[...] = turned(scaled.astype(BF16)).astype(BF16)
    rest = scaled - scaled.astype(BF16).astype(F32)
    first_rest[...] = turned(rest.astype(BF16)).astype(BF16)


def seat_tile(width, pk, nbr, table, seated, edges, owns, depth, delta_out, basis_out, kinds_out, place_out, index):
    atoms = pk.shape[1]
    blocks = atoms // width
    index[...] = nbr[...].astype(F32)
    table[...] = pk[...]
    found = [seat_block(pk, index, b * width, width, seated) for b in range(blocks)]
    both = [counts[0] + counts[1] for _, _, counts in found]
    most = functools.reduce(jnp.maximum, both)
    most = jnp.max(most, axis=1, keepdims=True)
    fan = nbr.shape[0]
    limit = jnp.full(most.shape, float(fan), F32)
    for rows in depths(fan)[-2::-1]:
        limit = jnp.where(most <= float(2 * rows), float(rows), limit)
    depth[...] = jnp.broadcast_to(limit, depth.shape)
    for b, (seat, pieces, counts) in enumerate(found):
        table[SEAT_ROW : SEAT_ROW + 1, b * width : (b + 1) * width] = seat
        edges[b], owns[b] = fill_rows(pieces, counts, limit)
    for part in halves(2 * width):
        wanted = jnp.broadcast_to(pk[SEND_ROW : SEND_ROW + 1, part].astype(I32), (PACK_ROWS, LANES))
        seats = lane_lookup([table[SEAT_ROW : SEAT_ROW + 1, p] for p in halves(atoms)], wanted)
        seats = seats + (wanted // width).astype(F32) * float(width)
        table[SEND_ROW : SEND_ROW + 1, part] = seats[:1]

    for i in range(blocks - 2):
        lo = (i + 1) * width
        locate_block(
            i, table, lo - width, seated, edges[i + 1], owns[i + 1], lo, width,
            delta_out, basis_out, kinds_out, place_out,
        )


def first_inner(width, ref_energy, pk, seated, owns, depth, basis, kinds, embed, rad_in, rad_out, mixing, w_in, feats_out, embed_t, first, first_rest, spread, out_t, mix_half, w_row, ref_row, hid):
    prepare(embed, rad_in, rad_out, mixing, embed_t, first, first_rest, spread, out_t, mix_half)
    weights = (embed_t, first, first_rest, mix_half.at[0], spread.at[0])
    w_row[...] = w_in[...]
    kinds_row = pk[SPECIES_ROW : SPECIES_ROW + 1, :]
    energy = jnp.zeros(kinds_row.shape, F32)
    for k in range(ref_energy.shape[1]):
        energy = jnp.where(kinds_row == float(k), ref_energy[0:1, k : k + 1], energy)
    ref_row[...] = energy
    def run(rows):
        for i in range(kinds.shape[0]):
            fill_hidden(hid.at[i], spread.at[0], basis.at[i], rows, kinds.shape[1])
        for i in range(kinds.shape[0]):
            feats_out[:, i * width : (i + 1) * width] = first_block(
                rows, kinds.at[i], hid.at[i], owns.at[i + 1], seated, (i + 1) * width, width, weights
            )

    by_depth(depth, kinds.shape[1], run)


def pack_halo(feats, table, start, width, out):
    atoms = feats.shape[1]
    rows = lax.broadcasted_iota(I32, (width, width), 0).astype(F32).astype(BF16)
    one, zero = jnp.ones((), BF16), jnp.zeros((), BF16)
    wanted = table[SEND_ROW : SEND_ROW + 1, pl.ds(aligned(start, width), width)]
    picks = []
    for k in range(atoms // width):
        place = jnp.clip(wanted - float(k * width), -1.0, float(width)).astype(BF16)
        picks.append(jnp.where(rows == place, one, zero))
    out[...] = dot(feats[...], jnp.concatenate(picks, axis=0)).astype(BF16)


def halo_places(core, atoms, width):
    top = atoms + width
    return aligned((1 - core) * top, width), aligned(core * top, width)


def edge_blocks(blocks, width):
    return [(0, 0, 0), (1, blocks - 1, (blocks - 1) * width)]


def first_outer(width, pk, own_table, seated, mate, cross, edges, owns, depth, embed_t, first, first_rest, spread, mix_half, inner, delta_out, basis_out, place_out, feats_out, to_cross, pair_out, table, kinds, hid):
    core = core_index()
    atoms = pk.shape[1]
    blocks = atoms // width
    fan = edges.shape[1]
    weights = (embed_t, first, first_rest, mix_half.at[0], spread.at[0])
    table[:, width : width + atoms] = own_table[...]
    at_mate, at_cross = halo_places(core, atoms, width)
    for ref, start, at in ((mate, core * width, at_mate), (cross, (1 - core) * width, at_cross)):
        spans = [ref[:, part] for part in halves(atoms)]
        for k in range(width // LANES):
            wanted = ref[SEND_ROW : SEND_ROW + 1, pl.ds(aligned(start + k * LANES, LANES), LANES)]
            wanted = jnp.broadcast_to(wanted.astype(I32), (PACK_ROWS, LANES))
            place = pl.ds(aligned(at + k * LANES, LANES), LANES)
            table[:, place] = lane_lookup(spans, wanted)
            lane = lax.broadcasted_iota(I32, (1, LANES), 1) + k * LANES
            table[SEAT_ROW : SEAT_ROW + 1, place] = lane.astype(F32)
    feats_out[:, width : atoms - width] = inner[...]
    pair_out[0:4, :] = pk[0:4, :]
    pair_out[4:8, :] = mate[0:4, :]

    for i, b, lo in edge_blocks(blocks, width):
        locate_block(
            i, table, lo, seated, edges[b], owns[b], lo, width,
            delta_out, basis_out, kinds, place_out,
        )

    def run(rows):
        for i in range(2):
            fill_hidden(hid.at[i], spread.at[0], basis_out.at[i], rows, fan)
        for i, b, lo in edge_blocks(blocks, width):
            feats_out[:, lo : lo + width] = first_block(
                rows, kinds.at[i], hid.at[i], owns.at[b], seated, lo, width, weights
            )

    by_depth(depth, fan, run)
    pack_halo(feats_out, own_table, core * width, width, to_cross)


class Places:
    def __init__(self, place, width, tiles):
        self.place, self.width, self.tiles = place, width, tiles
        self.known = self.rows(place[...])

    def rows(self, place):
        width = float(self.width)
        return [jnp.clip(place - k * width, -1.0, width).astype(BF16) for k in self.tiles]

    def fetch(self, window, s):
        if isinstance(s, int):
            lines = [x[s : s + 1] for x in self.known]
        else:
            lines = self.rows(self.place[pl.ds(s, 1), :])
        rows = lax.broadcasted_iota(I32, (self.width, self.width), 0).astype(F32).astype(BF16)
        one, zero = jnp.ones((), BF16), jnp.zeros((), BF16)
        return dot(window, jnp.concatenate([jnp.where(rows == x, one, zero) for x in lines], axis=0))


def stored(hid, s, units):
    return hid[pl.ds(s * units, units), :]


def layer_inner(width, layer, owns, depth, spreads, outs_t, mixes, feats, basis, place, basis_edge, place_edge, pair, own_table, feats_out, field_edge, total_edge, lent_edge, pair_out, to_mate, hid):
    spread, out_t, mix_half = spreads.at[layer], outs_t[layer], mixes[layer]
    chans, units = out_t.shape
    fan = place.shape[1]
    inner = place.shape[0]
    pair_out[...] = pair[...]
    pack_halo(feats, own_table, (1 - core_index()) * width, width, to_mate)

    def run(rows):
        first = spill_from(rows, fan)
        for i in range(inner):
            fill_hidden(hid.at[i], spread, basis.at[i], rows, fan)
        for i in range(2):
            fill_hidden(hid.at[inner + i], spread, basis_edge.at[i], rows, fan)
        for i in range(inner):
            lo = (i + 1) * width
            window = feats[:, lo - width : lo + 2 * width]
            places = Places(place.at[i], width, (0, 1, 2))

            def step(s, carry):
                terms = places.fetch(window, s) * dot(out_t, stored(hid.at[i], s, units))
                return add_terms(carry, owns.at[i + 1], s, terms, first)

            sums = over_rows(rows, step, no_sums(chans, width))
            feats_out[:, lo - width : lo] = update_of(
                feats[:, lo : lo + width], summed_of(sums), mix_half, fan
            )
        for i, b, lo in edge_blocks(inner + 2, width):
            start = max(lo - width, 0)
            window = feats[:, start : start + 2 * width]
            places = Places(place_edge.at[i], width, (0, 1) if i else (1, 2))

            def step(s, carry):
                field = dot(out_t, stored(hid.at[inner + i], s, units))
                field_edge[i, s] = field
                return add_terms(carry, owns.at[b], s, places.fetch(window, s) * field, first)

            total_edge[i], lent_edge[i] = over_rows(rows, step, no_sums(chans, width))

    by_depth(depth, fan, run)


def halo_of(i, core, mate, cross):
    lower_by_mate = core == (0 if i else 1)
    return jnp.where(lower_by_mate, mate[...], cross[...])


def layer_outer(width, layer, own_table, owns, depth, mixes, feats, place, mate, cross, field_edge, total_edge, lent_edge, inner, feats_out, to_mate, to_cross):
    core = core_index()
    atoms = feats.shape[1]
    fan = place.shape[1]
    mix_half = mixes[layer]
    feats_out[:, width : atoms - width] = inner[...]

    def run(rows):
        for i, b, lo in edge_blocks(atoms // width, width):
            halo = halo_of(i, core, mate, cross)
            places = Places(place.at[i], width, (2,) if i else (0,))

            def step(s, carry):
                terms = places.fetch(halo, s) * field_edge[i, s]
                return add_terms(carry, owns.at[b], s, terms, spill_from(rows, fan))

            sums = over_rows(rows, step, (total_edge[i], lent_edge[i]))
            feats_out[:, lo : lo + width] = update_of(
                feats[:, lo : lo + width], summed_of(sums), mix_half, fan
            )

    by_depth(depth, fan, run)
    pack_halo(feats_out, own_table, core * width, width, to_cross)
    pack_halo(feats_out, own_table, (1 - core) * width, width, to_mate)


def near_of(near, own, s, first):
    if not may_spill(s, first):
        return near
    lower = jnp.where(own[pl.ds(s, 1), :] > 0.5, near[:, LANES:], near[:, :LANES])
    return jnp.concatenate([near[:, :LANES], lower], axis=1)


def put_pair(pairs, s, terms):
    pairs[pl.ds(s, 1), :] = jnp.sum(terms, axis=0, keepdims=True)


def force_of(pair, own, delta, seat, chans):
    fan, width = pair.shape
    pair = pair * (1.0 / math.sqrt(chans))
    mine = own[...] > 0.5
    out = []
    for c in range(3):
        terms = pair * delta[c * fan : (c + 1) * fan, :]
        second = terms[:, LANES:]
        lent = jnp.where(mine, 0.0, second)
        out.append(
            jnp.concatenate(
                [
                    jnp.sum(terms[:, :LANES] + lent, axis=0, keepdims=True),
                    jnp.sum(jnp.where(mine, second, 0.0), axis=0, keepdims=True),
                ],
                axis=1,
            )
        )
    seated = jnp.concatenate(out + [jnp.zeros((PACK_ROWS - 3, width), F32)], axis=0)
    spans = [seated[:, part] for part in halves(width)]
    seat = seat.astype(I32)
    return jnp.concatenate(
        [
            lane_lookup(spans, jnp.broadcast_to(seat[:, part], (PACK_ROWS, LANES)))
            for part in halves(width)
        ],
        axis=1,
    )


def head_inner(width, layer, own_table, owns, depth, spreads, outs_t, feats, basis, place, delta, basis_edge, place_edge, force_out, field_edge, pair_edge, hid, pairs):
    spread, out_t = spreads.at[layer], outs_t[layer]
    chans, units = out_t.shape
    fan = place.shape[1]
    inner = place.shape[0]
    pairs[...] = jnp.zeros(pairs.shape, F32)
    pair_edge[...] = jnp.zeros(pair_edge.shape, F32)

    def run(rows):
        first = spill_from(rows, fan)
        for i in range(inner):
            fill_hidden(hid.at[i], spread, basis.at[i], rows, fan)
        for i in range(2):
            fill_hidden(hid.at[inner + i], spread, basis_edge.at[i], rows, fan)
        for i in range(inner):
            lo = (i + 1) * width
            window = feats[:, lo - width : lo + 2 * width]
            near = feats[:, lo : lo + width].astype(F32)
            places = Places(place.at[i], width, (0, 1, 2))

            def step(s, carry):
                field = dot(out_t, stored(hid.at[i], s, units))
                field = field * near_of(near, owns.at[i + 1], s, first)
                put_pair(pairs.at[i], s, places.fetch(window, s) * field)
                return carry

            over_rows(rows, step, 0)
            force_out[:, lo - width : lo] = force_of(
                pairs[i], owns.at[i + 1], delta.at[i],
                own_table[SEAT_ROW : SEAT_ROW + 1, lo : lo + width], chans,
            )
        for i, b, lo in edge_blocks(inner + 2, width):
            start = max(lo - width, 0)
            window = feats[:, start : start + 2 * width]
            near = feats[:, lo : lo + width].astype(F32)
            places = Places(place_edge.at[i], width, (0, 1) if i else (1, 2))

            def step(s, carry):
                field = dot(out_t, stored(hid.at[inner + i], s, units))
                field = field * near_of(near, owns.at[b], s, first)
                field_edge[i, s] = field
                put_pair(pair_edge.at[i], s, places.fetch(window, s) * field)
                return carry

            over_rows(rows, step, 0)

    by_depth(depth, fan, run)


def lane_sum(values):
    total = values[:, :LANES]
    for part in halves(values.shape[1])[1:]:
        total = total + values[:, part]
    return jnp.sum(total, axis=0, keepdims=True)


def head_outer(width, own_table, owns, depth, place, delta, cross, mate, field_edge, pair_edge, inner, force_out, pairs):
    core = core_index()
    chans = mate.shape[0]
    atoms = own_table.shape[1]
    fan = place.shape[1]
    force_out[:, width : atoms - width] = inner[...]
    pairs[...] = jnp.zeros(pairs.shape, F32)

    def run(rows):
        for i, b, lo in edge_blocks(atoms // width, width):
            halo = halo_of(i, core, mate, cross)
            places = Places(place.at[i], width, (2,) if i else (0,))

            def step(s, carry):
                put_pair(pairs.at[i], s, places.fetch(halo, s) * field_edge[i, s])
                return carry

            over_rows(rows, step, 0)
            force_out[:, lo : lo + width] = force_of(
                pair_edge[i] + pairs[i], owns.at[b], delta.at[i],
                own_table[SEAT_ROW : SEAT_ROW + 1, lo : lo + width], chans,
            )

    by_depth(depth, fan, run)


def pass_on(received, _, out):
    out[...] = received[...]


def tail(pk, received, relayed, w_row, ref_row, feats, force_in, band_out, sums_out):
    core = core_index()
    energy = dot(w_row[...], feats[...]) + ref_row[...]
    direct, by_mate = received[0:4, :], relayed[4:8, :]
    direct_ahead = lax.rem(core + lax.axis_index("img"), 2) == 0
    back = pk[0:4, :] - jnp.where(direct_ahead, by_mate, direct)
    fore = jnp.where(direct_ahead, direct, by_mate) - pk[0:4, :]
    band_out[0:4, :] = back
    band_out[4:8, :] = fore
    back, fore, force = back[:3], fore[:3], force_in[0:3, :]
    rows = [energy, back * back, fore * fore, back * fore, force * back, force * fore]
    sums = [lane_sum(row) for row in rows]
    sums.append(jnp.zeros((SUM_ROWS - len(sums), LANES), F32))
    sums_out[...] = jnp.concatenate(sums, axis=0)


def add_sums(mine, other, out):
    out[...] = mine[...] + other[...]


def finish(count, pk, band, force, *rest):
    *parts, result, energy_out = rest
    total = parts[0][...]
    for part in parts[1:]:
        total = total + part[...]
    total = jnp.sum(total, axis=1, keepdims=True)
    energy, back_sq, fore_sq, cross, along_back, along_fore = (total[i : i + 1] for i in range(6))
    back_len = jnp.sqrt(back_sq + 1e-06)
    fore_len = jnp.sqrt(fore_sq + 1e-06)
    by_back, by_fore = 1.0 / back_len, 1.0 / fore_len
    tau_sq = (
        back_sq * by_back * by_back + fore_sq * by_fore * by_fore + 2.0 * cross * by_back * by_fore
    )
    proj = (along_back * by_back + along_fore * by_fore) / tau_sq
    spring = SPRING * (fore_len - back_len) / jnp.sqrt(tau_sq)
    image = lax.axis_index("img")
    is_end = jnp.logical_or(image == 0, image == lax.axis_size("img") - 1)
    factor = jnp.where(pk[CLIMB_ROW : CLIMB_ROW + 1, 0:1] == 1.0, -2.0 * proj, spring - proj)
    tangent = band[0:3, :] * by_back + band[4:7, :] * by_fore
    moved = jnp.where(is_end, force[0:3, :], force[0:3, :] + factor * tangent)
    for c in range(3):
        result[c] = moved[c : c + 1]
    energy_out[...] = energy * (1.0 / count)


def swap_pairs(count, offset):
    pairs = []
    for low in range(offset, count, 2):
        high = (low + 1) % count
        pairs += [(low, high), (high, low)]
    return pairs


def image_pairs(images, tiles):
    pairs = []
    for tile in range(tiles):
        pairs += [(a * tiles + tile, b * tiles + tile) for a, b in swap_pairs(images, tile % 2)]
    return pairs


def on_device(positions, species, counts, neighbours, send_list, climb, embed, ref_energy, rad_in, rad_out, mixing, w_energy):
    atoms = species.shape[0]
    width = send_list.shape[0] // 2
    fan = neighbours.shape[0]
    chans = embed.shape[1]
    layers = mixing.shape[0]
    basis_count, units = rad_in.shape[1:]
    blocks = atoms // width
    inner_atoms = (blocks - 2) * width
    tiles = lax.axis_size("atom")
    images = lax.axis_size("img")
    def call(body, operands, outs, scratch=(), flops=0):
        return pl.pallas_call(
            body,
            out_shape=[jax.ShapeDtypeStruct(shape, dtype) for shape, dtype in outs],
            in_specs=[VMEM] * len(operands),
            out_specs=[VMEM] * len(outs),
            scratch_shapes=[pltpu.VMEM(*x) for x in scratch],
            cost_estimate=pl.CostEstimate(flops=flops, bytes_accessed=2**20, transcendentals=0),
            compiler_params=pltpu.CompilerParams(vmem_limit_bytes=16 * 2**20),
        )(*operands)

    def swap(block, offset):
        return lax.ppermute(block, "atom", swap_pairs(tiles, offset))

    pack_type = ((PACK_ROWS, atoms), F32)
    feats_type = ((chans, atoms), BF16)
    halo_type = ((chans, width), BF16)
    hid_type = ((2, fan * units, width), BF16)
    hid_scratch = ((blocks - 2, fan * units, width), BF16)

    def block_outs(count):
        return [
            ((count, 3 * fan, width), F32),
            ((count, fan * basis_count, width), BF16),
            ((count, fan, width), F32),
        ]

    row = lax.broadcasted_iota(I32, (PACK_ROWS, atoms), 0)
    sends = jnp.pad(send_list, (0, atoms - 2 * width))
    (pk,) = call(blank, (), [pack_type], flops=2**33)
    lines = [positions[0, c] for c in range(3)] + [species, counts, sends, climb]
    for place, line in zip((0, 1, 2, SPECIES_ROW, COUNT_ROW, SEND_ROW, CLIMB_ROW), lines):
        pk = jnp.where(row == place, lax.broadcast_in_dim(line, pk.shape, (1,)).astype(F32), pk)
    mate = swap(pk, 0)
    cross = swap(pk, 1)
    kinds_type = ((blocks - 2, fan, width), F32)
    own_table, seated, edges, owns, depth, delta_in, basis_in, kinds_in, place_in = call(
        functools.partial(seat_tile, width),
        (pk, neighbours),
        [
            pack_type,
            pack_type,
            ((blocks, fan, width), F32),
            ((blocks, fan, LANES), F32),
            ((PACK_ROWS, LANES), F32),
        ]
        + block_outs(blocks - 2)[:2]
        + [kinds_type, kinds_type],
        [((fan, atoms), F32)],
        flops=2**32,
    )
    inner, embed_t, first, first_rest, spread, out_t, mix_half, w_row, ref_row = call(
        functools.partial(first_inner, width),
        (ref_energy[None], pk, seated, owns, depth, basis_in, kinds_in, embed, rad_in, rad_out, mixing, w_energy[None]),
        [
            ((chans, inner_atoms), BF16),
            ((chans, -(-embed.shape[0] // 16) * 16), BF16),
            ((chans, embed.shape[0] * units), BF16),
            ((chans, embed.shape[0] * units), BF16),
            ((layers + 1, fan * units, fan * basis_count), BF16),
            ((layers + 1, chans, units), BF16),
            ((layers, chans, chans), BF16),
            ((1, chans), BF16),
            ((1, atoms), F32),
        ],
        [hid_scratch],
        flops=2**32,
    )
    delta_out, basis_out, place_out, feats, to_cross, pair = call(
        functools.partial(first_outer, width),
        (pk, own_table, seated, mate, cross, edges, owns, depth, embed_t, first, first_rest, spread, mix_half, inner),
        block_outs(2) + [feats_type, halo_type, pack_type],
        [((PACK_ROWS, atoms + 2 * width), F32), ((2, fan, width), F32), hid_type],
    )
    for layer in range(1, layers):
        cross = swap(to_cross, 1)
        inner, field_edge, total_edge, lent_edge, pair, to_mate = call(
            functools.partial(layer_inner, width, layer),
            (owns, depth, spread, out_t, mix_half, feats, basis_in, place_in, basis_out, place_out, pair, own_table),
            [
                ((chans, inner_atoms), BF16),
                ((2, fan, chans, width), F32),
                ((2, chans, width), F32),
                ((2, chans, LANES), F32),
                pack_type,
                halo_type,
            ],
            [((blocks, fan * units, width), BF16)],
            flops=2**32,
        )
        mate = swap(to_mate, 0)
        feats, to_mate, to_cross = call(
            functools.partial(layer_outer, width, layer),
            (own_table, owns, depth, mix_half, feats, place_out, mate, cross, field_edge, total_edge, lent_edge, inner),
            [feats_type, halo_type, halo_type],
        )
    received = lax.ppermute(pair, ("img", "atom"), image_pairs(images, tiles))
    mate = swap(to_mate, 0)
    cross = swap(to_cross, 1)
    inner, field_edge, pair_edge = call(
        functools.partial(head_inner, width, layers),
        (own_table, owns, depth, spread, out_t, feats, basis_in, place_in, delta_in, basis_out, place_out),
        [((PACK_ROWS, inner_atoms), F32), ((2, fan, chans, width), F32), ((2, fan, width), F32)],
        [((blocks, fan * units, width), BF16), ((blocks - 2, fan, width), F32)],
        flops=2**32,
    )
    (late,) = call(pass_on, (received, inner), [pack_type])
    relayed = swap(late, 0)
    (force,) = call(
        functools.partial(head_outer, width),
        (own_table, owns, depth, place_out, delta_out, cross, mate, field_edge, pair_edge, inner),
        [pack_type],
        [((2, fan, width), F32)],
        flops=2**32,
    )
    band, sums = call(
        tail,
        (pk, received, relayed, w_row, ref_row, feats, force),
        [pack_type, ((SUM_ROWS, LANES), F32)],
    )
    step = 2 * REDUCE_CHIPS
    while step < tiles:
        sums = sums + lax.ppermute(sums, "atom", [(i, i ^ step) for i in range(tiles)])
        step *= 2
    (both,) = call(add_sums, (sums, swap(sums, 0)), [((SUM_ROWS, LANES), F32)])
    near = lax.ppermute(both, "atom", [(i, i ^ 2 if i % 2 == 0 else i ^ 6) for i in range(tiles)])
    far = lax.ppermute(both, "atom", [(i, i ^ 4) for i in range(tiles)])
    other = swap(near, 0)
    result, energy = call(
        functools.partial(finish, atoms * tiles),
        (pk, band, force, both, near, far, other),
        [((3, 1, atoms), F32), ((1, 1), F32)],
    )
    return jnp.transpose(result, (1, 0, 2)), energy.reshape(1)


def solution(mesh):
    return jax.shard_map(
        on_device,
        mesh=mesh,
        in_specs=(
            P("img", None, "atom"),
            P("atom"),
            P("atom"),
            P(None, "atom"),
            P("atom"),
            P("img"),
            P(),
            P(),
            P(),
            P(),
            P(),
            P(),
        ),
        out_specs=(P("img", None, "atom"), P("img")),
        check_vma=False,
    )
```

```python
import functools
import math

import jax
import jax.numpy as jnp
from jax import lax
from jax.experimental import pallas as pl
from jax.experimental.pallas import tpu as pltpu
from jax.sharding import PartitionSpec as P

F32 = jnp.float32
BF16 = jnp.bfloat16
I32 = jnp.int32
LANES = 128
SPRING = 5.0
SPECIES_ROW = 3
COUNT_ROW = 4
SEND_ROW = 5
SEAT_ROW = 6
CLIMB_ROW = 7
CODE_ROW = 7
KIND_STEP = 1024.0
PACK_ROWS = 8
SUM_ROWS = 8
REDUCE_CHIPS = 4
VMEM = pl.BlockSpec(memory_space=pltpu.VMEM)


def core_index():
    return lax.rem(lax.axis_index("atom"), 2)


def dot(a, b):
    return jnp.dot(a, b, preferred_element_type=F32)


def silu_of_half(half):
    return half + half * jnp.tanh(half)


def aligned(start, step):
    return pl.multiple_of(start, step)


def halves(width):
    return [slice(k * LANES, (k + 1) * LANES) for k in range(width // LANES)]


def depths(fan):
    short = -(-5 * fan // 8)
    return [short, short + 1, short + 2, fan]


def lane_fetch(windows, group, place):
    found = jnp.zeros(place.shape, F32)
    for k, window in enumerate(windows):
        rows = jnp.broadcast_to(window, place.shape)
        picked = jnp.take_along_axis(rows, place, axis=1, mode="promise_in_bounds")
        found = jnp.where(group == k, picked, found)
    return found


def lane_lookup(windows, index):
    return lane_fetch(windows, index // LANES, index & (LANES - 1))


def blank(out):
    out[...] = jnp.zeros(out.shape, F32)


def seat_atoms(pk, lo, width, most):
    counts = pk[COUNT_ROW : COUNT_ROW + 1, lo : lo + width]
    value = lax.broadcasted_iota(I32, (most, width), 0).astype(F32) + 1.0
    same = counts == value
    row = lax.broadcasted_iota(I32, (width, width), 0)
    lane = lax.broadcasted_iota(I32, (width, width), 1)
    earlier = dot(jnp.where(same, 1.0, 0.0).astype(BF16), jnp.where(row < lane, 1.0, 0.0).astype(BF16))
    larger = jnp.sum(jnp.where(counts > value, 1.0, 0.0), axis=1, keepdims=True)
    rank = jnp.sum(jnp.where(same, earlier + larger, 0.0), axis=0, keepdims=True)
    seat = jnp.where(rank < width // 2, rank, 1.5 * width - 1.0 - rank)
    taken = jnp.where(row.astype(F32) == seat, 1.0, 0.0).astype(BF16)
    atoms = lax.broadcasted_iota(I32, (PACK_ROWS, width), 1).astype(F32).astype(BF16)
    taker = lax.dot_general(
        atoms, taken, (((1,), (1,)), ((), ())), preferred_element_type=F32
    )
    return seat, taker[:1]


def seat_block(pk, nbr, lo, width, seated):
    fan = nbr.shape[0]
    seat, taker = seat_atoms(pk, lo, width, fan)
    pieces, tables = [], []
    for part in halves(width):
        who = taker[:, part].astype(I32)
        spans = [nbr[:, lo + p.start : lo + p.stop] for p in halves(width)]
        pieces.append(lane_lookup(spans, jnp.broadcast_to(who, (fan, LANES))) - float(lo))
        spans = [pk[:, lo + p.start : lo + p.stop] for p in halves(width)]
        tables.append(lane_lookup(spans, jnp.broadcast_to(who, (PACK_ROWS, LANES))))
    seated[:, lo : lo + width] = jnp.concatenate(tables, axis=1)
    return seat, pieces, [x[COUNT_ROW : COUNT_ROW + 1] for x in tables]


def fill_rows(pieces, counts, limit):
    first, second = pieces
    fan = first.shape[0]
    row = lax.broadcasted_iota(I32, (fan, LANES), 0).astype(F32)
    mine = row < counts[1]
    spilled, over = jnp.zeros((fan, LANES), F32), first
    for rows in depths(fan)[:-1]:
        slots = [2 * rows - 1 - r if 0 <= 2 * rows - 1 - r < fan else 0 for r in range(fan)]
        here = jnp.logical_and(limit == float(rows), 2.0 * rows - 1.0 - row < counts[0])
        here = jnp.logical_and(here, row < float(rows))
        here = jnp.logical_and(here, row >= float(2 * rows - fan))
        here = jnp.logical_and(here, jnp.logical_not(mine))
        over = jnp.where(here, jnp.concatenate([first[r : r + 1] for r in slots], axis=0), over)
        spilled = jnp.where(here, 1.0, spilled)
    spilled = spilled > 0.5
    first = jnp.where(row < jnp.minimum(counts[0], limit), first, -1.0)
    second = jnp.where(mine, second, jnp.where(spilled, over, -1.0))
    return jnp.concatenate([first, second], axis=1), jnp.where(spilled, 0.0, 1.0)


def by_depth(depth, fan, run):
    limit = jnp.max(depth[...])
    short = depths(fan)[0]

    @pl.when(limit < short + 0.5)
    def _():
        run(short)

    @pl.when(limit > short + 0.5)
    def _():
        run(limit.astype(I32))


def over_rows(rows, step, carry):
    if isinstance(rows, int):
        for s in range(rows):
            carry = step(s, carry)
        return carry
    return lax.fori_loop(0, rows, step, carry)


def spill_from(rows, fan):
    return 2 * rows - fan if isinstance(rows, int) else 0


def may_spill(s, first):
    return not isinstance(s, int) or s >= first


def locate_block(i, table, table_lo, seated, edges, own, lo, width, delta_out, basis_out, kinds_out, place_out):
    fan = edges.shape[0]
    spans = [
        table[:, table_lo + p.start : table_lo + p.stop] for p in halves(3 * width)
    ]
    mine = own > 0.5
    home = seated[:, lo : lo + width]
    parts = []
    for part in halves(width):
        rel = edges[:, part].astype(I32)
        live = rel >= 0
        group, place = rel >> 7, rel & (LANES - 1)
        fetch = lambda r: lane_fetch([span[r : r + 1] for span in spans], group, place)
        values = []
        for c in range(3):
            here = home[c : c + 1, part]
            if part.start > 0:
                here = jnp.where(mine, here, home[c : c + 1, :LANES])
            values.append(fetch(c) - here)
        code = fetch(CODE_ROW)
        seat = jnp.floor(code * (1.0 / KIND_STEP))
        values.append(jnp.where(live, code - seat * KIND_STEP, -1.0))
        tile = (rel // width).astype(F32) * float(width)
        values.append(jnp.where(live, seat + tile, -1.0))
        parts.append(values)
    joined = [jnp.concatenate(list(piece), axis=1) for piece in zip(*parts)]
    for c in range(3):
        delta_out[i, c * fan : (c + 1) * fan, :] = joined[c]
    kinds_out[i] = joined[3]
    place_out[i] = joined[4]
    dist_sq = joined[0] * joined[0] + joined[1] * joined[1] + joined[2] * joined[2]
    count = basis_out.shape[1] // fan
    centres = 2.0 * lax.broadcasted_iota(I32, (count, width), 0).astype(F32)
    rows = []
    for s in range(fan):
        away = jnp.broadcast_to(dist_sq[s : s + 1], (count, width)) - centres
        rows.append(jnp.exp(away * away * -0.125))
    basis_out[i] = jnp.concatenate(rows, axis=0).astype(BF16)


def fill_hidden(target, spread, basis, rows, fan):
    units = spread.shape[0] // fan

    def part(start, used):
        place = pl.ds(start, used)
        target[place, :] = silu_of_half(dot(spread[place, :], basis[...])).astype(BF16)

    if isinstance(rows, int):
        part(0, rows * units)
    else:

        def step(s, carry):
            part(aligned(s * units, units), units)
            return carry

        lax.fori_loop(0, fan, step, 0)


def add_terms(carry, own, s, terms, first):
    total, lent = carry
    if may_spill(s, first):
        lent = lent + jnp.where(own[pl.ds(s, 1), :] > 0.5, 0.0, terms[:, LANES:])
    return total + terms, lent


def no_sums(chans, width):
    return jnp.zeros((chans, width), F32), jnp.zeros((chans, LANES), F32)


def summed_of(carry):
    total, lent = carry
    return jnp.concatenate([total[:, :LANES] + lent, total[:, LANES:] - lent], axis=1)


def update_of(feats, summed, mix_half, fan):
    scaled = (summed * (1.0 / math.sqrt(fan))).astype(BF16)
    return (feats.astype(F32) + silu_of_half(dot(mix_half, scaled))).astype(BF16)


def first_block(rows, kinds, hid, own, seated, lo, width, weights):
    embed_t, first, first_rest, mix_half, spread = weights
    fan = kinds.shape[0]
    units = spread.shape[0] // fan
    species = first.shape[1] // units
    zero = jnp.zeros((), BF16)

    def step(s, carry):
        sums, whole, away = carry
        mine = hid[pl.ds(s * units, units), :]
        kind = jnp.broadcast_to(kinds[pl.ds(s, 1), :].astype(BF16), (units, width))
        sorted_out = [
            jnp.where(kind == jnp.full((), k, BF16), mine, zero) for k in range(species)
        ]
        sorted_out = jnp.concatenate(sorted_out, axis=0)
        whole = whole + sorted_out
        if may_spill(s, spill_from(rows, fan)):
            mine = jnp.broadcast_to(own[pl.ds(s, 1), :].astype(BF16), away.shape)
            away = away + jnp.where(mine > jnp.full((), 0.5, BF16), zero, sorted_out[:, LANES:])
        sums = add_terms(sums, own, s, dot(first[...], sorted_out), spill_from(rows, fan))
        return sums, whole, away

    whole = jnp.zeros((species * units, width), BF16)
    carry = no_sums(mix_half.shape[0], width), whole, whole[:, :LANES]
    (total, lent), whole, away = over_rows(rows, step, carry)
    sums = total + dot(first_rest[...], whole), lent + dot(first_rest[...], away)
    rows_of = lax.broadcasted_iota(I32, (embed_t.shape[1], width), 0).astype(F32)
    same = rows_of == seated[SPECIES_ROW : SPECIES_ROW + 1, lo : lo + width]
    feats = dot(embed_t[...], jnp.where(same, 1.0, 0.0).astype(BF16))
    return update_of(feats, summed_of(sums), mix_half[...], fan)


def turned(matrix):
    size = matrix.shape[1]
    row = lax.broadcasted_iota(I32, (size, size), 0)
    column = lax.broadcasted_iota(I32, (size, size), 1)
    identity = jnp.where(row == column, 1.0, 0.0).astype(BF16)
    return lax.dot_general(
        identity, matrix, (((1,), (1,)), ((), ())), preferred_element_type=F32
    )


def prepare(embed, rad_in, rad_out, mixing, embed_t, first, first_rest, spread, out_t, mix_half):
    layers, count, units = rad_in.shape
    fan = spread.shape[1] // units
    for layer in range(layers):
        half = rad_in[layer].astype(F32) * 0.5
        weight = turned(jnp.concatenate([half] * fan, axis=0).astype(BF16))
        owner = lax.broadcasted_iota(I32, weight.shape, 1) // count
        for s in range(fan):
            only = jnp.where(owner == s, weight, 0.0).astype(BF16)
            spread[layer, s * units : (s + 1) * units, :] = only
        out_t[layer] = turned(rad_out[layer]).astype(BF16)
    for layer in range(mixing.shape[0]):
        mix_half[layer] = (turned(mixing[layer]) * 0.5).astype(BF16)
    out = rad_out[0].astype(F32)
    table = embed[...].astype(F32)
    species = table.shape[0]
    padded = jnp.concatenate(
        [table, jnp.zeros((embed_t.shape[1] - species, table.shape[1]), F32)], axis=0
    )
    embed_t[...] = turned(padded.astype(BF16)).astype(BF16)
    scaled = jnp.concatenate([out * table[k : k + 1] for k in range(species)], axis=0)
    first[...] = turned(scaled.astype(BF16)).astype(BF16)
    rest = scaled - scaled.astype(BF16).astype(F32)
    first_rest[...] = turned(rest.astype(BF16)).astype(BF16)


def seat_tile(width, pk, nbr, table, seated, edges, owns, depth, delta_out, basis_out, kinds_out, place_out, index):
    atoms = pk.shape[1]
    blocks = atoms // width
    index[...] = nbr[...].astype(F32)
    table[...] = pk[...]
    found = [seat_block(pk, index, b * width, width, seated) for b in range(blocks)]
    both = [counts[0] + counts[1] for _, _, counts in found]
    most = functools.reduce(jnp.maximum, both)
    most = jnp.max(most, axis=1, keepdims=True)
    fan = nbr.shape[0]
    limit = jnp.full(most.shape, float(fan), F32)
    for rows in depths(fan)[-2::-1]:
        limit = jnp.where(most <= float(2 * rows), float(rows), limit)
    depth[...] = jnp.broadcast_to(limit, depth.shape)
    for b, (seat, pieces, counts) in enumerate(found):
        here = slice(b * width, (b + 1) * width)
        table[SEAT_ROW : SEAT_ROW + 1, here] = seat
        table[CODE_ROW : CODE_ROW + 1, here] = seat * KIND_STEP + pk[SPECIES_ROW : SPECIES_ROW + 1, here]
        edges[b], owns[b] = fill_rows(pieces, counts, limit)
    for part in halves(2 * width):
        wanted = jnp.broadcast_to(pk[SEND_ROW : SEND_ROW + 1, part].astype(I32), (PACK_ROWS, LANES))
        seats = lane_lookup([table[SEAT_ROW : SEAT_ROW + 1, p] for p in halves(atoms)], wanted)
        seats = seats + (wanted // width).astype(F32) * float(width)
        table[SEND_ROW : SEND_ROW + 1, part] = seats[:1]

    for i in range(blocks - 2):
        lo = (i + 1) * width
        locate_block(
            i, table, lo - width, seated, edges[i + 1], owns[i + 1], lo, width,
            delta_out, basis_out, kinds_out, place_out,
        )


def first_inner(width, ref_energy, pk, seated, owns, depth, basis, kinds, embed, rad_in, rad_out, mixing, w_in, feats_out, embed_t, first, first_rest, spread, out_t, mix_half, w_row, ref_row, hid):
    prepare(embed, rad_in, rad_out, mixing, embed_t, first, first_rest, spread, out_t, mix_half)
    weights = (embed_t, first, first_rest, mix_half.at[0], spread.at[0])
    w_row[...] = w_in[...]
    kinds_row = pk[SPECIES_ROW : SPECIES_ROW + 1, :]
    energy = jnp.zeros(kinds_row.shape, F32)
    for k in range(ref_energy.shape[1]):
        energy = jnp.where(kinds_row == float(k), ref_energy[0:1, k : k + 1], energy)
    ref_row[...] = energy
    def run(rows):
        for i in range(kinds.shape[0]):
            fill_hidden(hid.at[i], spread.at[0], basis.at[i], rows, kinds.shape[1])
        for i in range(kinds.shape[0]):
            feats_out[:, i * width : (i + 1) * width] = first_block(
                rows, kinds.at[i], hid.at[i], owns.at[i + 1], seated, (i + 1) * width, width, weights
            )

    by_depth(depth, kinds.shape[1], run)


def pack_halo(feats, table, start, width, out):
    atoms = feats.shape[1]
    rows = lax.broadcasted_iota(I32, (width, width), 0).astype(F32).astype(BF16)
    one, zero = jnp.ones((), BF16), jnp.zeros((), BF16)
    wanted = table[SEND_ROW : SEND_ROW + 1, pl.ds(aligned(start, width), width)]
    picks = []
    for k in range(atoms // width):
        place = jnp.clip(wanted - float(k * width), -1.0, float(width)).astype(BF16)
        picks.append(jnp.where(rows == place, one, zero))
    out[...] = dot(feats[...], jnp.concatenate(picks, axis=0)).astype(BF16)


def halo_places(core, atoms, width):
    top = atoms + width
    return aligned((1 - core) * top, width), aligned(core * top, width)


def edge_blocks(blocks, width):
    return [(0, 0, 0), (1, blocks - 1, (blocks - 1) * width)]


def first_outer(width, pk, own_table, seated, mate, cross, edges, owns, depth, embed_t, first, first_rest, spread, mix_half, inner, delta_out, basis_out, place_out, feats_out, to_cross, pair_out, table, kinds, hid):
    core = core_index()
    atoms = pk.shape[1]
    blocks = atoms // width
    fan = edges.shape[1]
    weights = (embed_t, first, first_rest, mix_half.at[0], spread.at[0])
    table[:, width : width + atoms] = own_table[...]
    at_mate, at_cross = halo_places(core, atoms, width)
    for ref, start, at in ((mate, core * width, at_mate), (cross, (1 - core) * width, at_cross)):
        spans = [ref[:, part] for part in halves(atoms)]
        for k in range(width // LANES):
            wanted = ref[SEND_ROW : SEND_ROW + 1, pl.ds(aligned(start + k * LANES, LANES), LANES)]
            wanted = jnp.broadcast_to(wanted.astype(I32), (PACK_ROWS, LANES))
            place = pl.ds(aligned(at + k * LANES, LANES), LANES)
            table[:, place] = lane_lookup(spans, wanted)
            lane = lax.broadcasted_iota(I32, (1, LANES), 1) + k * LANES
            kind = table[SPECIES_ROW : SPECIES_ROW + 1, place]
            table[CODE_ROW : CODE_ROW + 1, place] = lane.astype(F32) * KIND_STEP + kind
    feats_out[:, width : atoms - width] = inner[...]
    pair_out[0:4, :] = pk[0:4, :]
    pair_out[4:8, :] = mate[0:4, :]

    for i, b, lo in edge_blocks(blocks, width):
        locate_block(
            i, table, lo, seated, edges[b], owns[b], lo, width,
            delta_out, basis_out, kinds, place_out,
        )

    def run(rows):
        for i in range(2):
            fill_hidden(hid.at[i], spread.at[0], basis_out.at[i], rows, fan)
        for i, b, lo in edge_blocks(blocks, width):
            feats_out[:, lo : lo + width] = first_block(
                rows, kinds.at[i], hid.at[i], owns.at[b], seated, lo, width, weights
            )

    by_depth(depth, fan, run)
    pack_halo(feats_out, own_table, core * width, width, to_cross)


class Places:
    def __init__(self, place, width, tiles):
        self.place, self.width, self.tiles = place, width, tiles
        self.known = self.rows(place[...])

    def rows(self, place):
        width = float(self.width)
        return [jnp.clip(place - k * width, -1.0, width).astype(BF16) for k in self.tiles]

    def fetch(self, window, s):
        if isinstance(s, int):
            lines = [x[s : s + 1] for x in self.known]
        else:
            lines = self.rows(self.place[pl.ds(s, 1), :])
        rows = lax.broadcasted_iota(I32, (self.width, self.width), 0).astype(F32).astype(BF16)
        one, zero = jnp.ones((), BF16), jnp.zeros((), BF16)
        return dot(window, jnp.concatenate([jnp.where(rows == x, one, zero) for x in lines], axis=0))


def stored(hid, s, units):
    return hid[pl.ds(s * units, units), :]


def layer_inner(width, layer, owns, depth, spreads, outs_t, mixes, feats, basis, place, basis_edge, place_edge, pair, own_table, feats_out, field_edge, total_edge, lent_edge, pair_out, to_mate, hid):
    spread, out_t, mix_half = spreads.at[layer], outs_t[layer], mixes[layer]
    chans, units = out_t.shape
    fan = place.shape[1]
    inner = place.shape[0]
    pair_out[...] = pair[...]
    pack_halo(feats, own_table, (1 - core_index()) * width, width, to_mate)

    def run(rows):
        first = spill_from(rows, fan)
        for i in range(inner):
            fill_hidden(hid.at[i], spread, basis.at[i], rows, fan)
        for i in range(2):
            fill_hidden(hid.at[inner + i], spread, basis_edge.at[i], rows, fan)
        for i in range(inner):
            lo = (i + 1) * width
            window = feats[:, lo - width : lo + 2 * width]
            places = Places(place.at[i], width, (0, 1, 2))

            def step(s, carry):
                terms = places.fetch(window, s) * dot(out_t, stored(hid.at[i], s, units))
                return add_terms(carry, owns.at[i + 1], s, terms, first)

            sums = over_rows(rows, step, no_sums(chans, width))
            feats_out[:, lo - width : lo] = update_of(
                feats[:, lo : lo + width], summed_of(sums), mix_half, fan
            )
        for i, b, lo in edge_blocks(inner + 2, width):
            start = max(lo - width, 0)
            window = feats[:, start : start + 2 * width]
            places = Places(place_edge.at[i], width, (0, 1) if i else (1, 2))

            def step(s, carry):
                field = dot(out_t, stored(hid.at[inner + i], s, units))
                field_edge[i, s] = field
                return add_terms(carry, owns.at[b], s, places.fetch(window, s) * field, first)

            total_edge[i], lent_edge[i] = over_rows(rows, step, no_sums(chans, width))

    by_depth(depth, fan, run)


def halo_of(i, core, mate, cross):
    lower_by_mate = core == (0 if i else 1)
    return jnp.where(lower_by_mate, mate[...], cross[...])


def layer_outer(width, layer, own_table, owns, depth, mixes, feats, place, mate, cross, field_edge, total_edge, lent_edge, inner, feats_out, to_mate, to_cross):
    core = core_index()
    atoms = feats.shape[1]
    fan = place.shape[1]
    mix_half = mixes[layer]
    feats_out[:, width : atoms - width] = inner[...]

    def run(rows):
        for i, b, lo in edge_blocks(atoms // width, width):
            halo = halo_of(i, core, mate, cross)
            places = Places(place.at[i], width, (2,) if i else (0,))

            def step(s, carry):
                terms = places.fetch(halo, s) * field_edge[i, s]
                return add_terms(carry, owns.at[b], s, terms, spill_from(rows, fan))

            sums = over_rows(rows, step, (total_edge[i], lent_edge[i]))
            feats_out[:, lo : lo + width] = update_of(
                feats[:, lo : lo + width], summed_of(sums), mix_half, fan
            )

    by_depth(depth, fan, run)
    pack_halo(feats_out, own_table, core * width, width, to_cross)
    pack_halo(feats_out, own_table, (1 - core) * width, width, to_mate)


def near_of(near, own, s, first):
    if not may_spill(s, first):
        return near
    lower = jnp.where(own[pl.ds(s, 1), :] > 0.5, near[:, LANES:], near[:, :LANES])
    return jnp.concatenate([near[:, :LANES], lower], axis=1)


def put_pair(pairs, s, terms):
    pairs[pl.ds(s, 1), :] = jnp.sum(terms, axis=0, keepdims=True)


def force_of(pair, own, delta, seat, chans):
    fan, width = pair.shape
    pair = pair * (1.0 / math.sqrt(chans))
    mine = own[...] > 0.5
    out = []
    for c in range(3):
        terms = pair * delta[c * fan : (c + 1) * fan, :]
        second = terms[:, LANES:]
        lent = jnp.where(mine, 0.0, second)
        out.append(
            jnp.concatenate(
                [
                    jnp.sum(terms[:, :LANES] + lent, axis=0, keepdims=True),
                    jnp.sum(jnp.where(mine, second, 0.0), axis=0, keepdims=True),
                ],
                axis=1,
            )
        )
    seated = jnp.concatenate(out + [jnp.zeros((PACK_ROWS - 3, width), F32)], axis=0)
    spans = [seated[:, part] for part in halves(width)]
    seat = seat.astype(I32)
    return jnp.concatenate(
        [
            lane_lookup(spans, jnp.broadcast_to(seat[:, part], (PACK_ROWS, LANES)))
            for part in halves(width)
        ],
        axis=1,
    )


def head_inner(width, layer, own_table, owns, depth, spreads, outs_t, feats, basis, place, delta, basis_edge, place_edge, force_out, field_edge, pair_edge, hid, pairs):
    spread, out_t = spreads.at[layer], outs_t[layer]
    chans, units = out_t.shape
    fan = place.shape[1]
    inner = place.shape[0]
    pairs[...] = jnp.zeros(pairs.shape, F32)
    pair_edge[...] = jnp.zeros(pair_edge.shape, F32)

    def run(rows):
        first = spill_from(rows, fan)
        for i in range(inner):
            fill_hidden(hid.at[i], spread, basis.at[i], rows, fan)
        for i in range(2):
            fill_hidden(hid.at[inner + i], spread, basis_edge.at[i], rows, fan)
        for i in range(inner):
            lo = (i + 1) * width
            window = feats[:, lo - width : lo + 2 * width]
            near = feats[:, lo : lo + width].astype(F32)
            places = Places(place.at[i], width, (0, 1, 2))

            def step(s, carry):
                field = dot(out_t, stored(hid.at[i], s, units))
                field = field * near_of(near, owns.at[i + 1], s, first)
                put_pair(pairs.at[i], s, places.fetch(window, s) * field)
                return carry

            over_rows(rows, step, 0)
            force_out[:, lo - width : lo] = force_of(
                pairs[i], owns.at[i + 1], delta.at[i],
                own_table[SEAT_ROW : SEAT_ROW + 1, lo : lo + width], chans,
            )
        for i, b, lo in edge_blocks(inner + 2, width):
            start = max(lo - width, 0)
            window = feats[:, start : start + 2 * width]
            near = feats[:, lo : lo + width].astype(F32)
            places = Places(place_edge.at[i], width, (0, 1) if i else (1, 2))

            def step(s, carry):
                field = dot(out_t, stored(hid.at[inner + i], s, units))
                field = field * near_of(near, owns.at[b], s, first)
                field_edge[i, s] = field
                put_pair(pair_edge.at[i], s, places.fetch(window, s) * field)
                return carry

            over_rows(rows, step, 0)

    by_depth(depth, fan, run)


def lane_sum(values):
    total = values[:, :LANES]
    for part in halves(values.shape[1])[1:]:
        total = total + values[:, part]
    return jnp.sum(total, axis=0, keepdims=True)


def head_outer(width, own_table, owns, depth, place, delta, cross, mate, field_edge, pair_edge, inner, force_out, pairs):
    core = core_index()
    chans = mate.shape[0]
    atoms = own_table.shape[1]
    fan = place.shape[1]
    force_out[:, width : atoms - width] = inner[...]
    pairs[...] = jnp.zeros(pairs.shape, F32)

    def run(rows):
        for i, b, lo in edge_blocks(atoms // width, width):
            halo = halo_of(i, core, mate, cross)
            places = Places(place.at[i], width, (2,) if i else (0,))

            def step(s, carry):
                put_pair(pairs.at[i], s, places.fetch(halo, s) * field_edge[i, s])
                return carry

            over_rows(rows, step, 0)
            force_out[:, lo : lo + width] = force_of(
                pair_edge[i] + pairs[i], owns.at[b], delta.at[i],
                own_table[SEAT_ROW : SEAT_ROW + 1, lo : lo + width], chans,
            )

    by_depth(depth, fan, run)


def pass_on(received, _, out):
    out[...] = received[...]


def tail(pk, received, relayed, w_row, ref_row, feats, force_in, band_out, sums_out):
    core = core_index()
    energy = dot(w_row[...], feats[...]) + ref_row[...]
    direct, by_mate = received[0:4, :], relayed[4:8, :]
    direct_ahead = lax.rem(core + lax.axis_index("img"), 2) == 0
    back = pk[0:4, :] - jnp.where(direct_ahead, by_mate, direct)
    fore = jnp.where(direct_ahead, direct, by_mate) - pk[0:4, :]
    band_out[0:4, :] = back
    band_out[4:8, :] = fore
    back, fore, force = back[:3], fore[:3], force_in[0:3, :]
    rows = [energy, back * back, fore * fore, back * fore, force * back, force * fore]
    sums = [lane_sum(row) for row in rows]
    sums.append(jnp.zeros((SUM_ROWS - len(sums), LANES), F32))
    sums_out[...] = jnp.concatenate(sums, axis=0)


def add_sums(mine, other, out):
    out[...] = mine[...] + other[...]


def finish(count, pk, band, force, *rest):
    *parts, result, energy_out = rest
    total = parts[0][...]
    for part in parts[1:]:
        total = total + part[...]
    total = jnp.sum(total, axis=1, keepdims=True)
    energy, back_sq, fore_sq, cross, along_back, along_fore = (total[i : i + 1] for i in range(6))
    back_len = jnp.sqrt(back_sq + 1e-06)
    fore_len = jnp.sqrt(fore_sq + 1e-06)
    by_back, by_fore = 1.0 / back_len, 1.0 / fore_len
    tau_sq = (
        back_sq * by_back * by_back + fore_sq * by_fore * by_fore + 2.0 * cross * by_back * by_fore
    )
    proj = (along_back * by_back + along_fore * by_fore) / tau_sq
    spring = SPRING * (fore_len - back_len) / jnp.sqrt(tau_sq)
    image = lax.axis_index("img")
    is_end = jnp.logical_or(image == 0, image == lax.axis_size("img") - 1)
    factor = jnp.where(pk[CLIMB_ROW : CLIMB_ROW + 1, 0:1] == 1.0, -2.0 * proj, spring - proj)
    tangent = band[0:3, :] * by_back + band[4:7, :] * by_fore
    moved = jnp.where(is_end, force[0:3, :], force[0:3, :] + factor * tangent)
    for c in range(3):
        result[c] = moved[c : c + 1]
    energy_out[...] = energy * (1.0 / count)


def swap_pairs(count, offset):
    pairs = []
    for low in range(offset, count, 2):
        high = (low + 1) % count
        pairs += [(low, high), (high, low)]
    return pairs


def image_pairs(images, tiles):
    pairs = []
    for tile in range(tiles):
        pairs += [(a * tiles + tile, b * tiles + tile) for a, b in swap_pairs(images, tile % 2)]
    return pairs


def on_device(positions, species, counts, neighbours, send_list, climb, embed, ref_energy, rad_in, rad_out, mixing, w_energy):
    atoms = species.shape[0]
    width = send_list.shape[0] // 2
    fan = neighbours.shape[0]
    chans = embed.shape[1]
    layers = mixing.shape[0]
    basis_count, units = rad_in.shape[1:]
    blocks = atoms // width
    inner_atoms = (blocks - 2) * width
    tiles = lax.axis_size("atom")
    images = lax.axis_size("img")
    def call(body, operands, outs, scratch=(), flops=0):
        return pl.pallas_call(
            body,
            out_shape=[jax.ShapeDtypeStruct(shape, dtype) for shape, dtype in outs],
            in_specs=[VMEM] * len(operands),
            out_specs=[VMEM] * len(outs),
            scratch_shapes=[pltpu.VMEM(*x) for x in scratch],
            cost_estimate=pl.CostEstimate(flops=flops, bytes_accessed=2**20, transcendentals=0),
            compiler_params=pltpu.CompilerParams(vmem_limit_bytes=16 * 2**20),
        )(*operands)

    def swap(block, offset):
        return lax.ppermute(block, "atom", swap_pairs(tiles, offset))

    pack_type = ((PACK_ROWS, atoms), F32)
    feats_type = ((chans, atoms), BF16)
    halo_type = ((chans, width), BF16)
    hid_type = ((2, fan * units, width), BF16)
    hid_scratch = ((blocks - 2, fan * units, width), BF16)

    def block_outs(count):
        return [
            ((count, 3 * fan, width), F32),
            ((count, fan * basis_count, width), BF16),
            ((count, fan, width), F32),
        ]

    row = lax.broadcasted_iota(I32, (PACK_ROWS, atoms), 0)
    sends = jnp.pad(send_list, (0, atoms - 2 * width))
    (pk,) = call(blank, (), [pack_type], flops=2**33)
    lines = [positions[0, c] for c in range(3)] + [species, counts, sends, climb]
    for place, line in zip((0, 1, 2, SPECIES_ROW, COUNT_ROW, SEND_ROW, CLIMB_ROW), lines):
        pk = jnp.where(row == place, lax.broadcast_in_dim(line, pk.shape, (1,)).astype(F32), pk)
    mate = swap(pk, 0)
    cross = swap(pk, 1)
    kinds_type = ((blocks - 2, fan, width), F32)
    own_table, seated, edges, owns, depth, delta_in, basis_in, kinds_in, place_in = call(
        functools.partial(seat_tile, width),
        (pk, neighbours),
        [
            pack_type,
            pack_type,
            ((blocks, fan, width), F32),
            ((blocks, fan, LANES), F32),
            ((PACK_ROWS, LANES), F32),
        ]
        + block_outs(blocks - 2)[:2]
        + [kinds_type, kinds_type],
        [((fan, atoms), F32)],
        flops=2**32,
    )
    inner, embed_t, first, first_rest, spread, out_t, mix_half, w_row, ref_row = call(
        functools.partial(first_inner, width),
        (ref_energy[None], pk, seated, owns, depth, basis_in, kinds_in, embed, rad_in, rad_out, mixing, w_energy[None]),
        [
            ((chans, inner_atoms), BF16),
            ((chans, -(-embed.shape[0] // 16) * 16), BF16),
            ((chans, embed.shape[0] * units), BF16),
            ((chans, embed.shape[0] * units), BF16),
            ((layers + 1, fan * units, fan * basis_count), BF16),
            ((layers + 1, chans, units), BF16),
            ((layers, chans, chans), BF16),
            ((1, chans), BF16),
            ((1, atoms), F32),
        ],
        [hid_scratch],
        flops=2**32,
    )
    delta_out, basis_out, place_out, feats, to_cross, pair = call(
        functools.partial(first_outer, width),
        (pk, own_table, seated, mate, cross, edges, owns, depth, embed_t, first, first_rest, spread, mix_half, inner),
        block_outs(2) + [feats_type, halo_type, pack_type],
        [((PACK_ROWS, atoms + 2 * width), F32), ((2, fan, width), F32), hid_type],
    )
    for layer in range(1, layers):
        cross = swap(to_cross, 1)
        inner, field_edge, total_edge, lent_edge, pair, to_mate = call(
            functools.partial(layer_inner, width, layer),
            (owns, depth, spread, out_t, mix_half, feats, basis_in, place_in, basis_out, place_out, pair, own_table),
            [
                ((chans, inner_atoms), BF16),
                ((2, fan, chans, width), F32),
                ((2, chans, width), F32),
                ((2, chans, LANES), F32),
                pack_type,
                halo_type,
            ],
            [((blocks, fan * units, width), BF16)],
            flops=2**32,
        )
        mate = swap(to_mate, 0)
        feats, to_mate, to_cross = call(
            functools.partial(layer_outer, width, layer),
            (own_table, owns, depth, mix_half, feats, place_out, mate, cross, field_edge, total_edge, lent_edge, inner),
            [feats_type, halo_type, halo_type],
        )
    received = lax.ppermute(pair, ("img", "atom"), image_pairs(images, tiles))
    mate = swap(to_mate, 0)
    cross = swap(to_cross, 1)
    inner, field_edge, pair_edge = call(
        functools.partial(head_inner, width, layers),
        (own_table, owns, depth, spread, out_t, feats, basis_in, place_in, delta_in, basis_out, place_out),
        [((PACK_ROWS, inner_atoms), F32), ((2, fan, chans, width), F32), ((2, fan, width), F32)],
        [((blocks, fan * units, width), BF16), ((blocks - 2, fan, width), F32)],
        flops=2**32,
    )
    (late,) = call(pass_on, (received, inner), [pack_type])
    relayed = swap(late, 0)
    (force,) = call(
        functools.partial(head_outer, width),
        (own_table, owns, depth, place_out, delta_out, cross, mate, field_edge, pair_edge, inner),
        [pack_type],
        [((2, fan, width), F32)],
        flops=2**32,
    )
    band, sums = call(
        tail,
        (pk, received, relayed, w_row, ref_row, feats, force),
        [pack_type, ((SUM_ROWS, LANES), F32)],
    )
    step = 2 * REDUCE_CHIPS
    while step < tiles:
        sums = sums + lax.ppermute(sums, "atom", [(i, i ^ step) for i in range(tiles)])
        step *= 2
    (both,) = call(add_sums, (sums, swap(sums, 0)), [((SUM_ROWS, LANES), F32)])
    near = lax.ppermute(both, "atom", [(i, i ^ 2 if i % 2 == 0 else i ^ 6) for i in range(tiles)])
    far = lax.ppermute(both, "atom", [(i, i ^ 4) for i in range(tiles)])
    other = swap(near, 0)
    result, energy = call(
        functools.partial(finish, atoms * tiles),
        (pk, band, force, both, near, far, other),
        [((3, 1, atoms), F32), ((1, 1), F32)],
    )
    return jnp.transpose(result, (1, 0, 2)), energy.reshape(1)


def solution(mesh):
    return jax.shard_map(
        on_device,
        mesh=mesh,
        in_specs=(
            P("img", None, "atom"),
            P("atom"),
            P("atom"),
            P(None, "atom"),
            P("atom"),
            P("img"),
            P(),
            P(),
            P(),
            P(),
            P(),
            P(),
        ),
        out_specs=(P("img", None, "atom"), P("img")),
        check_vma=False,
    )
```
